32 devices in a mesh: img: 8 (over z, x), seq: 4 (over y, core).
Axes of the slice: x: 2, y: 2, z: 4, core: 2. Of those that a mesh axis runs over, the one named last changes fastest.
Arguments:
- hidden_in: bfloat16 [8, 1024, 1408], P('img', 'seq'), may hold values from -6 to 6
- skip_in: bfloat16 [8, 1024, 1408], P('img', 'seq'), may hold values from -6 to 6
- text: bfloat16 [8, 256, 1024], P('img'), may hold values from -6 to 6
- condition: bfloat16 [8, 1408], P('img'), may hold values from -6 to 6
- positions: int32 [8, 1024, 2], P('img', 'seq'), may hold values from 0 to 511, as said below
- out_grad: bfloat16 [8, 1024, 1408], P('img', 'seq'), may hold values from -6 to 6
- skip_gain: float32 [2816], replicated, may hold values from 0.1 to 1.9
- skip_bias: float32 [2816], replicated, may hold values from -4 to 4
- w_skip: float32 [2816, 1408], P('img', 'seq'), may hold values from -0.109375 to 0.109375
- w_mod: float32 [1408, 8448], P('img', 'seq'), may hold values from -0.15625 to 0.15625
- q_gain: float32 [88], replicated, may hold values from 0.1 to 1.9
- k_gain: float32 [88], replicated, may hold values from 0.1 to 1.9
- w_qkv: float32 [1408, 4224], P('img', 'seq'), may hold values from -0.15625 to 0.15625
- w_attn_out: float32 [1408, 1408], P('img', 'seq'), may hold values from -3 to 3
- cross_gain: float32 [1408], replicated, may hold values from 0.1 to 1.9
- cross_bias: float32 [1408], replicated, may hold values from -4 to 4
- w_cross_q: float32 [1408, 1408], P('img', 'seq'), may hold values from -0.15625 to 0.15625
- w_cross_kv: float32 [1024, 2, 1408], P('img', None, 'seq'), may hold values from -0.1875 to 0.1875
- w_cross_out: float32 [1408, 1408], P('img', 'seq'), may hold values from -1.5 to 1.5
- w_fc1: float32 [1408, 6144], P('img', 'seq'), may hold values from -0.15625 to 0.15625
- w_fc2: float32 [6144, 1408], P('img', 'seq'), may hold values from -0.078125 to 0.078125
Outputs:
- block_out: bfloat16 [8, 1024, 1408], P('img', 'seq')
- grad_hidden: float32 [8, 1024, 1408], P('img', 'seq')
- grad_skip: float32 [8, 1024, 1408], P('img', 'seq')
- grad_text: float32 [8, 256, 1024], P('img')
- grad_condition: float32 [8, 1408], P('img')
- grad_skip_gain: float32 [2816], replicated
- grad_skip_bias: float32 [2816], replicated
- grad_w_skip: float32 [2816, 1408], P('img', 'seq')
- grad_w_mod: float32 [1408, 8448], P('img', 'seq')
- grad_q_gain: float32 [88], replicated
- grad_k_gain: float32 [88], replicated
- grad_w_qkv: float32 [1408, 4224], P('img', 'seq')
- grad_w_attn_out: float32 [1408, 1408], P('img', 'seq')
- grad_cross_gain: float32 [1408], replicated
- grad_cross_bias: float32 [1408], replicated
- grad_w_cross_q: float32 [1408, 1408], P('img', 'seq')
- grad_w_cross_kv: float32 [1024, 2, 1408], P('img', None, 'seq')
- grad_w_cross_out: float32 [1408, 1408], P('img', 'seq')
- grad_w_fc1: float32 [1408, 6144], P('img', 'seq')
- grad_w_fc2: float32 [6144, 1408], P('img', 'seq')
The draws below stay inside these ranges and needn't reach their ends.
Inputs may be any that keep to these rules, and one draw needn't show every extreme that they name: `positions`: each image's tokens lie in raster order on a grid whose width is one of 128, 256 and 512; entry 0 is the row, entry 1 the column; at least one image has the widest grid.
All inputs are finite; a program needn't handle non-finite values.
Results may differ from the reference program's by a relative error of at most 0.02.
Values may be sent and summed in bfloat16 or wider, within the bound.
No kernel may reach another device: no remote copies, remote signals or barrier semaphores. Data moves between devices by JAX's collectives and lax.ppermute only.
A program may use at most 448 MiB of HBM per device.

```python
import jax
import jax.numpy as jnp
from jax import lax

D = 1408
H = 16
HD = 88
FF = 6144
TW = 1024
TXT = 256
TOK_DEV = 256
SEQ_LEN = 1024
IMAGES = 8


def draw_positions(key, part):
    key = jax.random.fold_in(key, 11)
    pick_key = jax.random.fold_in(key, 1)
    wide_key = jax.random.fold_in(key, 2)
    widths = jnp.array([TOK_DEV // 2, TOK_DEV, TOK_DEV * 2], dtype=jnp.int32)
    picked = jax.random.randint(pick_key, (IMAGES,), 0, 3)
    widest_image = jax.random.randint(wide_key, (), 0, IMAGES)
    picked = jnp.where(jnp.arange(IMAGES, dtype=jnp.int32) == widest_image, 2, picked)
    image_width = widths[picked]
    order = jnp.arange(SEQ_LEN, dtype=jnp.int32)
    row_index = order[None, :] // image_width[:, None]
    col_index = order[None, :] % image_width[:, None]
    return jnp.stack([row_index, col_index], axis=-1).astype(jnp.int32)


def levels(stream_key, extent, split, smallest, high):
    def one(dim, parts):
        steps = jax.random.uniform(jax.random.fold_in(jax.random.fold_in(stream_key, 6), dim), (parts,), jnp.float32, smallest / len(split), high / len(split))
        return jnp.repeat(jnp.exp(steps), extent[dim] // parts).reshape((-1,) + (1,) * (len(extent) - dim - 1))

    loudness = one(*split[0])
    for cut in split[1:]:
        loudness = loudness * one(*cut)
    return loudness


def normal_values(stream_key, extent, width, limit, cuts=(), held_as=jnp.bfloat16):
    values = jax.random.normal(stream_key, extent, jnp.float32) * width
    if len(cuts) > 0:
        values = levels(stream_key, extent, cuts, -0.22, 0.18) * values
    return jnp.clip(values, min=-limit, max=limit).astype(held_as)


def setup_inputs(seed: int = 0) -> dict:
    seeds = jax.random.split(jax.random.key(seed), 22)
    return {
        "hidden_in": normal_values(seeds[0], (IMAGES, SEQ_LEN, D), 1.0, 6.0, ((0, 8), (1, 4))),
        "skip_in": normal_values(seeds[1], (IMAGES, SEQ_LEN, D), 1.0, 6.0, ((0, 8), (1, 4))),
        "text": normal_values(seeds[2], (IMAGES, TXT, TW), 1.0, 6.0, ((0, 8),)),
        "condition": normal_values(seeds[3], (IMAGES, D), 1.0, 6.0, ((0, 8),)),
        "positions": draw_positions(jax.random.fold_in(seeds[21], 71), 0),
        "out_grad": normal_values(seeds[5], (IMAGES, SEQ_LEN, D), 1.0, 6.0, ((0, 8), (1, 4))),
        "skip_gain": jnp.clip(1.0 + 0.18 * jax.random.normal(seeds[6], (2 * D,), jnp.float32), 0.1, 1.9),
        "skip_bias": normal_values(seeds[7], (2 * D,), 0.3, 4.0, (), jnp.float32),
        "w_skip": normal_values(seeds[8], (2 * D, D), (2 * D) ** -0.5, 0.109375, ((0, 8), (1, 4)), jnp.float32),
        "w_mod": normal_values(seeds[9], (D, 6 * D), D ** -0.5, 0.15625, ((0, 8), (1, 4)), jnp.float32),
        "q_gain": jnp.clip(1.0 + 0.18 * jax.random.normal(seeds[10], (HD,), jnp.float32), 0.1, 1.9),
        "k_gain": jnp.clip(1.0 + 0.18 * jax.random.normal(seeds[11], (HD,), jnp.float32), 0.1, 1.9),
        "w_qkv": normal_values(seeds[12], (D, 3 * D), D ** -0.5, 0.15625, ((0, 8), (1, 4)), jnp.float32),
        "w_attn_out": normal_values(seeds[13], (D, D), (max(1, 3 * D // SEQ_LEN)) ** -0.5, 3.0, ((0, 8), (1, 4)), jnp.float32),
        "cross_gain": jnp.clip(1.0 + 0.18 * jax.random.normal(seeds[14], (D,), jnp.float32), 0.1, 1.9),
        "cross_bias": normal_values(seeds[15], (D,), 0.3, 4.0, (), jnp.float32),
        "w_cross_q": normal_values(seeds[16], (D, D), D ** -0.5, 0.15625, ((0, 8), (1, 4)), jnp.float32),
        "w_cross_kv": normal_values(seeds[17], (TW, 2, D), TW ** -0.5, 0.1875, ((0, 8), (2, 4)), jnp.float32),
        "w_cross_out": normal_values(seeds[18], (D, D), (max(1, 3 * D // TXT)) ** -0.5, 1.5, ((0, 8), (1, 4)), jnp.float32),
        "w_fc1": normal_values(seeds[19], (D, FF), D ** -0.5, 0.15625, ((0, 8), (1, 4)), jnp.float32),
        "w_fc2": normal_values(seeds[20], (FF, D), FF ** -0.5, 0.078125, ((0, 8), (1, 4)), jnp.float32),
    }


@jax.custom_vjp
def low(v):
    return lax.optimization_barrier(v.astype(jnp.bfloat16)).astype(jnp.float32)

@jax.custom_vjp
def low_back(v):
    return v

def low_keep(v):
    return (low(v), None)

def low_pass(kept, grad):
    return (grad,)

def back_keep(v):
    return (v, None)

def back_low(kept, grad):
    return (low(grad),)
low.defvjp(low_keep, low_pass)
low_back.defvjp(back_keep, back_low)
norm_eps = 1e-06

def matmul(left, right):
    return jnp.dot(left, right, precision=lax.Precision.HIGHEST)

def mixing(form, left, right):
    return jnp.einsum(form, left, right, precision=lax.Precision.HIGHEST)

def layer_norm(tensor):
    center = tensor - lax.optimization_barrier(jnp.mean(tensor, axis=-1, keepdims=True))
    spread = lax.optimization_barrier(jnp.mean(center * center, axis=-1, keepdims=True))
    return center * lax.rsqrt(spread + norm_eps)

def modulate(tensor, scale_vec, shift_vec):
    return layer_norm(tensor) * (1.0 + scale_vec) + shift_vec

def affine_norm(tensor, gain_vec, bias_vec):
    return layer_norm(tensor) * gain_vec + bias_vec

def rotary(tensor, grid_pos):
    rows_count, head_count, head_size = tensor.shape
    quarter = head_size // 4
    frequency = 10000.0 ** (-jnp.arange(quarter, dtype=jnp.float32) / quarter)
    angles = grid_pos.astype(jnp.float32)[:, None, :, None] * frequency
    cosine = jnp.cos(angles)
    sine_part = jnp.sin(angles)
    pieces = tensor.reshape(rows_count, head_count, 2, 2, quarter)
    first_half = pieces[:, :, :, 0]
    second_half = pieces[:, :, :, 1]
    turned = jnp.stack([first_half * cosine - second_half * sine_part, first_half * sine_part + second_half * cosine], axis=3)
    return turned.reshape(rows_count, head_count, head_size)

def head_rope(tensor, gain_vec, grid_pos):
    return rotary(layer_norm(tensor) * gain_vec, grid_pos)

def attention(queries, keys, values):
    scores = low_back(mixing('qhd,khd->hqk', queries, keys) * queries.shape[-1] ** (-0.5))
    row_peak = lax.optimization_barrier(jnp.max(scores, axis=-1, keepdims=True))
    exp_scores = jnp.exp(scores - row_peak)
    attn_probs = exp_scores / lax.optimization_barrier(jnp.sum(exp_scores, axis=-1, keepdims=True))
    return mixing('hqk,khd->qhd', low(attn_probs), values)

def block_layer(weights, tokens, skip_rows, text_rows, cond_vec, grid_pos):
    skip_gain, skip_bias, w_skip, w_mod, q_gain, k_gain, w_qkv, w_attn_out, cross_gain, cross_bias, w_cross_q, w_cross_kv, w_cross_out, w_fc1, w_fc2 = weights
    rows_count = tokens.shape[0]
    joined = jnp.concatenate([tokens, skip_rows], axis=-1)
    resid_one = low_back(matmul(low(affine_norm(joined, skip_gain, skip_bias)), low(w_skip)))
    modul = matmul(low(jax.nn.silu(cond_vec))[None], low(w_mod))[0].reshape(6, D)
    attn_in = low(modulate(resid_one, modul[1], modul[0]))
    qkv_raw = low_back(matmul(attn_in, low(w_qkv)))
    query_low = low(head_rope(qkv_raw[:, :D].reshape(rows_count, H, HD), q_gain, grid_pos))
    key_low = low(head_rope(qkv_raw[:, D:2 * D].reshape(rows_count, H, HD), k_gain, grid_pos))
    value_low = low(qkv_raw[:, 2 * D:].reshape(rows_count, H, HD))
    attn_low = low(low_back(attention(query_low, key_low, value_low).reshape(rows_count, D)))
    branch = low_back(matmul(attn_low, low(w_attn_out)))
    resid_two = resid_one + modul[2] * branch
    cross_in = low(affine_norm(resid_two, cross_gain, cross_bias))
    cross_query = low(low_back(matmul(cross_in, low(w_cross_q)))).reshape(rows_count, H, HD)
    text_kv = low(low_back(mixing('tw,wcd->tcd', text_rows, low(w_cross_kv))))
    text_keys = text_kv[:, 0].reshape(-1, H, HD)
    text_values = text_kv[:, 1].reshape(-1, H, HD)
    cross_low = low(low_back(attention(cross_query, text_keys, text_values).reshape(rows_count, D)))
    cross_branch = low_back(matmul(cross_low, low(w_cross_out)))
    resid_three = resid_two + cross_branch
    mlp_in = low(modulate(resid_three, modul[4], modul[3]))
    upper = low_back(matmul(mlp_in, low(w_fc1)))
    act_low = low(jax.nn.gelu(upper, approximate=True))
    mlp_out = low_back(matmul(act_low, low(w_fc2)))
    return resid_three + modul[5] * mlp_out

def reference(hidden_in, skip_in, text, condition, positions, out_grad, skip_gain, skip_bias, w_skip, w_mod, q_gain, k_gain, w_qkv, w_attn_out, cross_gain, cross_bias, w_cross_q, w_cross_kv, w_cross_out, w_fc1, w_fc2):
    params = (skip_gain, skip_bias, w_skip, w_mod, q_gain, k_gain, w_qkv, w_attn_out, cross_gain, cross_bias, w_cross_q, w_cross_kv, w_cross_out, w_fc1, w_fc2)

    def per_image(totals, pieces):
        tokens, skip_rows, text_rows, cond_vec, grid_pos, cotangent = pieces

        def forward(weights, tokens_in, skips_in, words_in, cond_in):
            return block_layer(weights, tokens_in, skips_in, words_in, cond_in, grid_pos)
        result, pullback = jax.vjp(forward, params, tokens.astype(jnp.float32), skip_rows.astype(jnp.float32), text_rows.astype(jnp.float32), cond_vec.astype(jnp.float32))
        gradients = pullback(cotangent.astype(jnp.float32))
        totals = jax.tree.map(jnp.add, totals, gradients[0])
        return (totals, (result.astype(jnp.bfloat16), gradients[1], gradients[2], gradients[3], gradients[4]))
    initial = jax.tree.map(jnp.zeros_like, params)
    totals, stacked = lax.scan(per_image, initial, (hidden_in, skip_in, text, condition, positions, out_grad))
    return (stacked[0], stacked[1], stacked[2], stacked[3], stacked[4], totals[0], totals[1], totals[2], totals[3], totals[4], totals[5], totals[6], totals[7], totals[8], totals[9], totals[10], totals[11], totals[12], totals[13], totals[14])
```

```python
import jax
import jax.numpy as jnp
from jax import lax
from jax.sharding import PartitionSpec as P

D = 1408
H = 16
HD = 88

norm_eps = 1e-06
shards = 4
own_cols = D // shards
own_heads = H // shards

core_pairs = ((0, 1), (1, 0), (2, 3), (3, 2))
chip_pairs = ((0, 2), (2, 0), (1, 3), (3, 1))
cross_pairs = ((0, 3), (3, 0), (1, 2), (2, 1))


def rounded(tensor):
    return tensor.astype(jnp.bfloat16)


def wide(tensor):
    return tensor.astype(jnp.float32)


def matmul(left, right):
    return jnp.dot(left, right, preferred_element_type=jnp.float32)


def matmul_back(left, right):
    return jnp.einsum("tc,kc->tk", left, right, preferred_element_type=jnp.float32)


def contract(left, right):
    return rounded(jnp.einsum("tr,tc->rc", left, right, preferred_element_type=jnp.float32))


def layer_norm(tensor):
    center = tensor - jnp.mean(tensor, axis=-1, keepdims=True)
    spread = jnp.mean(center * center, axis=-1, keepdims=True)
    return center * lax.rsqrt(spread + norm_eps)


def norm_stats(tensor):
    middle = jnp.mean(tensor, axis=-1, keepdims=True)
    center = tensor - middle
    spread = jnp.mean(center * center, axis=-1, keepdims=True)
    return middle, lax.rsqrt(spread + norm_eps)


def rotary(tensor, grid_pos):
    rows_count, head_count, head_size = tensor.shape
    quarter = head_size // 4
    frequency = 10000.0 ** (-jnp.arange(quarter, dtype=jnp.float32) / quarter)
    angles = grid_pos.astype(jnp.float32)[:, None, :, None] * frequency
    cosine = jnp.cos(angles)
    sine_part = jnp.sin(angles)
    pieces = tensor.reshape(rows_count, head_count, 2, 2, quarter)
    first_half = pieces[:, :, :, 0]
    second_half = pieces[:, :, :, 1]
    turned = jnp.stack(
        [
            first_half * cosine - second_half * sine_part,
            first_half * sine_part + second_half * cosine,
        ],
        axis=3,
    )
    return turned.reshape(rows_count, head_count, head_size)


def head_rope(tensor, gain_vec, grid_pos):
    return rotary(layer_norm(tensor) * gain_vec, grid_pos)


def by_heads(tensor):
    return tensor.reshape(tensor.shape[0], own_heads, HD)


def attend(queries, keys, values):
    scores = jnp.einsum(
        "qhd,khd->hqk", queries, keys, preferred_element_type=jnp.float32
    ) * HD ** (-0.5)
    row_peak = jnp.max(scores, axis=-1, keepdims=True)
    exp_scores = jnp.exp(scores - row_peak)
    row_total = jnp.sum(exp_scores, axis=-1, keepdims=True)
    attn_probs = exp_scores / row_total
    outputs = jnp.einsum(
        "hqk,khd->qhd", rounded(attn_probs), values, preferred_element_type=jnp.float32
    )
    return outputs, row_peak + jnp.log(row_total)


def attend_back(queries, keys, values, lse, grad_out):
    inv_root = HD ** (-0.5)
    scores = (
        jnp.einsum("qhd,khd->hqk", queries, keys, preferred_element_type=jnp.float32) * inv_root
    )
    attn_probs = jnp.exp(scores - lse)
    grad_probs = jnp.einsum("qhd,khd->hqk", grad_out, values, preferred_element_type=jnp.float32)
    row_delta = jnp.sum(attn_probs * grad_probs, axis=-1, keepdims=True)
    grad_scores = rounded(attn_probs * (grad_probs - row_delta))
    grad_query = (
        jnp.einsum("hqk,khd->qhd", grad_scores, keys, preferred_element_type=jnp.float32) * inv_root
    )
    grad_key = (
        jnp.einsum("hqk,qhd->khd", grad_scores, queries, preferred_element_type=jnp.float32)
        * inv_root
    )
    grad_value = jnp.einsum(
        "hqk,qhd->khd", rounded(attn_probs), grad_out, preferred_element_type=jnp.float32
    )
    return grad_query, grad_key, grad_value


def swap_core(tensor):
    return lax.ppermute(tensor, "seq", core_pairs)


def swap_chip(tensor):
    return lax.ppermute(tensor, "seq", chip_pairs)


def pick(tensor, index):
    return lax.dynamic_index_in_dim(tensor, index, 0, keepdims=False)


def spread_cols(own):
    far = swap_chip(own)
    near = swap_core(own)
    return jnp.concatenate([own, far, near, swap_core(far)], axis=-1)


def fold_cols(grad, weight):
    split = weight.shape[0] // 2
    half = split // 2
    away = matmul_back(grad, weight[split:])
    got = swap_core(rounded(away))
    keep = matmul_back(grad, weight[:split])
    far = swap_chip(rounded(keep[:, half:] + wide(got[:, half:])))
    total = keep[:, :half] + wide(got[:, :half]) + wide(far)
    return total, keep, away


def fold_rows(part, here):
    blocks = part.reshape(shards, part.shape[0] // shards, part.shape[1])
    away = rounded(jnp.stack([pick(blocks, here ^ 1), pick(blocks, here ^ 3)]))
    got = swap_core(away)
    far = swap_chip(rounded(pick(blocks, here ^ 2) + wide(got[1])))
    return pick(blocks, here) + wide(got[0]) + wide(far)


def place(blocks, here):
    filled = jnp.zeros((shards,) + blocks[0].shape, blocks[0].dtype)
    for distance, block in enumerate(blocks):
        filled = lax.dynamic_update_index_in_dim(filled, block, here ^ distance, 0)
    return filled


def gather_rows(own, here):
    far = swap_chip(own)
    near = swap_core(own)
    filled = place((own, near, far, swap_core(far)), here)
    return filled.reshape(shards * own.shape[0], own.shape[1])


def trade(pieces, here):
    received = [
        pick(pieces, here),
        swap_core(pick(pieces, here ^ 1)),
        swap_chip(pick(pieces, here ^ 2)),
        lax.ppermute(pick(pieces, here ^ 3), "seq", cross_pairs),
    ]
    return place(received, here)


def ring_order(count):
    return [0] + list(range(1, count, 2)) + list(range(count - 2, 0, -2))


def ring_tables(count):
    order = ring_order(count)
    spot = [order.index(index) for index in range(count)]
    up = tuple((order[step], order[(step + 1) % count]) for step in range(count))
    down = tuple((after, before) for before, after in up)
    return order, spot, up, down


class Ring:

    def __init__(self, count):
        self.count = count
        self.direct = count > 16
        order, spot, self.up, self.down = ring_tables(count)
        self.order = jnp.array(order, jnp.int32)
        self.at = jnp.array(spot, jnp.int32)[lax.axis_index("img")]

    def owner(self, offset):
        return self.order[(self.at + offset + self.count) % self.count]

    def gather(self, shard, slots):
        count = self.count
        rows = shard.shape[0]
        if self.direct:
            whole = lax.all_gather(shard, "img", axis=0)
            back = jnp.argsort(slots(jnp.arange(count, dtype=jnp.int32)))
            return jnp.take(whole, back, axis=0), whole[0]
        filled = jnp.zeros((count,) + shard.shape, shard.dtype)

        def put(target, block, offset, row=0):
            start = (slots(self.owner(offset)), row) + (0,) * (shard.ndim - 1)
            return lax.dynamic_update_slice(target, block[None], start)

        filled = put(filled, shard, 0)
        upward, downward = shard, shard
        mark = None
        for step in range(1, count // 2):
            upward = lax.ppermute(upward, "img", self.up)
            downward = lax.ppermute(downward, "img", self.down)
            filled = put(filled, upward, -step)
            filled = put(filled, downward, step)
            if step == 2:
                mark = upward
        top = lax.ppermute(upward[: rows // 2], "img", self.up)
        bottom = lax.ppermute(downward[rows // 2 :], "img", self.down)
        filled = put(filled, top, -(count // 2))
        filled = put(filled, bottom, -(count // 2), rows // 2)
        return filled, mark

    def scatter(self, block_of):
        count = self.count
        if self.direct:
            every = jnp.stack([block_of(index) for index in range(count)])
            return lax.psum_scatter(wide(every), "img", scatter_dimension=0, tiled=False)
        reach = count // 2
        first = block_of(self.owner(reach))
        rows = first.shape[0]
        upward = lax.ppermute(first[: rows // 2], "img", self.up)
        downward = lax.ppermute(first[rows // 2 :], "img", self.down)
        for step in range(2, reach + 1):
            ahead = wide(block_of(self.owner(reach - step + 1)))
            behind = wide(block_of(self.owner(step - reach - 1)))
            if step == 2:
                ahead = jnp.concatenate([ahead[: rows // 2] + wide(upward), ahead[rows // 2 :]])
                behind = jnp.concatenate(
                    [behind[: rows // 2], behind[rows // 2 :] + wide(downward)]
                )
            else:
                ahead = ahead + wide(upward)
                behind = behind + wide(downward)
            upward = lax.ppermute(rounded(ahead), "img", self.up)
            downward = lax.ppermute(rounded(behind), "img", self.down)
        return wide(block_of(self.owner(0))) + wide(upward) + wide(downward)


def after(tensor, mark):
    return lax.optimization_barrier((tensor, mark))[0]


def per_device(
    hidden_in,
    skip_in,
    text,
    condition,
    positions,
    out_grad,
    skip_gain,
    skip_bias,
    w_skip,
    w_mod,
    q_gain,
    k_gain,
    w_qkv,
    w_attn_out,
    cross_gain,
    cross_bias,
    w_cross_q,
    w_cross_kv,
    w_cross_out,
    w_fc1,
    w_fc2,
):
    here = lax.axis_index("seq")
    image = lax.axis_index("img")
    images = lax.axis_size("img")
    ring = Ring(images)
    per_shard = images // shards
    rows_here = D // images
    hidden_units = w_fc2.shape[0] // shards
    tokens = shards * hidden_in.shape[1]
    relative = here ^ jnp.array([0, 2, 1, 3], jnp.int32)

    def straight(index):
        return index

    def turned(index):
        shard = (index // per_shard) ^ here
        shard = jnp.where(shard == 1, 2, jnp.where(shard == 2, 1, shard))
        return shard * per_shard + index % per_shard

    def own_part(vector):
        return pick(vector.reshape(shards, own_cols), here)

    def relative_part(vector):
        return jnp.take(vector.reshape(shards, own_cols), relative, axis=0).reshape(D)

    joined = gather_rows(jnp.concatenate([hidden_in[0], skip_in[0]], axis=-1), here)
    grid_pos = lax.all_gather(positions[0], "seq", axis=0, tiled=True)
    cotangent = lax.all_gather(out_grad[0], "seq", axis=0, tiled=True)

    cond_vec = wide(condition[0])
    cond_low = rounded(jax.nn.silu(cond_vec))
    cond_all = lax.all_gather(cond_low, "img", axis=0)
    cond_rows = lax.dynamic_slice_in_dim(cond_all, image * rows_here, rows_here, 1)
    mod_low = rounded(w_mod)
    mod_part = matmul(cond_rows, mod_low)
    mod_own = lax.psum_scatter(mod_part, "img", scatter_dimension=0, tiled=True)
    modul = lax.all_gather(mod_own[0], "seq", axis=0, tiled=True).reshape(6, D)

    skip_all, mark = ring.gather(rounded(w_skip), straight)
    qkv_here = rounded(w_qkv).reshape(rows_here, 3, own_cols)
    odd = here % 2
    kept = jnp.where(odd == 1, qkv_here[:, 2], qkv_here[:, 0])
    sent = jnp.where(odd == 1, qkv_here[:, 0], qkv_here[:, 2])
    qkv_mix = jnp.stack([kept, swap_core(qkv_here[:, 1]), swap_chip(sent)])
    qkv_order = jnp.array([[0, 1, 2], [1, 0, 2], [2, 0, 1], [2, 1, 0]], jnp.int32)[here]
    qkv_own = jnp.take(qkv_mix, qkv_order, axis=0)
    qkv_all, mark = ring.gather(after(jnp.swapaxes(qkv_own, 0, 1), mark), turned)
    qkv_all = qkv_all.reshape(D, 3 * own_cols)
    small = jnp.concatenate(
        [rounded(w_attn_out), rounded(w_cross_q), rounded(w_cross_out)], axis=-1
    )
    small_all, mark = ring.gather(after(small, mark), turned)
    small_all = small_all.reshape(D, 3 * own_cols)
    attn_out_all = small_all[:, :own_cols]
    cross_q_all = small_all[:, own_cols : 2 * own_cols]
    cross_out_all = small_all[:, 2 * own_cols :]
    crosskv_all, mark = ring.gather(after(rounded(w_cross_kv), mark), straight)
    crosskv_all = crosskv_all.reshape(-1, 2 * own_cols)
    fc1_pieces = rounded(w_fc1).reshape(rows_here, per_shard, shards, -1)
    fc1_pieces = jnp.moveaxis(fc1_pieces, 2, 0).reshape(shards, rows_here, -1)
    fc1_own = jnp.swapaxes(trade(fc1_pieces, here), 0, 1).reshape(rows_here, -1)
    fc1_all, mark = ring.gather(after(fc1_own, mark), turned)
    fc1_all = fc1_all.reshape(D, -1)
    fc2_pieces = rounded(w_fc2).reshape(shards, hidden_units, own_cols)
    fc2_own = jnp.swapaxes(trade(fc2_pieces, here), 0, 1).reshape(hidden_units, D)
    fc2_all, mark = ring.gather(after(fc2_own, mark), straight)
    fc2_all = fc2_all.reshape(-1, D)

    joined_mid, joined_inv = norm_stats(wide(joined))
    joined_norm = (wide(joined) - joined_mid) * joined_inv
    cat_low = rounded(joined_norm * skip_gain + skip_bias)
    one_own = matmul(cat_low, skip_all.reshape(-1, own_cols))
    mod_rel = jnp.take(modul.reshape(6, shards, own_cols), relative, axis=1).reshape(6, D)
    shift_one, scale_one, gate_one = mod_rel[0], mod_rel[1], mod_rel[2, :own_cols]
    shift_two, scale_two = mod_rel[3], mod_rel[4]
    gate_two = modul[5]
    one_low = spread_cols(rounded(one_own))
    one_mid, one_inv = norm_stats(wide(one_low))
    one_norm = (wide(one_low) - one_mid) * one_inv
    attn_in = rounded(one_norm * (1.0 + scale_one) + shift_one)
    qkv_raw = matmul(attn_in, qkv_all)
    query_raw = by_heads(qkv_raw[:, :own_cols])
    key_raw = by_heads(qkv_raw[:, own_cols : 2 * own_cols])
    values = by_heads(rounded(qkv_raw[:, 2 * own_cols :]))
    query_low = rounded(head_rope(query_raw, q_gain, grid_pos))
    key_low = rounded(head_rope(key_raw, k_gain, grid_pos))
    attn_raw, self_lse = attend(query_low, key_low, values)
    attn_low = spread_cols(rounded(attn_raw.reshape(tokens, own_cols)))
    branch_own = matmul(attn_low, attn_out_all)
    two_own = one_own + gate_one * branch_own
    two_low = spread_cols(rounded(two_own))
    two_mid, two_inv = norm_stats(wide(two_low))
    two_norm = (wide(two_low) - two_mid) * two_inv
    cross_gain_rel = relative_part(cross_gain)
    cross_in = rounded(two_norm * cross_gain_rel + relative_part(cross_bias))
    cross_query = by_heads(rounded(matmul(cross_in, cross_q_all)))
    text_low = rounded(matmul(text[0], crosskv_all))
    text_keys = by_heads(text_low[:, :own_cols])
    text_values = by_heads(text_low[:, own_cols:])
    cross_raw, cross_lse = attend(cross_query, text_keys, text_values)
    cross_low = spread_cols(rounded(cross_raw.reshape(tokens, own_cols)))
    three_own = two_own + matmul(cross_low, cross_out_all)
    three_low = spread_cols(rounded(three_own))
    three_mid, three_inv = norm_stats(wide(three_low))
    three_norm = (wide(three_low) - three_mid) * three_inv
    mlp_in = rounded(three_norm * (1.0 + scale_two) + shift_two)
    upper = matmul(mlp_in, fc1_all)
    act_low = rounded(jax.nn.gelu(upper, approximate=True))
    mlp_part = matmul(act_low, fc2_all)
    mlp_rows = fold_rows(mlp_part, here)
    three_rows = lax.dynamic_slice_in_dim(three_low, here * hidden_in.shape[1], hidden_in.shape[1], 0)
    three_rows = jnp.take(
        three_rows.reshape(-1, shards, own_cols),
        jnp.array([0, 2, 1, 3], jnp.int32)[here ^ jnp.arange(shards, dtype=jnp.int32)],
        axis=1,
    ).reshape(-1, D)
    block_out = rounded(wide(three_rows) + gate_two * mlp_rows)[None]

    cot_wide = wide(cotangent)
    d_gate_two = jnp.sum(cot_wide * mlp_part, axis=0)
    grad_mlp = rounded(cot_wide * gate_two)
    grad_act = matmul_back(grad_mlp, fc2_all)
    gelu_pair = jax.vjp(lambda upper_in: jax.nn.gelu(upper_in, approximate=True), upper)
    grad_upper = rounded(gelu_pair[1](grad_act)[0])

    def norm_back(grad, weight, gain_rel, norm_full, norm_inv, own):
        total, keep, away = fold_cols(grad, weight)
        half = D // 2
        kept = keep * gain_rel[:half]
        gone = away * gain_rel[half:]
        sums = jnp.stack(
            [
                jnp.sum(kept, axis=-1) + jnp.sum(gone, axis=-1),
                jnp.sum(kept * norm_full[:, :half], axis=-1)
                + jnp.sum(gone * norm_full[:, half:], axis=-1),
            ]
        )
        means = lax.psum(sums, "seq")[:, :, None] * (1.0 / D)
        scaled = total * gain_rel[:own_cols]
        grad_in = norm_inv * (scaled - means[0] - own * means[1])
        return grad_in, jnp.sum(total * own, axis=0), jnp.sum(total, axis=0)

    three_own_norm = (three_own - three_mid) * three_inv
    back_three, d_scale_two, d_shift_two = norm_back(
        grad_upper, fc1_all, 1.0 + scale_two, three_norm, three_inv, three_own_norm
    )
    cot_own = pick(jnp.moveaxis(cot_wide.reshape(tokens, shards, own_cols), 1, 0), here)
    grad_three = cot_own + back_three

    grad_cross = rounded(grad_three)
    grad_cross_attn = by_heads(rounded(fold_cols(grad_cross, cross_out_all)[0]))
    cross_back = attend_back(cross_query, text_keys, text_values, cross_lse, grad_cross_attn)
    grad_cquery = rounded(cross_back[0].reshape(tokens, own_cols))
    two_own_norm = (two_own - two_mid) * two_inv
    back_two, d_cross_gain, d_cross_bias = norm_back(
        grad_cquery, cross_q_all, cross_gain_rel, two_norm, two_inv, two_own_norm
    )
    grad_two = grad_three + back_two
    text_grad = rounded(
        jnp.concatenate(
            [cross_back[1].reshape(-1, own_cols), cross_back[2].reshape(-1, own_cols)], axis=-1
        )
    )
    text_part = matmul_back(text_grad, crosskv_all)
    grad_text = wide(lax.psum(rounded(text_part), "seq"))[None]

    d_gate_one = jnp.sum(grad_two * branch_own, axis=0)
    grad_branch = rounded(grad_two * gate_one)
    grad_attn = by_heads(rounded(fold_cols(grad_branch, attn_out_all)[0]))
    self_back = attend_back(query_low, key_low, values, self_lse, grad_attn)
    query_back = jax.vjp(
        lambda tensor, gain_vec: head_rope(tensor, gain_vec, grid_pos), query_raw, q_gain
    )[1](self_back[0])
    key_back = jax.vjp(
        lambda tensor, gain_vec: head_rope(tensor, gain_vec, grid_pos), key_raw, k_gain
    )[1](self_back[1])
    grad_qkv = rounded(
        jnp.concatenate(
            [
                query_back[0].reshape(tokens, own_cols),
                key_back[0].reshape(tokens, own_cols),
                self_back[2].reshape(tokens, own_cols),
            ],
            axis=-1,
        )
    )
    one_own_norm = (one_own - one_mid) * one_inv
    back_one, d_scale_one, d_shift_one = norm_back(
        grad_qkv, qkv_all, 1.0 + scale_one, one_norm, one_inv, one_own_norm
    )
    grad_one = rounded(grad_two + back_one)

    cat_part = matmul_back(grad_one, skip_all.reshape(-1, own_cols))
    d_skip_gain = jnp.sum(cat_part * joined_norm, axis=0)
    d_skip_bias = jnp.sum(cat_part, axis=0)
    cat_rows = fold_rows(cat_part, here)
    joined_here = wide(jnp.concatenate([hidden_in[0], skip_in[0]], axis=-1))
    here_mid, here_inv = norm_stats(joined_here)
    here_norm = (joined_here - here_mid) * here_inv
    cat_scaled = cat_rows * skip_gain
    grad_joined = here_inv * (
        cat_scaled
        - jnp.mean(cat_scaled, axis=-1, keepdims=True)
        - here_norm * jnp.mean(cat_scaled * here_norm, axis=-1, keepdims=True)
    )
    grad_hidden = grad_joined[:, :D][None]
    grad_skip = grad_joined[:, D:][None]

    dmod_sent = jnp.concatenate(
        [d_shift_one, d_scale_one, d_gate_one, d_shift_two, d_scale_two, d_gate_two]
    )
    dmod_all = lax.all_gather(dmod_sent, ("img", "seq"), axis=0).reshape(images, shards, -1)
    five = dmod_all[:, :, : 5 * own_cols].reshape(images, shards, 5, own_cols)
    five = jnp.swapaxes(five, 1, 2).reshape(images, 5 * D)
    dmod_all = jnp.concatenate([five, jnp.sum(dmod_all[:, :, 5 * own_cols :], axis=1)], axis=-1)
    cols_here = w_mod.shape[1]
    dmod_cols = lax.dynamic_slice_in_dim(dmod_all, here * cols_here, cols_here, 1)
    grad_mod = jnp.einsum(
        "nr,nc->rc",
        wide(cond_rows),
        dmod_cols,
        precision=lax.Precision.HIGHEST,
        preferred_element_type=jnp.float32,
    )
    cond_part = jnp.einsum(
        "nc,rc->nr",
        dmod_cols,
        wide(mod_low),
        precision=lax.Precision.HIGHEST,
        preferred_element_type=jnp.float32,
    )
    cond_sum = lax.all_gather(lax.psum(cond_part, "seq"), "img", axis=1)
    cond_grad = pick(cond_sum, image).reshape(D)
    grad_condition = jax.vjp(jax.nn.silu, cond_vec)[1](cond_grad)[0][None]

    def settle(grads, slots):
        blocks = grads.reshape((images, grads.shape[0] // images) + grads.shape[1:])
        return ring.scatter(lambda index: pick(blocks, slots(index)))

    fc2_sum = settle(contract(act_low, grad_mlp), straight)
    fc2_back = trade(
        jnp.swapaxes(rounded(fc2_sum).reshape(hidden_units, shards, own_cols), 0, 1), here
    )
    grad_fc2 = wide(fc2_back).reshape(-1, own_cols)
    fc1_sum = settle(contract(mlp_in, grad_upper), turned)
    fc1_back = trade(jnp.swapaxes(rounded(fc1_sum).reshape(rows_here, shards, -1), 0, 1), here)
    fc1_back = jnp.moveaxis(fc1_back.reshape(shards, rows_here, per_shard, -1), 0, 2)
    grad_fc1 = wide(fc1_back).reshape(rows_here, -1)
    grad_cross_out = settle(contract(cross_low, grad_cross), turned)
    grad_cross_q = settle(contract(cross_in, grad_cquery), turned)
    grad_crosskv = settle(contract(text[0], text_grad), straight).reshape(-1, 2, own_cols)
    grad_attn_out = settle(contract(attn_low, grad_branch), turned)
    qkv_sum = settle(contract(attn_in, grad_qkv), turned).reshape(rows_here, 3, own_cols)
    qkv_sum = jnp.take(rounded(jnp.swapaxes(qkv_sum, 0, 1)), jnp.argsort(qkv_order), axis=0)
    middle = swap_core(qkv_sum[1])
    other = swap_chip(qkv_sum[2])
    low_end = jnp.where(odd == 1, other, qkv_sum[0])
    high_end = jnp.where(odd == 1, qkv_sum[0], other)
    grad_w_qkv = wide(jnp.concatenate([low_end, middle, high_end], axis=-1))
    grad_w_skip = settle(contract(cat_low, grad_one), straight)

    gains = jnp.concatenate(
        [d_skip_gain, d_skip_bias, query_back[1], key_back[1], d_cross_gain, d_cross_bias]
    )
    gains = lax.all_gather(gains, ("img", "seq"), axis=0)
    summed = jnp.sum(gains[:, : 4 * D + 2 * HD], axis=0)
    cross_gains = jnp.sum(gains[:, 4 * D + 2 * HD :].reshape(images, shards, 2, own_cols), axis=0)
    cross_gains = jnp.swapaxes(cross_gains, 0, 1).reshape(2, D)

    return (
        block_out,
        grad_hidden,
        grad_skip,
        grad_text,
        grad_condition,
        summed[: 2 * D],
        summed[2 * D : 4 * D],
        grad_w_skip,
        grad_mod,
        summed[4 * D : 4 * D + HD],
        summed[4 * D + HD :],
        grad_w_qkv,
        grad_attn_out,
        cross_gains[0],
        cross_gains[1],
        grad_cross_q,
        grad_crosskv,
        grad_cross_out,
        grad_fc1,
        grad_fc2,
    )


def solution(mesh):
    in_specs = (
        P("img", "seq", None),
        P("img", "seq", None),
        P("img", None, None),
        P("img", None),
        P("img", "seq", None),
        P("img", "seq", None),
        P(),
        P(),
        P("img", "seq"),
        P("img", "seq"),
        P(),
        P(),
        P("img", "seq"),
        P("img", "seq"),
        P(),
        P(),
        P("img", "seq"),
        P("img", None, "seq"),
        P("img", "seq"),
        P("img", "seq"),
        P("img", "seq"),
    )
    out_specs = (
        P("img", "seq", None),
        P("img", "seq", None),
        P("img", "seq", None),
        P("img", None, None),
        P("img", None),
        P(),
        P(),
        P("img", "seq"),
        P("img", "seq"),
        P(),
        P(),
        P("img", "seq"),
        P("img", "seq"),
        P(),
        P(),
        P("img", "seq"),
        P("img", None, "seq"),
        P("img", "seq"),
        P("img", "seq"),
        P("img", "seq"),
    )
    return jax.shard_map(
        per_device, mesh=mesh, in_specs=in_specs, out_specs=out_specs, check_vma=False
    )
```

```python
import functools
import math

import jax
import jax.numpy as jnp
import numpy as np
from jax import lax
from jax.experimental import pallas as pl
from jax.experimental.pallas import tpu as pltpu
from jax.sharding import PartitionSpec as P

D = 1408
H = 16
HD = 88

norm_eps = 1e-06
shards = 4
own_cols = D // shards
own_heads = H // shards
head_rows = 96
half_rows = head_rows // 2
quarter = HD // 4
padded_cols = own_heads * head_rows
vmem_bytes = 56 * 1024 * 1024
gelu_root = math.sqrt(2.0 / math.pi)
gelu_cube = 0.044715
log2_scale = HD ** (-0.5) / math.log(2.0)

core_pairs = ((0, 1), (1, 0), (2, 3), (3, 2))
chip_pairs = ((0, 2), (2, 0), (1, 3), (3, 1))
cross_pairs = ((0, 3), (3, 0), (1, 2), (2, 1))


def rounded(tensor):
    return tensor.astype(jnp.bfloat16)


def wide(tensor):
    return tensor.astype(jnp.float32)


def weigh(weights, tensors):
    return sum(
        jnp.einsum("kn,kt->nt", weight, tensor, preferred_element_type=jnp.float32)
        for weight, tensor in zip(weights, tensors)
    )


def weigh_back(weight, grad):
    return jnp.einsum("kn,nt->kt", weight, grad, preferred_element_type=jnp.float32)


def contract(left, right):
    return rounded(jnp.einsum("kt,nt->kn", left, right, preferred_element_type=jnp.float32))


def contract_pair(lefts, right):
    return tuple(contract(left, right) for left in lefts)


def norm_stats(tensor, axis):
    middle = jnp.mean(tensor, axis=axis, keepdims=True)
    center = tensor - middle
    spread = jnp.mean(center * center, axis=axis, keepdims=True)
    return middle, lax.rsqrt(spread + norm_eps)


def by_heads(tensor):
    return tensor.reshape(own_heads, HD, tensor.shape[-1])


def attend(queries, keys, values):
    scores = jnp.einsum(
        "hdk,hdq->hkq", keys, queries, preferred_element_type=jnp.float32
    ) * HD ** (-0.5)
    peak = jnp.max(scores, axis=1, keepdims=True)
    exp_scores = jnp.exp(scores - peak)
    total = jnp.sum(exp_scores, axis=1, keepdims=True)
    attn_probs = exp_scores / total
    outputs = jnp.einsum(
        "hdk,hkq->hdq", values, rounded(attn_probs), preferred_element_type=jnp.float32
    )
    return outputs, peak + jnp.log(total)


def attend_back(queries, keys, values, lse, grad_out):
    inv_root = HD ** (-0.5)
    scores = (
        jnp.einsum("hdk,hdq->hkq", keys, queries, preferred_element_type=jnp.float32) * inv_root
    )
    attn_probs = jnp.exp(scores - lse)
    grad_probs = jnp.einsum("hdk,hdq->hkq", values, grad_out, preferred_element_type=jnp.float32)
    delta = jnp.sum(attn_probs * grad_probs, axis=1, keepdims=True)
    grad_scores = rounded(attn_probs * (grad_probs - delta))
    grad_query = (
        jnp.einsum("hdk,hkq->hdq", keys, grad_scores, preferred_element_type=jnp.float32) * inv_root
    )
    grad_key = (
        jnp.einsum("hdq,hkq->hdk", queries, grad_scores, preferred_element_type=jnp.float32)
        * inv_root
    )
    grad_value = jnp.einsum(
        "hdq,hkq->hdk", grad_out, rounded(attn_probs), preferred_element_type=jnp.float32
    )
    return grad_query, grad_key, grad_value


def turned_rows():
    entry = np.arange(HD)
    axis, place = entry // (2 * quarter), entry % (2 * quarter)
    return (place // quarter) * half_rows + axis * quarter + place % quarter


def column_map(rows_of_entry):
    spread = np.zeros((own_cols, padded_cols), np.float32)
    for head in range(own_heads):
        spread[head * HD + np.arange(HD), head * head_rows + rows_of_entry] = 1.0
    return jnp.asarray(spread, jnp.bfloat16)


def select(left, right):
    return rounded(jnp.dot(left, right, preferred_element_type=jnp.float32))


def dot_across(left, right):
    return jnp.dot(left, right, preferred_element_type=jnp.float32)


def turn_head(raw, gain, cosine, sine_part):
    row = lax.broadcasted_iota(jnp.int32, raw.shape, 0)
    used = jnp.where(row % half_rows < 2 * quarter, 1.0, 0.0)
    center = (raw - jnp.sum(raw, axis=0, keepdims=True) * (1.0 / HD)) * used
    spread = jnp.sum(center * center, axis=0, keepdims=True) * (1.0 / HD)
    inverse = lax.rsqrt(spread + norm_eps)
    normed = center * inverse
    scaled = normed * gain
    first, second = scaled[:half_rows], scaled[half_rows:]
    turned = jnp.concatenate(
        [first * cosine - second * sine_part, first * sine_part + second * cosine], axis=0
    )
    return turned, normed, inverse, used


def turn_head_back(grad, normed, inverse, used, gain, cosine, sine_part):
    first, second = grad[:half_rows], grad[half_rows:]
    straight = jnp.concatenate(
        [first * cosine + second * sine_part, second * cosine - first * sine_part], axis=0
    )
    gain_grad = jnp.sum(straight * normed, axis=1, keepdims=True)
    scaled = straight * gain
    middle = jnp.sum(scaled, axis=0, keepdims=True) * (1.0 / HD)
    along = jnp.sum(scaled * normed, axis=0, keepdims=True) * (1.0 / HD)
    return inverse * (scaled - middle - normed * along) * used, gain_grad


key_chunk = 256


def attend_body(raw_ref, gain_ref, cos_ref, sin_ref, out_ref, low_ref, total_ref):
    cosine, sine_part = cos_ref[...], sin_ref[...]
    query = rounded(turn_head(raw_ref[0, 0], gain_ref[0], cosine, sine_part)[0])
    key_wide = turn_head(raw_ref[1, 0], gain_ref[1], cosine, sine_part)[0]
    value = rounded(raw_ref[2, 0])
    low_ref[0, 0] = query
    low_ref[1, 0] = rounded(key_wide)
    low_ref[2, 0] = value
    key_rows = rounded(key_wide.T)
    tokens = query.shape[1]
    total = jnp.zeros((1, tokens), jnp.float32)
    output = jnp.zeros((head_rows, tokens), jnp.float32)
    for start in range(0, tokens, key_chunk):
        scores = dot_across(key_rows[start : start + key_chunk], query)
        weights = jnp.exp2(scores * log2_scale)
        total = total + jnp.sum(weights, axis=0, keepdims=True)
        output = output + dot_across(value[:, start : start + key_chunk], rounded(weights))
    inverse = 1.0 / total
    total_ref[0] = inverse
    out_ref[0] = rounded((output * inverse)[:HD])


def attend_heads(raw, gains, cosine, sine_part):
    tokens = raw.shape[-1]
    heads = raw.shape[1]
    whole = lambda head: (0, 0)
    return pl.pallas_call(
        attend_body,
        grid=(heads,),
        out_shape=[
            jax.ShapeDtypeStruct((heads, HD, tokens), jnp.bfloat16),
            jax.ShapeDtypeStruct(raw.shape, jnp.bfloat16),
            jax.ShapeDtypeStruct((heads, 1, tokens), jnp.float32),
        ],
        in_specs=[
            pl.BlockSpec((3, 1, head_rows, tokens), lambda head: (0, head, 0, 0)),
            pl.BlockSpec((2, head_rows, 1), lambda head: (0, 0, 0)),
            pl.BlockSpec((half_rows, tokens), whole),
            pl.BlockSpec((half_rows, tokens), whole),
        ],
        out_specs=[
            pl.BlockSpec((1, HD, tokens), lambda head: (head, 0, 0)),
            pl.BlockSpec((3, 1, head_rows, tokens), lambda head: (0, head, 0, 0)),
            pl.BlockSpec((1, 1, tokens), lambda head: (head, 0, 0)),
        ],
        compiler_params=pltpu.CompilerParams(vmem_limit_bytes=vmem_bytes),
        cost_estimate=pl.CostEstimate(
            flops=4 * heads * tokens * tokens * 256,
            bytes_accessed=heads * tokens * 2000,
            transcendentals=heads * tokens * tokens,
        ),
    )(raw, gains, cosine, sine_part)


def attend_back_body(
    raw_ref, low_ref, total_ref, grad_ref, gain_ref, cos_ref, sin_ref, back_ref, gains_ref
):
    cosine, sine_part = cos_ref[...], sin_ref[...]
    query, key, value = low_ref[0, 0], low_ref[1, 0], low_ref[2, 0]
    tokens = query.shape[1]
    inverse_total = total_ref[0]
    grad_wide = wide(grad_ref[0])
    grad_wide = jnp.concatenate(
        [grad_wide, jnp.zeros((head_rows - HD, tokens), jnp.float32)], axis=0
    )
    grad = rounded(grad_wide)
    query_rows = rounded(wide(query).T)
    key_rows = rounded(wide(key).T)
    value_rows = rounded(wide(value).T)
    grad_rows = rounded(grad_wide.T)
    query_back = jnp.zeros((head_rows, tokens), jnp.float32)
    key_back, value_back = [], []
    delta = jnp.zeros((1, tokens), jnp.float32)
    chunks = [slice(start, start + key_chunk) for start in range(0, tokens, key_chunk)]
    held = []
    for chunk in chunks:
        scores = dot_across(key_rows[chunk], query)
        probs = jnp.exp2(scores * log2_scale) * inverse_total
        grad_probs = dot_across(value_rows[chunk], grad)
        delta = delta + jnp.sum(probs * grad_probs, axis=0, keepdims=True)
        held.append((probs, grad_probs))
    for chunk, (probs, grad_probs) in zip(chunks, held):
        grad_scores = rounded(probs * (grad_probs - delta))
        query_back = query_back + dot_across(key[:, chunk], grad_scores)
        key_back.append(dot_across(grad_scores, query_rows))
        value_back.append(dot_across(rounded(probs), grad_rows))
    root = HD ** (-0.5)
    key_back = jnp.concatenate(key_back, axis=0).T * root
    value_back = jnp.concatenate(value_back, axis=0).T
    for index, turned in enumerate((query_back * root, key_back)):
        gain = gain_ref[index]
        _, normed, inverse, used = turn_head(raw_ref[index, 0], gain, cosine, sine_part)
        straight, gain_grad = turn_head_back(
            turned, normed, inverse, used, gain, cosine, sine_part
        )
        back_ref[index, 0] = rounded(straight)
        gains_ref[0, index] = gain_grad
    back_ref[2, 0] = rounded(value_back)


def attend_heads_back(raw, low, inverse_total, grad, gains, cosine, sine_part):
    heads, tokens = raw.shape[1], raw.shape[-1]
    three = pl.BlockSpec((3, 1, head_rows, tokens), lambda head: (0, head, 0, 0))
    one = lambda rows: pl.BlockSpec((1, rows, tokens), lambda head: (head, 0, 0))
    whole = pl.BlockSpec((half_rows, tokens), lambda head: (0, 0))
    return pl.pallas_call(
        attend_back_body,
        grid=(heads,),
        out_shape=[
            jax.ShapeDtypeStruct(raw.shape, jnp.bfloat16),
            jax.ShapeDtypeStruct((heads, 2, head_rows, 1), jnp.float32),
        ],
        in_specs=[
            three,
            three,
            one(1),
            one(HD),
            pl.BlockSpec((2, head_rows, 1), lambda head: (0, 0, 0)),
            whole,
            whole,
        ],
        out_specs=[three, pl.BlockSpec((1, 2, head_rows, 1), lambda head: (head, 0, 0, 0))],
        compiler_params=pltpu.CompilerParams(vmem_limit_bytes=vmem_bytes),
        cost_estimate=pl.CostEstimate(
            flops=10 * heads * tokens * tokens * 256,
            bytes_accessed=heads * tokens * 3000,
            transcendentals=heads * tokens * tokens,
        ),
    )(raw, low, inverse_total, grad, gains, cosine, sine_part)


def norm_body(scale_at, shift_at, *refs):
    blocks, (columns_ref, keep_ref, away_ref, mid_ref, inv_ref) = refs[:4], refs[4:]
    base = wide(blocks[0][0:1])
    total = jnp.zeros(base.shape, jnp.float32)
    square = jnp.zeros(base.shape, jnp.float32)
    for block in blocks:
        shifted = wide(block[...]) - base
        total = total + jnp.sum(shifted, axis=0, keepdims=True)
        square = square + jnp.sum(shifted * shifted, axis=0, keepdims=True)
    total = total * (1.0 / D)
    inverse = lax.rsqrt(square * (1.0 / D) - total * total + norm_eps)
    middle = base + total
    mid_ref[...] = middle
    inv_ref[...] = inverse
    for index, block in enumerate(blocks):
        target = (keep_ref, away_ref)[index // 2]
        inner = (index % 2) * own_cols
        rows = slice(index * own_cols, (index + 1) * own_cols)
        scale = columns_ref[rows, scale_at : scale_at + 1]
        shift = columns_ref[rows, shift_at : shift_at + 1]
        normed = (wide(block[...]) - middle) * inverse
        target[inner : inner + own_cols] = rounded(normed * scale + shift)


def norm_columns(blocks, columns, scale_at, shift_at):
    tokens = blocks[0].shape[1]
    tile = 256
    part = pl.BlockSpec((own_cols, tile), lambda step: (0, step))
    half = pl.BlockSpec((2 * own_cols, tile), lambda step: (0, step))
    row = pl.BlockSpec((1, tile), lambda step: (0, step))
    keep, away, middle, inverse = pl.pallas_call(
        functools.partial(norm_body, scale_at, shift_at),
        grid=(tokens // tile,),
        out_shape=[
            jax.ShapeDtypeStruct((2 * own_cols, tokens), jnp.bfloat16),
            jax.ShapeDtypeStruct((2 * own_cols, tokens), jnp.bfloat16),
            jax.ShapeDtypeStruct((1, tokens), jnp.float32),
            jax.ShapeDtypeStruct((1, tokens), jnp.float32),
        ],
        in_specs=[part] * 4 + [pl.BlockSpec(columns.shape, lambda step: (0, 0))],
        out_specs=[half, half, row, row],
        compiler_params=pltpu.CompilerParams(vmem_limit_bytes=vmem_bytes),
        cost_estimate=pl.CostEstimate(
            flops=10 * D * tokens, bytes_accessed=4 * D * tokens, transcendentals=0
        ),
    )(*blocks, columns)
    return (keep, away), middle, inverse


def joined_body(places_ref, *refs):
    blocks, (gain_ref, bias_ref, cat_ref, norm_ref) = refs[:4], refs[4:]
    for index, block in enumerate(blocks):
        tensor = wide(block[...])
        center = tensor - jnp.mean(tensor, axis=1, keepdims=True)
        spread = jnp.mean(center * center, axis=1, keepdims=True)
        normed = center * lax.rsqrt(spread + norm_eps)
        norm_ref[places_ref[index]] = rounded(normed)
        cat_ref[places_ref[index]] = rounded(normed * gain_ref[...] + bias_ref[...])


def norm_joined(blocks, places, gain, bias):
    rows, cols = blocks[0].shape
    tile = 64
    shape = jax.ShapeDtypeStruct((4, rows, cols), jnp.bfloat16)
    part = pl.BlockSpec((tile, cols), lambda step: (step, 0))
    vector = pl.BlockSpec((1, cols), lambda step: (0, 0))
    every = pl.BlockSpec((4, tile, cols), lambda step: (0, step, 0))
    cat_low, norm_low = pl.pallas_call(
        joined_body,
        grid=(rows // tile,),
        out_shape=[shape, shape],
        in_specs=[pl.BlockSpec(memory_space=pltpu.SMEM)] + [part] * 4 + [vector] * 2,
        out_specs=[every, every],
        compiler_params=pltpu.CompilerParams(vmem_limit_bytes=vmem_bytes),
        cost_estimate=pl.CostEstimate(
            flops=40 * rows * cols, bytes_accessed=24 * rows * cols, transcendentals=0
        ),
    )(places, *blocks, gain[None], bias[None])
    return cat_low.reshape(4 * rows, cols), norm_low.reshape(4 * rows, cols)


def swap_core(tensor):
    return lax.ppermute(tensor, "seq", core_pairs)


def swap_chip(tensor):
    return lax.ppermute(tensor, "seq", chip_pairs)


def pick(tensor, index):
    return lax.dynamic_index_in_dim(
        tensor, index, 0, keepdims=False, allow_negative_indices=False
    )


def part_at(tensor, start, size, axis):
    return lax.dynamic_slice_in_dim(tensor, start, size, axis, allow_negative_indices=False)


def in_pairs(blocks):
    return jnp.concatenate(blocks[:2]), jnp.concatenate(blocks[2:])


def spread_rows(own):
    far = swap_chip(own)
    near = swap_core(own)
    return own, far, near, swap_core(far)


def fold_features(grad, weights):
    half = own_cols
    away = weigh_back(weights[1], grad)
    got = swap_core(rounded(away))
    keep = weigh_back(weights[0], grad)
    far = swap_chip(rounded(keep[half:] + wide(got[half:])))
    total = keep[:half] + wide(got[:half]) + wide(far)
    return total, keep, away


def fold_tokens(part, here):
    blocks = part.reshape(shards, part.shape[0] // shards, part.shape[1])
    away = jnp.stack([rounded(pick(blocks, here ^ 1)), rounded(pick(blocks, here ^ 3))])
    got = swap_core(away)
    far = swap_chip(rounded(pick(blocks, here ^ 2) + wide(got[1])))
    return pick(blocks, here) + wide(got[0]) + wide(far)


def place(blocks, here):
    places = here ^ jnp.arange(shards, dtype=jnp.int32)
    rows = blocks[0].shape[0]
    moves = [(index, 0, index, 0, rows) for index in range(shards)]
    return move_blocks(blocks, moves, places, [(shards, rows, blocks[0].shape[1])], False)[0]


def gather_tokens(own, here):
    far = swap_chip(own)
    near = swap_core(own)
    return place((own, near, far, swap_core(far)), here)


def reorder(tensor, order, axis=0):
    return jnp.concatenate([part_at(tensor, index, 1, axis) for index in order], axis=axis)


def split_cols(tensor, parts):
    size = tensor.shape[1] // parts
    return jnp.stack([tensor[:, part * size : (part + 1) * size] for part in range(parts)])


def join_cols(blocks):
    return jnp.concatenate([blocks[part] for part in range(blocks.shape[0])], axis=1)


def gather_small(own, here):
    far = swap_chip(own)
    near = swap_core(own)
    blocks = jnp.stack([own, near, far, swap_core(far)])
    return reorder(blocks, [here ^ shard for shard in range(shards)])


def sum_small(own):
    pair = own + swap_core(own)
    return pair + swap_chip(pair)


def trade(pieces, here):
    received = [
        pick(pieces, here),
        swap_core(pick(pieces, here ^ 1)),
        swap_chip(pick(pieces, here ^ 2)),
        lax.ppermute(pick(pieces, here ^ 3), "seq", cross_pairs),
    ]
    return place(received, here)


def ring_tables(count):
    order = [0] + list(range(1, count, 2)) + list(range(count - 2, 0, -2))
    spot = [order.index(index) for index in range(count)]
    up = tuple((order[step], order[(step + 1) % count]) for step in range(count))
    down = tuple((after, before) for before, after in up)
    return order, spot, up, down


def move_blocks(sources, moves, places, shapes, paired):
    def body(places_ref, *refs):
        targets = refs[len(sources) :]
        for source, row, entry, inner, size, *rest in moves:
            target, lane = rest if rest else (0, 0)
            block = refs[source][pl.ds(row, size)]
            lanes = pl.ds(lane, block.shape[1])
            spot = places_ref[entry]
            if not paired:
                targets[target][spot, pl.ds(inner, size), lanes] = block
                continue
            half = shapes[target][0]

            @pl.when(spot < half)
            def store_first():
                targets[2 * target][spot, pl.ds(inner, size), lanes] = block

            @pl.when(spot >= half)
            def store_second():
                targets[2 * target + 1][spot - half, pl.ds(inner, size), lanes] = block

    copies = 2 if paired else 1
    dtype = sources[0].dtype
    size = sum(math.prod(shape) for shape in shapes) * copies
    return pl.pallas_call(
        body,
        out_shape=[jax.ShapeDtypeStruct(shape, dtype) for shape in shapes for _ in range(copies)],
        in_specs=[pl.BlockSpec(memory_space=pltpu.SMEM)]
        + [pl.BlockSpec(memory_space=pltpu.VMEM)] * len(sources),
        out_specs=[pl.BlockSpec(memory_space=pltpu.VMEM)] * (len(shapes) * copies),
        compiler_params=pltpu.CompilerParams(vmem_limit_bytes=vmem_bytes),
        cost_estimate=pl.CostEstimate(flops=0, bytes_accessed=4 * size, transcendentals=0),
    )(places, *sources)


def arrange_blocks(grads, tables, entries):
    rows = [grad[0].shape[1] for grad in grads]
    cols = grads[0][0].shape[2]
    flat = [array for grad in grads for array in grad]

    def body(*refs):
        tables_refs, array_refs, target = refs[: len(grads)], refs[len(grads) : -1], refs[-1]
        base, first = 0, 0
        for grad, table_ref, size in zip(grads, tables_refs, rows):
            for entry in range(entries):
                spot = table_ref[entry]
                begin = 0
                for index, array in enumerate(grad):
                    end = begin + array.shape[0]

                    @pl.when((spot >= begin) & (spot < end))
                    def store(index=index, begin=begin):
                        target[entry, pl.ds(base, size)] = array_refs[first + index][spot - begin]

                    begin = end
            base, first = base + size, first + len(grad)

    shape = (entries, sum(rows), cols)
    return pl.pallas_call(
        body,
        out_shape=jax.ShapeDtypeStruct(shape, flat[0].dtype),
        in_specs=[pl.BlockSpec(memory_space=pltpu.SMEM)] * len(grads)
        + [pl.BlockSpec(memory_space=pltpu.VMEM)] * len(flat),
        out_specs=pl.BlockSpec(memory_space=pltpu.VMEM),
        compiler_params=pltpu.CompilerParams(vmem_limit_bytes=vmem_bytes),
        cost_estimate=pl.CostEstimate(
            flops=0, bytes_accessed=4 * math.prod(shape), transcendentals=0
        ),
    )(*tables, *flat)


class Images:

    def __init__(self):
        self.count = lax.axis_size("img")
        self.here = lax.axis_index("img")
        self.bits = [1 << bit for bit in range((self.count - 1).bit_length())]
        self.direct = self.count > 16
        order, spot, self.up, self.down = ring_tables(self.count)
        self.order = order
        self.spot = spot


    def swap(self, tensor, bit):
        return lax.ppermute(
            tensor, "img", tuple((index, index ^ bit) for index in range(self.count))
        )

    def gather_small(self, own):
        held = own[None]
        for bit in self.bits:
            held = jnp.concatenate([held, self.swap(held, bit)])
        return held

    def scatter_small(self, terms):
        held = terms
        for bit in reversed(self.bits):
            held = held[:bit] + self.swap(held[bit:], bit)
        return held[0]

    def trade_small(self, rows):
        held = rows
        for bit in self.bits:
            split = held.reshape((-1, 2, bit) + rows.shape[1:])
            split = jnp.stack([split[:, 0], self.swap(split[:, 1], bit)], axis=1)
            held = split.reshape(rows.shape)
        return held

    def sum_small(self, own):
        for bit in self.bits:
            own = own + self.swap(own, bit)
        return own


    def places(self, slots, offsets):
        table = np.zeros((shards, self.count, len(offsets)), np.int32)
        for shard in range(shards):
            for image in range(self.count):
                for index, offset in enumerate(offsets):
                    owner = self.order[(self.spot[image] + offset) % self.count]
                    table[shard, image, index] = slots(shard, owner)
        table = jnp.asarray(table.reshape(shards * self.count, len(offsets)))
        return pick(table, lax.axis_index("seq") * self.count + self.here)

    def gather(self, shard, parts, slots, paired, beside=False):
        count = self.count
        rows, cols = shard.shape[0] // parts, shard.shape[1]
        copies = 2 if paired else 1
        if self.direct:
            whole = lax.all_gather(shard, "img", axis=0)
            table = np.zeros((shards, count), np.int32)
            for shard_index in range(shards):
                for image in range(count):
                    table[shard_index, slots(shard_index, image)] = image
            back = pick(jnp.asarray(table), lax.axis_index("seq"))
            whole = jnp.take(whole, back, axis=0)
            pieces = [whole[:, part * rows : (part + 1) * rows] for part in range(parts)]
            if beside:
                pieces = [jnp.concatenate(pieces, axis=-1)]
            placed = [half for piece in pieces for half in jnp.split(piece, copies)]
            mark = whole[0]
        else:
            reach = count // 2
            middle = (shard.shape[0] // 2 + 15) // 16 * 16
            blocks, offsets = [shard], [0]
            upward, downward = shard, shard
            mark = None
            for step in range(1, reach):
                upward = lax.ppermute(upward, "img", self.up)
                downward = lax.ppermute(downward, "img", self.down)
                blocks += [upward, downward]
                offsets += [-step, step]
                if step == 2:
                    mark = upward
            blocks += [
                lax.ppermute(upward[:middle], "img", self.up),
                lax.ppermute(downward[middle:], "img", self.down),
            ]
            offsets += [-reach, -reach]
            starts = [0] * (len(blocks) - 1) + [middle]
            moves = []
            for index, (block, start) in enumerate(zip(blocks, starts)):
                row = 0
                while row < block.shape[0]:
                    part, inner = divmod(start + row, rows)
                    size = min(rows - inner, block.shape[0] - row)
                    where = (0, part * cols) if beside else (part, 0)
                    moves.append((index, row, index, inner, size) + where)
                    row += size
            shapes = [(count // copies, rows, cols * (parts if beside else 1))]
            shapes = shapes * (1 if beside else parts)
            places = self.places(slots, offsets)
            placed = move_blocks(blocks, moves, places, shapes, paired)
        placed = [piece.reshape(-1, piece.shape[-1]) for piece in placed]
        if paired:
            placed = list(zip(placed[::2], placed[1::2]))
        return placed, mark

    def scatter(self, grads, slots, ties=()):
        count = self.count
        reach = count // 2
        if self.direct:
            table = np.zeros((shards, len(grads), count), np.int32)
            for shard in range(shards):
                for index, slots_of in enumerate(slots):
                    for image in range(count):
                        table[shard, index, image] = slots_of(shard, image)
            orders = pick(jnp.asarray(table), lax.axis_index("seq"))
            every = [
                jnp.take(jnp.concatenate(grad), orders[index], axis=0)
                for index, grad in enumerate(grads)
            ]
            every = wide(jnp.concatenate(every, axis=1))
            return lax.psum_scatter(every, "img", scatter_dimension=0, tiled=False)
        offsets = [reach]
        for step in range(2, reach + 1):
            offsets += [reach - step + 1, step - reach - 1]
        offsets.append(0)
        tables = [self.places(slots_of, offsets) for slots_of in slots]
        blocks = arrange_blocks(grads, tables, len(offsets))
        middle = (blocks.shape[1] // 2 + 15) // 16 * 16
        upward = lax.ppermute(blocks[0, :middle], "img", self.up)
        downward = lax.ppermute(blocks[0, middle:], "img", self.down)
        for step in range(2, reach + 1):
            ahead = wide(blocks[2 * step - 3])
            behind = wide(blocks[2 * step - 2])
            if ties:
                upward, downward = lax.optimization_barrier((upward, downward, ties[step - 2]))[:2]
            if step == 2:
                ahead = jnp.concatenate([ahead[:middle] + wide(upward), ahead[middle:]])
                behind = jnp.concatenate([behind[:middle], behind[middle:] + wide(downward)])
            else:
                ahead = ahead + wide(upward)
                behind = behind + wide(downward)
            upward = lax.ppermute(rounded(ahead), "img", self.up)
            downward = lax.ppermute(rounded(behind), "img", self.down)
        return wide(blocks[-1]) + wide(upward) + wide(downward)


def after(tensor, mark):
    return lax.optimization_barrier((tensor, mark))[0]


def per_device(
    hidden_in,
    skip_in,
    text,
    condition,
    positions,
    out_grad,
    skip_gain,
    skip_bias,
    w_skip,
    w_mod,
    q_gain,
    k_gain,
    w_qkv,
    w_attn_out,
    cross_gain,
    cross_bias,
    w_cross_q,
    w_cross_kv,
    w_cross_out,
    w_fc1,
    w_fc2,
):
    here = lax.axis_index("seq")
    images = Images()
    count = images.count
    per_shard = count // shards
    rows_here = D // count
    text_rows = w_cross_kv.shape[0]
    hidden_units = w_fc2.shape[0] // shards
    tokens_here = hidden_in.shape[1]
    tokens = shards * tokens_here
    relative = [here, here ^ 2, here ^ 1, here ^ 3]

    def straight(shard, index):
        return index

    def turned(shard, index):
        return (0, 2, 1, 3)[(index // per_shard) ^ shard] * per_shard + index % per_shard

    joined_here = jnp.concatenate([hidden_in[0], skip_in[0]], axis=-1)
    joined_far = swap_chip(joined_here)
    joined_near = swap_core(joined_here)
    joined = (joined_here, joined_near, joined_far, swap_core(joined_far))

    (skip_all,), mark = images.gather(rounded(w_skip), 1, straight, False)
    qkv_here = rounded(w_qkv)
    qkv_parts = split_cols(qkv_here, 3)
    turn_map, plain_map = column_map(turned_rows()), column_map(np.arange(HD))
    column_maps = jnp.stack([turn_map, turn_map, plain_map])
    odd = here % 2
    kept = jnp.where(odd == 1, qkv_parts[2], qkv_parts[0])
    sent = jnp.where(odd == 1, qkv_parts[0], qkv_parts[2])
    qkv_mix = jnp.stack([kept, swap_core(qkv_parts[1]), swap_chip(sent)])
    qkv_order = pick(np.array([[0, 1, 2], [1, 0, 2], [2, 0, 1], [2, 1, 0]], np.int32), here)
    qkv_home = pick(np.array([[0, 1, 2], [1, 0, 2], [1, 2, 0], [2, 1, 0]], np.int32), here)
    qkv_own = jnp.concatenate(
        [select(pick(qkv_mix, qkv_order[part]), column_maps[part]) for part in range(3)]
    )
    (qkv_all,), mark_qkv = images.gather(after(qkv_own, mark), 3, turned, True, True)
    small = jnp.concatenate([rounded(w_attn_out), rounded(w_cross_q), rounded(w_cross_out)])
    small_all, mark_small = images.gather(after(small, mark_qkv), 3, turned, True)
    attn_out_all, cross_q_all, cross_out_all = small_all
    crosskv = rounded(w_cross_kv)
    crosskv = jnp.concatenate([crosskv[:, 0], crosskv[:, 1]])
    crosskv_all, _ = images.gather(after(crosskv, mark_small), 2, straight, False)
    unit = np.arange(w_fc1.shape[1])
    image_of, inner = unit // (w_fc1.shape[1] // per_shard), unit % (w_fc1.shape[1] // per_shard)
    slot_of = (inner // hidden_units) * per_shard * hidden_units
    slot_of = slot_of + image_of * hidden_units + inner % hidden_units
    unit_map = np.zeros((w_fc1.shape[1], w_fc1.shape[1]), np.float32)
    unit_map[unit, slot_of] = 1.0
    unit_map = jnp.asarray(unit_map, jnp.bfloat16)
    fc1_pieces = split_cols(select(rounded(w_fc1), unit_map), shards)
    fc1_own = join_cols(trade(after(fc1_pieces, joined_far), here))
    fc2_pieces = rounded(w_fc2).reshape(shards, hidden_units, own_cols)
    fc2_own = join_cols(trade(after(fc2_pieces, joined_far), here))
    fc1_rows = lax.all_gather(fc1_own, "img", axis=0, tiled=True)
    fc1_rows = fc1_rows.reshape(shards, own_cols, -1)
    fc1_rows = [pick(fc1_rows, index) for index in relative]
    fc1_all = in_pairs(fc1_rows)
    fc2_all = lax.all_gather(fc2_own, "img", axis=0, tiled=True)

    cond_vec = wide(condition[0])
    cond_low = rounded(jax.nn.silu(cond_vec))
    cond_all = images.gather_small(cond_low)
    cond_rows = part_at(cond_all, images.here * rows_here, rows_here, 1)
    mod_low = rounded(w_mod)
    mod_part = jnp.dot(cond_rows, mod_low, preferred_element_type=jnp.float32)
    modul = gather_small(images.scatter_small(mod_part), here).reshape(6, D)

    places = here ^ jnp.arange(shards, dtype=jnp.int32)
    cat_low, joined_norm = norm_joined(joined, places, skip_gain, skip_bias)
    one_own = jnp.einsum("kn,tk->nt", skip_all, cat_low, preferred_element_type=jnp.float32)
    vectors = jnp.concatenate([modul, cross_gain[None], cross_bias[None]])
    one_plus = np.zeros((8, 1), np.float32)
    one_plus[[1, 4]] = 1.0
    columns = (vectors + one_plus).T
    columns = jnp.concatenate(
        [part_at(columns, index * own_cols, own_cols, 0) for index in relative]
    )
    shift_one, scale_one = columns[:, 0:1], columns[:, 1:2]
    shift_two, scale_two = columns[:, 3:4], columns[:, 4:5]
    cross_scale, cross_shift = columns[:, 6:7], columns[:, 7:8]
    gate_one = columns[:own_cols, 2:3]
    gate_two = modul[5]
    one_blocks = spread_rows(after(rounded(one_own), (fc1_own, fc2_own)))
    cotangent = gather_tokens(after(out_grad[0], one_blocks[1]), here).reshape(tokens, D)
    attn_in, one_mid, one_inv = norm_columns(one_blocks, columns, 1, 0)
    qkv_raw = weigh(qkv_all, attn_in).reshape(3, own_heads, head_rows, tokens)
    grid_pos = gather_small(after(positions[0].T, mark), here)
    grid_pos = jnp.swapaxes(grid_pos, 0, 1).reshape(2, tokens)
    frequency = 10000.0 ** (-jnp.arange(quarter, dtype=jnp.float32) / quarter)
    angles = grid_pos.astype(jnp.float32)[:, None, :] * frequency[:, None]
    angles = jnp.pad(angles.reshape(2 * quarter, tokens), ((0, half_rows - 2 * quarter), (0, 0)))
    cosine, sine_part = jnp.cos(angles), jnp.sin(angles)
    entry_rows = turned_rows()
    head_map = np.zeros((head_rows, HD), np.float32)
    head_map[entry_rows, np.arange(HD)] = 1.0
    row_entry = np.zeros(head_rows, np.int32)
    row_entry[entry_rows] = np.arange(HD)
    row_used = head_map.sum(1)
    gains_low = jnp.stack([q_gain[row_entry] * row_used, k_gain[row_entry] * row_used])[:, :, None]
    attn_raw, qkv_low, attn_total = attend_heads(qkv_raw, gains_low, cosine, sine_part)
    attn_low = in_pairs(spread_rows(attn_raw.reshape(own_cols, tokens)))
    branch_own = weigh(attn_out_all, attn_low)
    two_own = one_own + gate_one * branch_own
    cross_in, two_mid, two_inv = norm_columns(spread_rows(rounded(two_own)), columns, 6, 7)
    cross_query = by_heads(rounded(weigh(cross_q_all, cross_in)))
    text_keys, text_values = [
        by_heads(
            rounded(
                jnp.einsum("kn,tk->nt", weight, text[0], preferred_element_type=jnp.float32)
            )
        )
        for weight in crosskv_all
    ]
    cross_raw, cross_lse = attend(cross_query, text_keys, text_values)
    cross_low = in_pairs(spread_rows(rounded(cross_raw.reshape(own_cols, tokens))))
    three_own = two_own + weigh(cross_out_all, cross_low)
    cot_wide = wide(cotangent)
    grad_mlp = rounded(cot_wide * gate_two)
    three_low = spread_rows(after(rounded(three_own), (grad_mlp, fc1_all)))
    mlp_in, three_mid, three_inv = norm_columns(three_low, columns, 4, 3)
    upper = weigh(fc1_all, mlp_in)
    bend = jnp.tanh(gelu_root * (upper + gelu_cube * upper * upper * upper))
    act_low = rounded(0.5 * upper * (1.0 + bend))
    slope = 0.5 * (1.0 + bend) + 0.5 * upper * (1.0 - bend * bend) * gelu_root * (
        1.0 + 3.0 * gelu_cube * upper * upper
    )
    act_low, slope = lax.optimization_barrier((act_low, slope))
    mlp_part = jnp.einsum("ut,uc->tc", act_low, fc2_all, preferred_element_type=jnp.float32)

    d_gate_two = jnp.sum(cot_wide * mlp_part, axis=0)
    grad_act = jnp.einsum("uc,tc->ut", fc2_all, grad_mlp, preferred_element_type=jnp.float32)
    grad_upper = rounded(grad_act * slope)

    def norm_back(grad, weights, gain_rel, normed, shift, norm_inv, own):
        total, keep, away = fold_features(grad, weights)
        half = D // 2
        kept = keep * gain_rel[:half]
        gone = away * gain_rel[half:]
        sums = jnp.stack(
            [
                jnp.sum(kept, axis=0) + jnp.sum(gone, axis=0),
                jnp.sum(keep * (wide(normed[0]) - shift[:half]), axis=0)
                + jnp.sum(away * (wide(normed[1]) - shift[half:]), axis=0),
            ]
        )
        means = sum_small(sums) * (1.0 / D)
        scaled = total * gain_rel[:own_cols]
        grad_in = norm_inv * (scaled - means[:1] - own * means[1:])
        return grad_in, jnp.sum(total * own, axis=1), jnp.sum(total, axis=1)

    three_own_norm = (three_own - three_mid) * three_inv
    back_three, d_scale_two, d_shift_two = norm_back(
        grad_upper, fc1_all, scale_two, mlp_in, shift_two, three_inv, three_own_norm
    )
    canonical = jnp.arange(D, dtype=jnp.int32)
    own_map = canonical[:, None] == here * own_cols + canonical[None, :own_cols]
    cot_own = jnp.einsum(
        "tc,cn->nt", cotangent, rounded(own_map), preferred_element_type=jnp.float32
    )
    grad_three = cot_own + back_three

    grad_cross = rounded(grad_three)
    grad_cross_attn = by_heads(rounded(fold_features(grad_cross, cross_out_all)[0]))
    cross_back = attend_back(cross_query, text_keys, text_values, cross_lse, grad_cross_attn)
    grad_cquery = rounded(cross_back[0].reshape(own_cols, tokens))
    two_own_norm = (two_own - two_mid) * two_inv
    back_two, d_cross_gain, d_cross_bias = norm_back(
        grad_cquery, cross_q_all, cross_scale, cross_in, cross_shift, two_inv, two_own_norm
    )
    grad_two = grad_three + back_two
    text_grad = rounded(jnp.concatenate([cross_back[1], cross_back[2]])).reshape(2 * own_cols, -1)

    d_gate_one = jnp.sum(grad_two * branch_own, axis=1)
    grad_branch = rounded(grad_two * gate_one)
    grad_attn = by_heads(rounded(fold_features(grad_branch, attn_out_all)[0]))
    grad_qkv, gain_terms = attend_heads_back(
        qkv_raw, qkv_low, attn_total, grad_attn, gains_low, cosine, sine_part
    )
    grad_qkv = grad_qkv.reshape(3 * padded_cols, tokens)
    gain_terms = jnp.sum(gain_terms[..., 0], axis=0)
    d_q_gain, d_k_gain = gain_terms[0][entry_rows], gain_terms[1][entry_rows]
    one_own_norm = (one_own - one_mid) * one_inv
    back_one, d_scale_one, d_shift_one = norm_back(
        grad_qkv, qkv_all, scale_one, attn_in, shift_one, one_inv, one_own_norm
    )
    grad_one = rounded(grad_two + back_one)

    cat_part = jnp.einsum("nt,kn->tk", grad_one, skip_all, preferred_element_type=jnp.float32)
    d_skip_gain = jnp.sum(cat_part * wide(joined_norm), axis=0)
    d_skip_bias = jnp.sum(cat_part, axis=0)
    cat_rows = fold_tokens(cat_part, here)
    here_wide = wide(joined_here)
    here_mid, here_inv = norm_stats(here_wide, 1)
    here_norm = (here_wide - here_mid) * here_inv
    cat_scaled = cat_rows * skip_gain
    grad_joined = here_inv * (
        cat_scaled
        - jnp.mean(cat_scaled, axis=-1, keepdims=True)
        - here_norm * jnp.mean(cat_scaled * here_norm, axis=-1, keepdims=True)
    )
    grad_hidden = grad_joined[:, :D][None]
    grad_skip = grad_joined[:, D:][None]

    dmod_sent = jnp.concatenate(
        [d_shift_one, d_scale_one, d_gate_one, d_shift_two, d_scale_two, d_gate_two]
    )
    dmod_seq = gather_small(dmod_sent, here)
    five = dmod_seq[:, : 5 * own_cols].reshape(shards, 5, own_cols)
    five = jnp.swapaxes(five, 0, 1).reshape(5 * D)
    dmod_full = jnp.concatenate([five, jnp.sum(dmod_seq[:, 5 * own_cols :], axis=0)])
    cols_here = w_mod.shape[1]
    dmod_cols = images.gather_small(
        part_at(dmod_full, here * cols_here, cols_here, 0)
    )
    grad_mod = jnp.einsum(
        "nr,nc->rc",
        wide(cond_rows),
        dmod_cols,
        precision=lax.Precision.HIGHEST,
        preferred_element_type=jnp.float32,
    )
    cond_part = jnp.einsum(
        "nc,rc->nr",
        dmod_cols,
        wide(mod_low),
        precision=lax.Precision.HIGHEST,
        preferred_element_type=jnp.float32,
    )
    cond_sum = sum_small(images.trade_small(cond_part))
    cond_grad = reorder(cond_sum, [images.here ^ image for image in range(count)]).reshape(D)
    grad_condition = jax.vjp(jax.nn.silu, cond_vec)[1](cond_grad)[0][None]

    def settle(grads, slots, ties=()):
        blocks = [
            tuple(part.reshape(-1, sum(p.shape[0] for p in grad) // count, part.shape[1]) for part in grad)
            for grad in grads
        ]
        return images.scatter(blocks, slots, ties)

    fc2_sum = lax.psum_scatter(
        contract(act_low, grad_mlp.T), "img", scatter_dimension=0, tiled=True
    )
    fc2_back = trade(split_cols(fc2_sum, shards), here)
    grad_fc2 = wide(fc2_back).reshape(-1, own_cols)
    fc1_part = move_blocks(
        contract_pair(mlp_in, grad_upper),
        [(index // 2, (index % 2) * own_cols, index, 0, own_cols) for index in range(shards)],
        jnp.stack(relative),
        [(shards, own_cols, w_fc1.shape[1])],
        False,
    )[0].reshape(D, -1)
    fc1_sum = lax.psum_scatter(fc1_part, "img", scatter_dimension=0, tiled=True)
    fc1_back = join_cols(trade(split_cols(fc1_sum, shards), here))
    grad_fc1 = jnp.dot(fc1_back, unit_map.T, preferred_element_type=jnp.float32)
    small_sum = settle(
        [
            contract_pair(attn_low, grad_branch),
            contract_pair(cross_in, grad_cquery),
            contract_pair(cross_low, grad_cross),
        ],
        [turned] * 3,
        (grad_attn, grad_qkv, grad_one),
    )
    grad_attn_out, grad_cross_q, grad_cross_out = jnp.split(small_sum, 3)
    kv_grads = [
        (rounded(jnp.einsum("tk,nt->kn", text[0], grad, preferred_element_type=jnp.float32)),)
        for grad in (text_grad[:own_cols], text_grad[own_cols:])
    ]
    kv_sum = settle(kv_grads, [straight] * 2)
    grad_crosskv = jnp.stack(jnp.split(kv_sum, 2), axis=1)
    qkv_sum = rounded(settle([contract_pair(attn_in, grad_qkv)], [turned]))
    qkv_sum = split_cols(qkv_sum, 3)
    qkv_sum = jnp.stack(
        [select(qkv_sum[part], column_maps[part].T) for part in range(3)]
    )
    stay = pick(qkv_sum, qkv_home[0])
    middle = swap_core(pick(qkv_sum, qkv_home[1]))
    other = swap_chip(pick(qkv_sum, qkv_home[2]))
    low_end = jnp.where(odd == 1, other, stay)
    high_end = jnp.where(odd == 1, stay, other)
    grad_w_qkv = wide(jnp.concatenate([low_end, middle, high_end], axis=-1))
    skip_grad = jnp.einsum("tk,nt->kn", cat_low, grad_one, preferred_element_type=jnp.float32)
    grad_w_skip = settle([(rounded(skip_grad),)], [straight])

    text_part = sum(
        jnp.einsum("nt,kn->tk", grad, weight, preferred_element_type=jnp.float32)
        for grad, weight in zip((text_grad[:own_cols], text_grad[own_cols:]), crosskv_all)
    )
    grad_text = sum_small(rounded(text_part))
    grad_text = wide(grad_text)[None]
    mlp_rows = fold_tokens(after(mlp_part, grad_attn), here)
    three_here = jnp.concatenate(
        [part_at(block, here * tokens_here, tokens_here, 1) for block in after(three_low, grad_attn)]
    )
    place_of = jnp.concatenate([index * own_cols + canonical[:own_cols] for index in relative])
    feature_map = rounded(place_of[:, None] == canonical[None, :])
    three_here = jnp.einsum(
        "kt,kc->tc", three_here, feature_map, preferred_element_type=jnp.float32
    )
    block_out = rounded(three_here + gate_two * mlp_rows)[None]

    cross_gains = lax.dynamic_update_index_in_dim(
        jnp.zeros((shards, 2 * own_cols), jnp.float32),
        jnp.concatenate([d_cross_gain, d_cross_bias]),
        here,
        0,
    )
    gains = jnp.concatenate(
        [d_skip_gain, d_skip_bias, d_q_gain, d_k_gain, cross_gains.reshape(-1)]
    )
    gains = images.sum_small(sum_small(gains))
    cross_gains = gains[4 * D + 2 * HD :].reshape(shards, 2, own_cols)
    cross_gains = jnp.swapaxes(cross_gains, 0, 1).reshape(2, D)

    return (
        block_out,
        grad_hidden,
        grad_skip,
        grad_text,
        grad_condition,
        gains[: 2 * D],
        gains[2 * D : 4 * D],
        grad_w_skip,
        grad_mod,
        gains[4 * D : 4 * D + HD],
        gains[4 * D + HD : 4 * D + 2 * HD],
        grad_w_qkv,
        grad_attn_out,
        cross_gains[0],
        cross_gains[1],
        grad_cross_q,
        grad_crosskv,
        grad_cross_out,
        grad_fc1,
        grad_fc2,
    )


def solution(mesh):
    in_specs = (
        P("img", "seq", None),
        P("img", "seq", None),
        P("img", None, None),
        P("img", None),
        P("img", "seq", None),
        P("img", "seq", None),
        P(),
        P(),
        P("img", "seq"),
        P("img", "seq"),
        P(),
        P(),
        P("img", "seq"),
        P("img", "seq"),
        P(),
        P(),
        P("img", "seq"),
        P("img", None, "seq"),
        P("img", "seq"),
        P("img", "seq"),
        P("img", "seq"),
    )
    out_specs = (
        P("img", "seq", None),
        P("img", "seq", None),
        P("img", "seq", None),
        P("img", None, None),
        P("img", None),
        P(),
        P(),
        P("img", "seq"),
        P("img", "seq"),
        P(),
        P(),
        P("img", "seq"),
        P("img", "seq"),
        P(),
        P(),
        P("img", "seq"),
        P("img", None, "seq"),
        P("img", "seq"),
        P("img", "seq"),
        P("img", "seq"),
    )
    return jax.shard_map(
        per_device, mesh=mesh, in_specs=in_specs, out_specs=out_specs, check_vma=False
    )
```

```python
import functools
import math

import jax
import jax.numpy as jnp
import numpy as np
from jax import lax
from jax.experimental import pallas as pl
from jax.experimental.pallas import tpu as pltpu
from jax.sharding import PartitionSpec as P

D = 1408
H = 16
HD = 88

norm_eps = 1e-06
shards = 4
own_cols = D // shards
own_heads = H // shards
head_rows = 96
half_rows = head_rows // 2
quarter = HD // 4
padded_cols = own_heads * head_rows
vmem_bytes = 56 * 1024 * 1024
gelu_root = math.sqrt(2.0 / math.pi)
gelu_cube = 0.044715
log2_scale = HD ** (-0.5) / math.log(2.0)

core_pairs = ((0, 1), (1, 0), (2, 3), (3, 2))
chip_pairs = ((0, 2), (2, 0), (1, 3), (3, 1))
cross_pairs = ((0, 3), (3, 0), (1, 2), (2, 1))


def rounded(tensor):
    return tensor.astype(jnp.bfloat16)


def wide(tensor):
    return tensor.astype(jnp.float32)


def weigh(weights, tensors):
    return sum(
        jnp.einsum("kn,kt->nt", weight, tensor, preferred_element_type=jnp.float32)
        for weight, tensor in zip(weights, tensors)
    )


def weigh_back(weight, grad):
    return jnp.einsum("kn,nt->kt", weight, grad, preferred_element_type=jnp.float32)


def contract(left, right):
    return rounded(jnp.einsum("kt,nt->kn", left, right, preferred_element_type=jnp.float32))


def contract_pair(lefts, right):
    return tuple(contract(left, right) for left in lefts)


def norm_stats(tensor, axis):
    middle = jnp.mean(tensor, axis=axis, keepdims=True)
    center = tensor - middle
    spread = jnp.mean(center * center, axis=axis, keepdims=True)
    return middle, lax.rsqrt(spread + norm_eps)


def by_heads(tensor):
    return tensor.reshape(own_heads, HD, tensor.shape[-1])


def attend(queries, keys, values):
    scores = jnp.einsum(
        "hdk,hdq->hkq", keys, queries, preferred_element_type=jnp.float32
    ) * HD ** (-0.5)
    peak = jnp.max(scores, axis=1, keepdims=True)
    exp_scores = jnp.exp(scores - peak)
    total = jnp.sum(exp_scores, axis=1, keepdims=True)
    attn_probs = exp_scores / total
    outputs = jnp.einsum(
        "hdk,hkq->hdq", values, rounded(attn_probs), preferred_element_type=jnp.float32
    )
    return outputs, peak + jnp.log(total)


def attend_back(queries, keys, values, lse, grad_out):
    inv_root = HD ** (-0.5)
    scores = (
        jnp.einsum("hdk,hdq->hkq", keys, queries, preferred_element_type=jnp.float32) * inv_root
    )
    attn_probs = jnp.exp(scores - lse)
    grad_probs = jnp.einsum("hdk,hdq->hkq", values, grad_out, preferred_element_type=jnp.float32)
    delta = jnp.sum(attn_probs * grad_probs, axis=1, keepdims=True)
    grad_scores = rounded(attn_probs * (grad_probs - delta))
    grad_query = (
        jnp.einsum("hdk,hkq->hdq", keys, grad_scores, preferred_element_type=jnp.float32) * inv_root
    )
    grad_key = (
        jnp.einsum("hdq,hkq->hdk", queries, grad_scores, preferred_element_type=jnp.float32)
        * inv_root
    )
    grad_value = jnp.einsum(
        "hdq,hkq->hdk", grad_out, rounded(attn_probs), preferred_element_type=jnp.float32
    )
    return grad_query, grad_key, grad_value


def turned_rows():
    entry = np.arange(HD)
    axis, place = entry // (2 * quarter), entry % (2 * quarter)
    return (place // quarter) * half_rows + axis * quarter + place % quarter


def column_map(rows_of_entry):
    spread = np.zeros((own_cols, padded_cols), np.float32)
    for head in range(own_heads):
        spread[head * HD + np.arange(HD), head * head_rows + rows_of_entry] = 1.0
    return jnp.asarray(spread, jnp.bfloat16)


def select(left, right):
    return rounded(jnp.dot(left, right, preferred_element_type=jnp.float32))


def dot_across(left, right):
    return jnp.dot(left, right, preferred_element_type=jnp.float32)


def turn_head(raw, gain, cosine, sine_part):
    row = lax.broadcasted_iota(jnp.int32, raw.shape, 0)
    used = jnp.where(row % half_rows < 2 * quarter, 1.0, 0.0)
    center = (raw - jnp.sum(raw, axis=0, keepdims=True) * (1.0 / HD)) * used
    spread = jnp.sum(center * center, axis=0, keepdims=True) * (1.0 / HD)
    inverse = lax.rsqrt(spread + norm_eps)
    normed = center * inverse
    scaled = normed * gain
    first, second = scaled[:half_rows], scaled[half_rows:]
    turned = jnp.concatenate(
        [first * cosine - second * sine_part, first * sine_part + second * cosine], axis=0
    )
    return turned, normed, inverse, used


def turn_head_back(grad, normed, inverse, used, gain, cosine, sine_part):
    first, second = grad[:half_rows], grad[half_rows:]
    straight = jnp.concatenate(
        [first * cosine + second * sine_part, second * cosine - first * sine_part], axis=0
    )
    gain_grad = jnp.sum(straight * normed, axis=1, keepdims=True)
    scaled = straight * gain
    middle = jnp.sum(scaled, axis=0, keepdims=True) * (1.0 / HD)
    along = jnp.sum(scaled * normed, axis=0, keepdims=True) * (1.0 / HD)
    return inverse * (scaled - middle - normed * along) * used, gain_grad


key_chunk = 256


def attend_body(raw_ref, gain_ref, cos_ref, sin_ref, out_ref, low_ref, total_ref):
    cosine, sine_part = cos_ref[...], sin_ref[...]
    query = rounded(turn_head(raw_ref[0, 0], gain_ref[0], cosine, sine_part)[0])
    key_wide = turn_head(raw_ref[1, 0], gain_ref[1], cosine, sine_part)[0]
    value = rounded(raw_ref[2, 0])
    low_ref[0, 0] = query
    low_ref[1, 0] = rounded(key_wide)
    low_ref[2, 0] = value
    key_rows = rounded(key_wide.T)
    tokens = query.shape[1]
    total = jnp.zeros((1, tokens), jnp.float32)
    output = jnp.zeros((head_rows, tokens), jnp.float32)
    for start in range(0, tokens, key_chunk):
        scores = dot_across(key_rows[start : start + key_chunk], query)
        weights = jnp.exp2(scores * log2_scale)
        total = total + jnp.sum(weights, axis=0, keepdims=True)
        output = output + dot_across(value[:, start : start + key_chunk], rounded(weights))
    inverse = 1.0 / total
    total_ref[0] = inverse
    out_ref[0] = rounded((output * inverse)[:HD])


def attend_heads(raw, gains, cosine, sine_part):
    tokens = raw.shape[-1]
    heads = raw.shape[1]
    whole = lambda head: (0, 0)
    return pl.pallas_call(
        attend_body,
        grid=(heads,),
        out_shape=[
            jax.ShapeDtypeStruct((heads, HD, tokens), jnp.bfloat16),
            jax.ShapeDtypeStruct(raw.shape, jnp.bfloat16),
            jax.ShapeDtypeStruct((heads, 1, tokens), jnp.float32),
        ],
        in_specs=[
            pl.BlockSpec((3, 1, head_rows, tokens), lambda head: (0, head, 0, 0)),
            pl.BlockSpec((2, head_rows, 1), lambda head: (0, 0, 0)),
            pl.BlockSpec((half_rows, tokens), whole),
            pl.BlockSpec((half_rows, tokens), whole),
        ],
        out_specs=[
            pl.BlockSpec((1, HD, tokens), lambda head: (head, 0, 0)),
            pl.BlockSpec((3, 1, head_rows, tokens), lambda head: (0, head, 0, 0)),
            pl.BlockSpec((1, 1, tokens), lambda head: (head, 0, 0)),
        ],
        compiler_params=pltpu.CompilerParams(vmem_limit_bytes=vmem_bytes),
        cost_estimate=pl.CostEstimate(
            flops=4 * heads * tokens * tokens * 256,
            bytes_accessed=heads * tokens * 2000,
            transcendentals=heads * tokens * tokens,
        ),
    )(raw, gains, cosine, sine_part)


def attend_back_body(
    raw_ref, low_ref, total_ref, grad_ref, gain_ref, cos_ref, sin_ref, back_ref, gains_ref
):
    cosine, sine_part = cos_ref[...], sin_ref[...]
    query, key, value = low_ref[0, 0], low_ref[1, 0], low_ref[2, 0]
    tokens = query.shape[1]
    inverse_total = total_ref[0]
    grad_wide = wide(grad_ref[0])
    grad_wide = jnp.concatenate(
        [grad_wide, jnp.zeros((head_rows - HD, tokens), jnp.float32)], axis=0
    )
    grad = rounded(grad_wide)
    query_rows = rounded(wide(query).T)
    key_rows = rounded(wide(key).T)
    value_rows = rounded(wide(value).T)
    grad_rows = rounded(grad_wide.T)
    query_back = jnp.zeros((head_rows, tokens), jnp.float32)
    key_back, value_back = [], []
    delta = jnp.zeros((1, tokens), jnp.float32)
    chunks = [slice(start, start + key_chunk) for start in range(0, tokens, key_chunk)]
    held = []
    for chunk in chunks:
        scores = dot_across(key_rows[chunk], query)
        probs = jnp.exp2(scores * log2_scale) * inverse_total
        grad_probs = dot_across(value_rows[chunk], grad)
        delta = delta + jnp.sum(probs * grad_probs, axis=0, keepdims=True)
        held.append((probs, grad_probs))
    for chunk, (probs, grad_probs) in zip(chunks, held):
        grad_scores = rounded(probs * (grad_probs - delta))
        query_back = query_back + dot_across(key[:, chunk], grad_scores)
        key_back.append(dot_across(grad_scores, query_rows))
        value_back.append(dot_across(rounded(probs), grad_rows))
    root = HD ** (-0.5)
    key_back = jnp.concatenate(key_back, axis=0).T * root
    value_back = jnp.concatenate(value_back, axis=0).T
    for index, turned in enumerate((query_back * root, key_back)):
        gain = gain_ref[index]
        _, normed, inverse, used = turn_head(raw_ref[index, 0], gain, cosine, sine_part)
        straight, gain_grad = turn_head_back(
            turned, normed, inverse, used, gain, cosine, sine_part
        )
        back_ref[index, 0] = rounded(straight)
        gains_ref[0, index] = gain_grad
    back_ref[2, 0] = rounded(value_back)


def attend_heads_back(raw, low, inverse_total, grad, gains, cosine, sine_part):
    heads, tokens = raw.shape[1], raw.shape[-1]
    three = pl.BlockSpec((3, 1, head_rows, tokens), lambda head: (0, head, 0, 0))
    one = lambda rows: pl.BlockSpec((1, rows, tokens), lambda head: (head, 0, 0))
    whole = pl.BlockSpec((half_rows, tokens), lambda head: (0, 0))
    return pl.pallas_call(
        attend_back_body,
        grid=(heads,),
        out_shape=[
            jax.ShapeDtypeStruct(raw.shape, jnp.bfloat16),
            jax.ShapeDtypeStruct((heads, 2, head_rows, 1), jnp.float32),
        ],
        in_specs=[
            three,
            three,
            one(1),
            one(HD),
            pl.BlockSpec((2, head_rows, 1), lambda head: (0, 0, 0)),
            whole,
            whole,
        ],
        out_specs=[three, pl.BlockSpec((1, 2, head_rows, 1), lambda head: (head, 0, 0, 0))],
        compiler_params=pltpu.CompilerParams(vmem_limit_bytes=vmem_bytes),
        cost_estimate=pl.CostEstimate(
            flops=10 * heads * tokens * tokens * 256,
            bytes_accessed=heads * tokens * 3000,
            transcendentals=heads * tokens * tokens,
        ),
    )(raw, low, inverse_total, grad, gains, cosine, sine_part)


def norm_body(scale_at, shift_at, *refs):
    blocks, (columns_ref, keep_ref, away_ref, mid_ref, inv_ref) = refs[:4], refs[4:]
    base = wide(blocks[0][0:1])
    total = jnp.zeros(base.shape, jnp.float32)
    square = jnp.zeros(base.shape, jnp.float32)
    for block in blocks:
        shifted = wide(block[...]) - base
        total = total + jnp.sum(shifted, axis=0, keepdims=True)
        square = square + jnp.sum(shifted * shifted, axis=0, keepdims=True)
    total = total * (1.0 / D)
    inverse = lax.rsqrt(square * (1.0 / D) - total * total + norm_eps)
    middle = base + total
    mid_ref[...] = middle
    inv_ref[...] = inverse
    for index, block in enumerate(blocks):
        target = (keep_ref, away_ref)[index // 2]
        inner = (index % 2) * own_cols
        rows = slice(index * own_cols, (index + 1) * own_cols)
        scale = columns_ref[rows, scale_at : scale_at + 1]
        shift = columns_ref[rows, shift_at : shift_at + 1]
        normed = (wide(block[...]) - middle) * inverse
        target[inner : inner + own_cols] = rounded(normed * scale + shift)


def norm_columns(blocks, columns, scale_at, shift_at):
    tokens = blocks[0].shape[1]
    tile = 256
    part = pl.BlockSpec((own_cols, tile), lambda step: (0, step))
    half = pl.BlockSpec((2 * own_cols, tile), lambda step: (0, step))
    row = pl.BlockSpec((1, tile), lambda step: (0, step))
    keep, away, middle, inverse = pl.pallas_call(
        functools.partial(norm_body, scale_at, shift_at),
        grid=(tokens // tile,),
        out_shape=[
            jax.ShapeDtypeStruct((2 * own_cols, tokens), jnp.bfloat16),
            jax.ShapeDtypeStruct((2 * own_cols, tokens), jnp.bfloat16),
            jax.ShapeDtypeStruct((1, tokens), jnp.float32),
            jax.ShapeDtypeStruct((1, tokens), jnp.float32),
        ],
        in_specs=[part] * 4 + [pl.BlockSpec(columns.shape, lambda step: (0, 0))],
        out_specs=[half, half, row, row],
        compiler_params=pltpu.CompilerParams(vmem_limit_bytes=vmem_bytes),
        cost_estimate=pl.CostEstimate(
            flops=10 * D * tokens, bytes_accessed=4 * D * tokens, transcendentals=0
        ),
    )(*blocks, columns)
    return (keep, away), middle, inverse


def joined_body(places_ref, *refs):
    blocks, (gain_ref, bias_ref, cat_ref, norm_ref) = refs[:4], refs[4:]
    for index, block in enumerate(blocks):
        tensor = wide(block[...])
        center = tensor - jnp.mean(tensor, axis=1, keepdims=True)
        spread = jnp.mean(center * center, axis=1, keepdims=True)
        normed = center * lax.rsqrt(spread + norm_eps)
        norm_ref[places_ref[index]] = rounded(normed)
        cat_ref[places_ref[index]] = rounded(normed * gain_ref[...] + bias_ref[...])


def norm_joined(blocks, places, gain, bias):
    rows, cols = blocks[0].shape
    tile = 64
    shape = jax.ShapeDtypeStruct((4, rows, cols), jnp.bfloat16)
    part = pl.BlockSpec((tile, cols), lambda step: (step, 0))
    vector = pl.BlockSpec((1, cols), lambda step: (0, 0))
    every = pl.BlockSpec((4, tile, cols), lambda step: (0, step, 0))
    cat_low, norm_low = pl.pallas_call(
        joined_body,
        grid=(rows // tile,),
        out_shape=[shape, shape],
        in_specs=[pl.BlockSpec(memory_space=pltpu.SMEM)] + [part] * 4 + [vector] * 2,
        out_specs=[every, every],
        compiler_params=pltpu.CompilerParams(vmem_limit_bytes=vmem_bytes),
        cost_estimate=pl.CostEstimate(
            flops=40 * rows * cols, bytes_accessed=24 * rows * cols, transcendentals=0
        ),
    )(places, *blocks, gain[None], bias[None])
    return cat_low.reshape(4 * rows, cols), norm_low.reshape(4 * rows, cols)


def swap_core(tensor):
    return lax.ppermute(tensor, "seq", core_pairs)


def swap_chip(tensor):
    return lax.ppermute(tensor, "seq", chip_pairs)


def pick(tensor, index):
    return lax.dynamic_index_in_dim(
        tensor, index, 0, keepdims=False, allow_negative_indices=False
    )


def part_at(tensor, start, size, axis):
    return lax.dynamic_slice_in_dim(tensor, start, size, axis, allow_negative_indices=False)


def in_pairs(blocks):
    return jnp.concatenate(blocks[:2]), jnp.concatenate(blocks[2:])


def spread_rows(own):
    far = swap_chip(own)
    near = swap_core(own)
    return own, far, near, swap_core(far)


def fold_features(grad, weights, work=None):
    half = own_cols
    away = weigh_back(weights[1], grad)
    got = swap_core(rounded(away))
    keep = weigh_back(weights[0], grad)
    sent = rounded(keep[half:] + wide(got[half:]))
    far = swap_chip(sent)
    if work is not None:
        far = after(far, work(sent))
    total = keep[:half] + wide(got[:half]) + wide(far)
    return total, keep, away


def place(blocks, here):
    places = here ^ jnp.arange(shards, dtype=jnp.int32)
    rows, cols = blocks[0].shape
    moves = [(index, 0, index, 0, rows, 0, 0, cols) for index in range(shards)]
    return move_blocks(blocks, moves, places, [((shards, rows, cols), False)])[0]


def reorder(tensor, order, axis=0):
    return jnp.concatenate([part_at(tensor, index, 1, axis) for index in order], axis=axis)


def split_cols(tensor, parts):
    size = tensor.shape[1] // parts
    return jnp.stack([tensor[:, part * size : (part + 1) * size] for part in range(parts)])


def join_cols(blocks):
    return jnp.concatenate([blocks[part] for part in range(blocks.shape[0])], axis=1)


def gather_small(own, here):
    far = swap_chip(own)
    near = swap_core(own)
    blocks = jnp.stack([own, near, far, swap_core(far)])
    return reorder(blocks, [here ^ shard for shard in range(shards)])


def sum_small(own):
    pair = own + swap_core(own)
    return pair + swap_chip(pair)


def trade_starts(pieces, here):
    return (
        pick(pieces, here),
        swap_core(pick(pieces, here ^ 1)),
        swap_chip(pick(pieces, here ^ 2)),
        lax.ppermute(pick(pieces, here ^ 3), "seq", cross_pairs),
    )


def ring_tables(count):
    order = [0] + list(range(1, count, 2)) + list(range(count - 2, 0, -2))
    spot = [order.index(index) for index in range(count)]
    up = tuple((order[step], order[(step + 1) % count]) for step in range(count))
    down = tuple((after, before) for before, after in up)
    return order, spot, up, down


def move_blocks(sources, moves, places, targets):
    def body(places_ref, *refs):
        outs, first = [], len(sources)
        for _, paired in targets:
            outs.append(refs[first : first + (2 if paired else 1)])
            first += len(outs[-1])
        for source, row, entry, inner, size, target, lane, width in moves:
            block = refs[source][pl.ds(row, size), pl.ds(0, width)]
            where = (pl.ds(inner, size), pl.ds(lane, width))
            spot = places_ref[entry]
            if len(outs[target]) == 1:
                outs[target][0][(spot,) + where] = block
                continue
            half = targets[target][0][0]

            @pl.when(spot < half)
            def store_first():
                outs[target][0][(spot,) + where] = block

            @pl.when(spot >= half)
            def store_second():
                outs[target][1][(spot - half,) + where] = block

    shapes = [
        jax.ShapeDtypeStruct(shape, sources[0].dtype)
        for shape, paired in targets
        for _ in range(2 if paired else 1)
    ]
    size = sum(math.prod(shape.shape) for shape in shapes)
    return pl.pallas_call(
        body,
        out_shape=shapes,
        in_specs=[pl.BlockSpec(memory_space=pltpu.SMEM)]
        + [pl.BlockSpec(memory_space=pltpu.VMEM)] * len(sources),
        out_specs=[pl.BlockSpec(memory_space=pltpu.VMEM)] * len(shapes),
        compiler_params=pltpu.CompilerParams(vmem_limit_bytes=vmem_bytes),
        cost_estimate=pl.CostEstimate(flops=0, bytes_accessed=4 * size, transcendentals=0),
    )(places, *sources)


def pick_blocks(source, table, paired_rows, plain_rows):
    count, _, cols = source.shape
    half = count // 2
    shapes = []
    for rows in paired_rows:
        shapes += [(half, rows, cols)] * 2
    shapes += [(count, rows, cols) for rows in plain_rows]

    def body(table_ref, source_ref, *targets):
        row = 0
        for part, rows in enumerate(paired_rows):
            for entry in range(count):
                target = targets[2 * part + entry // half]
                target[entry % half] = source_ref[table_ref[entry], pl.ds(row, rows)]
            row += rows
        for part, rows in enumerate(plain_rows):
            targets[2 * len(paired_rows) + part][...] = source_ref[:, pl.ds(row, rows)]
            row += rows

    picked = pl.pallas_call(
        body,
        out_shape=[jax.ShapeDtypeStruct(shape, source.dtype) for shape in shapes],
        in_specs=[
            pl.BlockSpec(memory_space=pltpu.SMEM),
            pl.BlockSpec(memory_space=pltpu.VMEM),
        ],
        out_specs=[pl.BlockSpec(memory_space=pltpu.VMEM)] * len(shapes),
        compiler_params=pltpu.CompilerParams(vmem_limit_bytes=vmem_bytes),
        cost_estimate=pl.CostEstimate(
            flops=0, bytes_accessed=4 * math.prod(source.shape), transcendentals=0
        ),
    )(table, source)
    picked = [piece.reshape(-1, cols) for piece in picked]
    first = 2 * len(paired_rows)
    return list(zip(picked[:first:2], picked[1:first:2])) + picked[first:]


def arrange_blocks(grads, tables, entries, cut):
    rows = [grad[0].shape[1] for grad in grads]
    cols = max(grad[0].shape[2] for grad in grads)
    flat = [array for grad in grads for array in grad]

    def body(*refs):
        tables_refs, array_refs, targets = refs[: len(grads)], refs[len(grads) : -3], refs[-3:]
        base, first = 0, 0

        def put(entry, base, lane, block):
            size, lanes = block.shape[0], pl.ds(lane, block.shape[1])
            if entry > 0:
                targets[2][entry - 1, pl.ds(base, size), lanes] = block
                return
            above = max(0, min(size, cut - base))
            if above > 0:
                targets[0][pl.ds(base, above), lanes] = block[:above]
            if above < size:
                start = base + above - cut
                targets[1][pl.ds(start, size - above), lanes] = block[above:]

        for grad, table_ref, size in zip(grads, tables_refs, rows):
            width = grad[0].shape[2]
            for entry in range(entries):
                spot = table_ref[entry]
                begin = 0
                for index, array in enumerate(grad):
                    end = begin + array.shape[0]

                    @pl.when((spot >= begin) & (spot < end))
                    def store(index=index, begin=begin):
                        put(entry, base, 0, array_refs[first + index][spot - begin])

                    begin = end
                if width < cols:
                    put(entry, base, width, jnp.zeros((size, cols - width), targets[0].dtype))
            base, first = base + size, first + len(grad)

    shape = (entries, sum(rows), cols)
    shapes = [(cut, cols), (sum(rows) - cut, cols), (entries - 1, sum(rows), cols)]
    return pl.pallas_call(
        body,
        out_shape=[jax.ShapeDtypeStruct(part, flat[0].dtype) for part in shapes],
        in_specs=[pl.BlockSpec(memory_space=pltpu.SMEM)] * len(grads)
        + [pl.BlockSpec(memory_space=pltpu.VMEM)] * len(flat),
        out_specs=[pl.BlockSpec(memory_space=pltpu.VMEM)] * 3,
        compiler_params=pltpu.CompilerParams(vmem_limit_bytes=vmem_bytes),
        cost_estimate=pl.CostEstimate(
            flops=0, bytes_accessed=4 * math.prod(shape), transcendentals=0
        ),
    )(*tables, *flat)


class Images:

    def __init__(self):
        self.count = lax.axis_size("img")
        self.here = lax.axis_index("img")
        self.bits = [1 << bit for bit in range((self.count - 1).bit_length())]
        self.direct = self.count != 8
        order, spot, self.up, self.down = ring_tables(self.count)
        self.order = order
        self.spot = spot


    def swap(self, tensor, bit):
        return lax.ppermute(
            tensor, "img", tuple((index, index ^ bit) for index in range(self.count))
        )

    def gather_small(self, own):
        held = own[None]
        for bit in self.bits:
            held = jnp.concatenate([held, self.swap(held, bit)])
        return held

    def scatter_small(self, terms):
        held = terms
        for bit in reversed(self.bits):
            held = held[:bit] + self.swap(held[bit:], bit)
        return held[0]

    def trade_small(self, rows):
        held = rows
        for bit in self.bits:
            split = held.reshape((-1, 2, bit) + rows.shape[1:])
            split = jnp.stack([split[:, 0], self.swap(split[:, 1], bit)], axis=1)
            held = split.reshape(rows.shape)
        return held

    def sum_small(self, own):
        for bit in self.bits:
            own = own + self.swap(own, bit)
        return own


    def table(self, entry_of, size):
        table = np.zeros((shards, self.count, size), np.int32)
        for shard in range(shards):
            for image in range(self.count):
                for entry in range(size):
                    table[shard, image, entry] = entry_of(shard, image, entry)
        table = jnp.asarray(table.reshape(shards * self.count, size))
        return pick(table, lax.axis_index("seq") * self.count + self.here)

    def places(self, slots, offsets):
        def entry_of(shard, image, entry):
            return slots(shard, self.order[(self.spot[image] + offsets[entry]) % self.count])

        return self.table(entry_of, len(offsets))


class GatherRing:
    def __init__(self, images, shard):
        self.images = images
        self.shard = shard
        self.blocks, self.offsets, self.starts = [shard], [0], [0]
        self.upward = self.downward = shard
        self.step = 0
        self.reach = images.count // 2
        self.cut = (shard.shape[0] // 2 + 15) // 16 * 16

    def advance(self, tie=()):
        images = self.images
        if images.direct:
            return self.shard
        self.step += 1
        upward, downward = after((self.upward, self.downward), tie)
        if self.step < self.reach:
            self.upward = lax.ppermute(upward, "img", images.up)
            self.downward = lax.ppermute(downward, "img", images.down)
            self.offsets += [-self.step, self.step]
            self.starts += [0, 0]
        else:
            self.upward = lax.ppermute(upward[: self.cut], "img", images.up)
            self.downward = lax.ppermute(downward[self.cut :], "img", images.down)
            self.offsets += [-self.reach, -self.reach]
            self.starts += [0, self.cut]
        self.blocks += [self.upward, self.downward]
        return upward, downward

    def result(self, segments, targets):
        images = self.images
        count = images.count
        if images.direct:
            whole = lax.all_gather(self.shard, "img", axis=0)
            wholes = [[] for _ in targets]
            row = 0
            for rows, slots, target, _, width in segments:
                back = images.table(
                    lambda shard, image, entry: next(
                        other for other in range(count) if slots(shard, other) == entry
                    ),
                    count,
                )
                piece = jnp.take(whole[:, row : row + rows, :width], back, axis=0)
                wholes[target].append(piece.reshape(count * rows, width))
                row += rows
            wholes = [jnp.concatenate(pieces, axis=-1) for pieces in wholes]
            return [
                tuple(jnp.split(whole, 2)) if paired else whole
                for whole, (_, paired) in zip(wholes, targets)
            ]
        all_slots = []
        for _, slots, _, _, _ in segments:
            if slots not in all_slots:
                all_slots.append(slots)
        places = jnp.concatenate([images.places(slots, self.offsets) for slots in all_slots])
        moves = []
        for index, (block, start) in enumerate(zip(self.blocks, self.starts)):
            base = 0
            for rows, slots, target, lane, width in segments:
                low, high = max(base, start), min(base + rows, start + block.shape[0])
                if low < high:
                    entry = all_slots.index(slots) * len(self.offsets) + index
                    moves.append(
                        (index, low - start, entry, low - base, high - low, target, lane, width)
                    )
                base += rows
        placed = iter(move_blocks(self.blocks, moves, places, targets))
        results = []
        for _, paired in targets:
            pieces = tuple(next(placed) for _ in range(2 if paired else 1))
            pieces = tuple(piece.reshape(-1, piece.shape[-1]) for piece in pieces)
            results.append(pieces if paired else pieces[0])
        return results


class ScatterRing:
    def __init__(self, images, grads, slots):
        self.images = images
        count = images.count
        grads = [
            tuple(
                part.reshape(-1, sum(each.shape[0] for each in grad) // count, part.shape[1])
                for part in grad
            )
            for grad in grads
        ]
        self.grads, self.slots = grads, slots
        self.reach = count // 2
        self.step = 0
        if images.direct:
            return
        offsets = [self.reach]
        for step in range(2, self.reach + 1):
            offsets += [self.reach - step + 1, step - self.reach - 1]
        offsets.append(0)
        tables = [images.places(slots_of, offsets) for slots_of in slots]
        rows = sum(grad[0].shape[1] for grad in grads)
        self.cut = (rows // 2 + 15) // 16 * 16
        *self.first, self.blocks = arrange_blocks(grads, tables, len(offsets), self.cut)

    def advance(self, tie=()):
        images = self.images
        if images.direct:
            return self.grads
        self.step += 1
        cut, blocks = self.cut, self.blocks
        if self.step == 1:
            ahead, behind = after(tuple(self.first), tie)
        else:
            ahead = wide(blocks[2 * self.step - 4])
            behind = wide(blocks[2 * self.step - 3])
            upward, downward = after((self.upward, self.downward), tie)
            if self.step == 2:
                ahead = jnp.concatenate([ahead[:cut] + wide(upward), ahead[cut:]])
                behind = jnp.concatenate([behind[:cut], behind[cut:] + wide(downward)])
            else:
                ahead = ahead + wide(upward)
                behind = behind + wide(downward)
            ahead, behind = rounded(ahead), rounded(behind)
        self.upward = lax.ppermute(ahead, "img", images.up)
        self.downward = lax.ppermute(behind, "img", images.down)
        return ahead, behind

    def result(self, tie=()):
        images = self.images
        if images.direct:
            count = images.count
            every = []
            cols = max(grad[0].shape[2] for grad in self.grads)
            for grad, slots in zip(self.grads, self.slots):
                order = images.table(lambda shard, image, entry: slots(shard, entry), count)
                block = jnp.take(jnp.concatenate(grad), order, axis=0)
                every.append(jnp.pad(block, ((0, 0), (0, 0), (0, cols - block.shape[2]))))
            every = wide(jnp.concatenate(every, axis=1))
            return lax.psum_scatter(every, "img", scatter_dimension=0, tiled=False)
        upward, downward = after((self.upward, self.downward), tie)
        return wide(self.blocks[-1]) + wide(upward) + wide(downward)


def after(tensor, mark):
    return lax.optimization_barrier((tensor, mark))[0]


class Order:
    def __init__(self):
        self.last = ()

    def __call__(self, *tensors):
        held = after(tensors, self.last)
        return held if len(tensors) > 1 else held[0]

    def mark(self, *tensors):
        self.last = tensors

    def step(self, ring):
        self.mark(ring.advance(self.last))


class Chain:
    def __init__(self, steps):
        self.steps = steps
        self.value = None
        self.running = True
        self.tick()

    def tick(self):
        if not self.running:
            return
        try:
            next(self.steps)
        except StopIteration as stop:
            self.value = stop.value
            self.running = False

    def finish(self):
        while self.running:
            self.tick()
        return self.value


def per_device(
    hidden_in,
    skip_in,
    text,
    condition,
    positions,
    out_grad,
    skip_gain,
    skip_bias,
    w_skip,
    w_mod,
    q_gain,
    k_gain,
    w_qkv,
    w_attn_out,
    cross_gain,
    cross_bias,
    w_cross_q,
    w_cross_kv,
    w_cross_out,
    w_fc1,
    w_fc2,
):
    here = lax.axis_index("seq")
    images = Images()
    count = images.count
    per_shard = count // shards
    rows_here = D // count
    text_rows = w_cross_kv.shape[0]
    hidden_units = w_fc2.shape[0] // shards
    tokens_here = hidden_in.shape[1]
    tokens = shards * tokens_here
    relative = [here, here ^ 2, here ^ 1, here ^ 3]

    def straight(shard, index):
        return index

    def turned(shard, index):
        return (0, 2, 1, 3)[(index // per_shard) ^ shard] * per_shard + index % per_shard

    order = Order()
    odd = here % 2
    places = here ^ jnp.arange(shards, dtype=jnp.int32)
    turn_map, plain_map = column_map(turned_rows()), column_map(np.arange(HD))
    column_maps = jnp.stack([turn_map, turn_map, plain_map])

    def send(own):
        order.mark(own)
        return swap_chip(own), swap_core(own)

    def receive(own, far, near):
        far = order(far)
        order.mark(far)
        return order(own, far, near, swap_core(far))

    skip_ring = GatherRing(images, rounded(w_skip))
    order.step(skip_ring)
    joined_here = order(jnp.concatenate([hidden_in[0], skip_in[0]], axis=-1))
    joined_far, joined_near = send(joined_here)
    cond_vec = wide(condition[0])
    cond_low = rounded(jax.nn.silu(cond_vec))
    mod_low = rounded(w_mod)

    def modulation():
        held = order(cond_low)[None]
        order.mark(held)
        for bit in images.bits:
            other = images.swap(held, bit)
            yield
            held = jnp.concatenate([held, order(other)])
            order.mark(held)
        rows = part_at(held, images.here * rows_here, rows_here, 1)
        held = jnp.dot(rows, mod_low, preferred_element_type=jnp.float32)
        order.mark(held)
        for bit in reversed(images.bits):
            other = images.swap(held[bit:], bit)
            yield
            held = held[:bit] + order(other)
            order.mark(held)
        own = held[0]
        far, near = swap_chip(own), swap_core(own)
        yield
        far = order(far)
        order.mark(far)
        diagonal = swap_core(far)
        yield
        blocks = jnp.stack(order(own, near, far, diagonal))
        vectors = reorder(blocks, [here ^ shard for shard in range(shards)]).reshape(6, D)
        order.mark(vectors)
        return rows, vectors

    mod_chain = Chain(modulation())
    qkv_here = rounded(order(w_qkv))
    qkv_parts = split_cols(qkv_here, 3)
    kept = jnp.where(odd == 1, qkv_parts[2], qkv_parts[0])
    sent = jnp.where(odd == 1, qkv_parts[0], qkv_parts[2])
    order.mark(kept, sent)
    qkv_mix = [kept, swap_core(qkv_parts[1]), swap_chip(sent)]
    grid_here = order(positions[0].T)
    grid_far, grid_near = send(grid_here)
    order.step(skip_ring)
    mod_chain.tick()
    mod_chain.tick()
    order.step(skip_ring)
    qkv_mix = jnp.stack(order(*qkv_mix))
    qkv_order = pick(np.array([[0, 1, 2], [1, 0, 2], [2, 0, 1], [2, 1, 0]], np.int32), here)
    qkv_home = pick(np.array([[0, 1, 2], [1, 0, 2], [1, 2, 0], [2, 1, 0]], np.int32), here)
    qkv_own = jnp.concatenate(
        [select(pick(qkv_mix, qkv_order[part]), column_maps[part]) for part in range(3)]
    )
    qkv_ring = GatherRing(images, qkv_own)
    order.mark(qkv_own)
    order.step(qkv_ring)
    mod_chain.tick()
    unit = np.arange(w_fc1.shape[1])
    image_of, inner = unit // (w_fc1.shape[1] // per_shard), unit % (w_fc1.shape[1] // per_shard)
    slot_of = (inner // hidden_units) * per_shard * hidden_units
    slot_of = slot_of + image_of * hidden_units + inner % hidden_units
    unit_map = np.zeros((w_fc1.shape[1], w_fc1.shape[1]), np.float32)
    unit_map[unit, slot_of] = 1.0
    unit_map = jnp.asarray(unit_map, jnp.bfloat16)
    later = order(w_fc1, w_fc2)
    fc1_pieces = split_cols(select(rounded(later[0]), unit_map), shards)
    fc2_pieces = rounded(later[1]).reshape(shards, hidden_units, own_cols)
    order.mark(fc1_pieces, fc2_pieces)
    grid = receive(grid_here, grid_far, grid_near)
    grid = jnp.stack([grid[0], grid[2], grid[1], grid[3]])
    grid = reorder(grid, [here ^ shard for shard in range(shards)])
    order.mark(grid)
    order.step(skip_ring)
    mod_chain.tick()
    mod_chain.tick()
    (skip_all,) = skip_ring.result(
        [(2 * rows_here, straight, 0, 0, own_cols)], [((count, 2 * rows_here, own_cols), False)]
    )
    skip_all = order(skip_all)
    order.mark(skip_all)
    order.step(qkv_ring)
    mod_chain.tick()
    later = order(w_attn_out, w_cross_q, w_cross_out, w_cross_kv)
    crosskv = rounded(later[3])
    small = [rounded(weight) for weight in later[:3]] + [crosskv[:, 0], crosskv[:, 1]]
    small = jnp.concatenate(small)
    order.mark(small)
    small_ring = GatherRing(images, small)
    joined = receive(joined_here, joined_far, joined_near)
    joined = (joined[0], joined[2], joined[1], joined[3])
    cotangent_far = swap_chip(order(out_grad[0]))
    fc1_trade, fc2_trade = trade_starts(order(fc1_pieces), here), trade_starts(fc2_pieces, here)
    cond_rows, modul = mod_chain.finish()
    cat_low, joined_norm = norm_joined(order(*joined), places, skip_gain, skip_bias)
    order.mark(cat_low)
    order.step(qkv_ring)
    order.step(small_ring)
    one_own = jnp.einsum("kn,tk->nt", skip_all, order(cat_low), preferred_element_type=jnp.float32)
    one_low = rounded(one_own)

    far, near = send(one_low)
    vectors = jnp.concatenate([order(modul), cross_gain[None], cross_bias[None]])
    one_plus = np.zeros((8, 1), np.float32)
    one_plus[[1, 4]] = 1.0
    columns = (vectors + one_plus).T
    columns = jnp.concatenate(
        [part_at(columns, index * own_cols, own_cols, 0) for index in relative]
    )
    shift_one, scale_one = columns[:, 0:1], columns[:, 1:2]
    shift_two, scale_two = columns[:, 3:4], columns[:, 4:5]
    cross_scale, cross_shift = columns[:, 6:7], columns[:, 7:8]
    gate_one = columns[:own_cols, 2:3]
    gate_two = modul[5]
    order.mark(columns)
    grid_pos = jnp.swapaxes(order(grid), 0, 1).reshape(2, tokens)
    frequency = 10000.0 ** (-jnp.arange(quarter, dtype=jnp.float32) / quarter)
    angles = grid_pos.astype(jnp.float32)[:, None, :] * frequency[:, None]
    angles = jnp.pad(angles.reshape(2 * quarter, tokens), ((0, half_rows - 2 * quarter), (0, 0)))
    cosine, sine_part = jnp.cos(angles), jnp.sin(angles)
    entry_rows = turned_rows()
    head_map = np.zeros((head_rows, HD), np.float32)
    head_map[entry_rows, np.arange(HD)] = 1.0
    gains_low = jnp.dot(
        jnp.stack([q_gain, k_gain]), head_map.T, precision=lax.Precision.HIGHEST
    )[:, :, None]
    order.mark(cosine, sine_part, gains_low)
    order.step(qkv_ring)
    order.step(small_ring)
    fc1_own = join_cols(place(order(*fc1_trade), here))
    fc2_own = join_cols(place(order(*fc2_trade), here))
    order.mark(fc1_own, fc2_own)
    (qkv_all,) = qkv_ring.result(
        [(rows_here, turned, 0, part * padded_cols, padded_cols) for part in range(3)],
        [((count // 2, rows_here, 3 * padded_cols), True)],
    )
    qkv_all = order(*qkv_all)
    order.mark(qkv_all)
    one_blocks = receive(one_low, far, near)
    attn_in, one_mid, one_inv = norm_columns(one_blocks, columns, 1, 0)
    order.mark(attn_in)
    order.step(small_ring)
    qkv_raw = weigh(qkv_all, order(*attn_in)).reshape(3, own_heads, head_rows, tokens)
    order.mark(qkv_raw)
    attn_raw, qkv_low, attn_total = attend_heads(order(qkv_raw), gains_low, cosine, sine_part)
    attn_own = attn_raw.reshape(own_cols, tokens)

    far, near = send(attn_own)
    order.step(small_ring)
    fc1_own, fc2_own = order(fc1_own, fc2_own)
    fc1_rows = lax.all_gather(fc1_own, "img", axis=0, tiled=True)
    fc2_all = lax.all_gather(fc2_own, "img", axis=0, tiled=True)
    cotangent_far = order(cotangent_far)
    cotangent = (out_grad[0], swap_core(order(out_grad[0])), cotangent_far, swap_core(cotangent_far))
    attn_out_all, cross_q_all, cross_out_all, *crosskv_all = small_ring.result(
        [(rows_here, turned, part, 0, own_cols) for part in range(3)]
        + [(text_rows, straight, part, 0, own_cols) for part in (3, 4)],
        [((count // 2, rows_here, own_cols), True)] * 3
        + [((count, text_rows, own_cols), False)] * 2,
    )
    crosskv_all = order(*crosskv_all)
    order.mark(crosskv_all)
    attn_low = in_pairs(receive(attn_own, far, near))
    branch_own = weigh(attn_out_all, attn_low)
    two_own = one_own + gate_one * branch_own
    two_low = rounded(two_own)

    far, near = send(two_low)
    text_keys, text_values = [
        by_heads(
            rounded(
                jnp.einsum("kn,tk->nt", weight, text[0], preferred_element_type=jnp.float32)
            )
        )
        for weight in order(*crosskv_all)
    ]
    order.mark(text_keys, text_values)
    cotangent = place(order(*cotangent), here).reshape(tokens, D)
    order.mark(cotangent)
    cot_wide = wide(order(cotangent))
    grad_mlp = rounded(cot_wide * gate_two)
    order.mark(grad_mlp)
    two_blocks = receive(two_low, far, near)
    cross_in, two_mid, two_inv = norm_columns(two_blocks, columns, 6, 7)
    cross_query = by_heads(rounded(weigh(cross_q_all, cross_in)))
    cross_raw, cross_lse = attend(cross_query, text_keys, text_values)
    cross_own = rounded(cross_raw.reshape(own_cols, tokens))
    far, near = send(cross_own)
    cross_low = in_pairs(receive(cross_own, far, near))
    three_own = two_own + weigh(cross_out_all, cross_low)
    three_sent = rounded(three_own)

    far, near = send(three_sent)
    fc1_rows = order(fc1_rows).reshape(shards, own_cols, -1)
    fc1_all = in_pairs([pick(fc1_rows, index) for index in relative])
    order.mark(fc1_all)
    three_low = receive(three_sent, far, near)
    mlp_in, three_mid, three_inv = norm_columns(three_low, columns, 4, 3)
    upper = weigh(fc1_all, mlp_in)
    bend = jnp.tanh(gelu_root * (upper + gelu_cube * upper * upper * upper))
    act_low = rounded(0.5 * upper * (1.0 + bend))
    slope = 0.5 * (1.0 + bend) + 0.5 * upper * (1.0 - bend * bend) * gelu_root * (
        1.0 + 3.0 * gelu_cube * upper * upper
    )
    act_low, slope = lax.optimization_barrier((act_low, slope))

    grad_act = jnp.einsum("uc,tc->ut", fc2_all, grad_mlp, preferred_element_type=jnp.float32)
    grad_upper = rounded(grad_act * slope)
    canonical = jnp.arange(D, dtype=jnp.int32)
    own_map = canonical[:, None] == here * own_cols + canonical[None, :own_cols]
    cot_own = jnp.einsum(
        "tc,cn->nt", cotangent, rounded(own_map), preferred_element_type=jnp.float32
    )
    held = {}

    def norm_back(grad, weights, gain_rel, normed, shift, norm_inv, own, work):
        total, keep, away = fold_features(grad, weights, work)
        half = D // 2
        kept = keep * gain_rel[:half]
        gone = away * gain_rel[half:]
        sums = jnp.stack(
            [
                jnp.sum(kept, axis=0) + jnp.sum(gone, axis=0),
                jnp.sum(keep * (wide(normed[0]) - shift[:half]), axis=0)
                + jnp.sum(away * (wide(normed[1]) - shift[half:]), axis=0),
            ]
        )
        means = sum_small(sums) * (1.0 / D)
        scaled = total * gain_rel[:own_cols]
        grad_in = norm_inv * (scaled - means[:1] - own * means[1:])
        return grad_in, jnp.sum(total * own, axis=1), jnp.sum(total, axis=1)

    def work_three(sent):
        fc2_grad = contract(after(act_low, sent), grad_mlp.T)
        fc1_grad = contract_pair(mlp_in, after(grad_upper, sent))
        held["fc1_pair"] = fc1_grad
        held["fc2"] = lax.psum_scatter(fc2_grad, "img", scatter_dimension=0, tiled=True)
        return fc2_grad, held["fc1_pair"]

    three_own_norm = (three_own - three_mid) * three_inv
    back_three, d_scale_two, d_shift_two = norm_back(
        grad_upper, fc1_all, scale_two, mlp_in, shift_two, three_inv, three_own_norm, work_three
    )
    grad_three = cot_own + back_three

    grad_cross = rounded(grad_three)

    def work_cross(sent):
        act_held = after(act_low, sent)
        mlp_part = jnp.einsum("ut,uc->tc", act_held, fc2_all, preferred_element_type=jnp.float32)
        held["mlp"] = mlp_part.reshape(shards, tokens_here, D)
        held["d_gate_two"] = jnp.sum(cot_wide * mlp_part, axis=0)
        held["cross_out"] = contract_pair(cross_low, after(grad_cross, sent))
        fc1_grad = move_blocks(
            after(held["fc1_pair"], sent),
            [
                (index // 2, (index % 2) * own_cols, index, 0, own_cols, 0, 0, w_fc1.shape[1])
                for index in range(shards)
            ],
            jnp.stack(relative),
            [((shards, own_cols, w_fc1.shape[1]), False)],
        )[0].reshape(D, -1)
        held["fc1"] = lax.psum_scatter(
            after(fc1_grad, held["fc2"]), "img", scatter_dimension=0, tiled=True
        )
        return held["d_gate_two"], held["cross_out"], fc1_grad

    grad_cross_attn = fold_features(grad_cross, cross_out_all, work_cross)[0]
    grad_cross_attn = by_heads(rounded(grad_cross_attn))
    cross_back = attend_back(cross_query, text_keys, text_values, cross_lse, grad_cross_attn)
    grad_cquery = rounded(cross_back[0].reshape(own_cols, tokens))
    text_grad = rounded(jnp.concatenate([cross_back[1], cross_back[2]])).reshape(2 * own_cols, -1)
    two_own_norm = (two_own - two_mid) * two_inv

    def work_two(sent):
        grad_held = after(text_grad, sent)
        kv_grads = [
            (rounded(jnp.einsum("tk,nt->kn", text[0], grad, preferred_element_type=jnp.float32)),)
            for grad in (grad_held[:own_cols], grad_held[own_cols:])
        ]
        held["kv"] = kv_grads
        text_part = sum(
            jnp.einsum("nt,kn->tk", grad, weight, preferred_element_type=jnp.float32)
            for grad, weight in zip((grad_held[:own_cols], grad_held[own_cols:]), crosskv_all)
        )
        held["text"] = rounded(text_part)
        held["text_got"] = swap_core(held["text"])
        held["cross_q"] = contract_pair(cross_in, after(grad_cquery, sent))
        three_here = jnp.concatenate(
            [part_at(block, here * tokens_here, tokens_here, 1) for block in after(three_low, sent)]
        )
        place_of = jnp.concatenate([index * own_cols + canonical[:own_cols] for index in relative])
        feature_map = rounded(place_of[:, None] == canonical[None, :])
        held["three"] = jnp.einsum(
            "kt,kc->tc", three_here, feature_map, preferred_element_type=jnp.float32
        )
        away = [rounded(pick(held["mlp"], here ^ distance)) for distance in (1, 3)]
        held["mlp_away"] = jnp.stack(away)
        held["mlp_got"] = swap_core(held["mlp_away"])
        return kv_grads, held["text"], held["cross_q"], held["mlp_away"], held["three"]

    back_two, d_cross_gain, d_cross_bias = norm_back(
        grad_cquery, cross_q_all, cross_scale, cross_in, cross_shift, two_inv, two_own_norm, work_two
    )
    grad_two = grad_three + back_two

    d_gate_one = jnp.sum(grad_two * branch_own, axis=1)
    grad_branch = rounded(grad_two * gate_one)

    def work_attn(sent):
        mlp_here = pick(held["mlp"], here ^ 2)
        held["mlp_sent"] = rounded(mlp_here + wide(held["mlp_got"][1]))
        held["text_pair"] = held["text"] + held["text_got"]
        attn_grads = contract_pair(attn_low, after(grad_branch, sent))
        held["small"] = ScatterRing(
            images,
            [attn_grads, held["cross_q"], held["cross_out"]] + held["kv"],
            [turned] * 3 + [straight] * 2,
        )
        return held["mlp_sent"], held["text_pair"], held["small"].advance(sent), held["fc2"]

    grad_attn = fold_features(grad_branch, attn_out_all, work_attn)[0]
    grad_attn = by_heads(rounded(grad_attn))
    mlp_sent, text_pair = after((held["mlp_sent"], held["text_pair"]), grad_attn)
    mlp_far = swap_chip(mlp_sent)
    text_far = swap_chip(text_pair)
    grad_qkv, gain_terms = attend_heads_back(
        qkv_raw,
        qkv_low,
        attn_total,
        after(grad_attn, (mlp_sent, text_pair)),
        gains_low,
        cosine,
        sine_part,
    )
    grad_qkv = grad_qkv.reshape(3 * padded_cols, tokens)
    gain_terms = jnp.sum(gain_terms[..., 0], axis=0)
    gain_terms = jnp.dot(gain_terms, head_map, precision=lax.Precision.HIGHEST)
    one_own_norm = (one_own - one_mid) * one_inv

    held["small"].advance(grad_qkv)

    def work_one(sent):
        qkv_grads = contract_pair(attn_in, after(grad_qkv, sent))
        held["qkv"] = ScatterRing(images, [qkv_grads], [turned])
        return held["qkv"].advance()

    back_one, d_scale_one, d_shift_one = norm_back(
        grad_qkv, qkv_all, scale_one, attn_in, shift_one, one_inv, one_own_norm, work_one
    )
    grad_one = rounded(grad_two + back_one)

    norm_rows = joined_norm.reshape(shards, tokens_here, 2 * D)

    def cat_block(distance):
        rows = part_at(grad_one, (here ^ distance) * tokens_here, tokens_here, 1)
        return jnp.einsum("nt,kn->tk", rows, skip_all, preferred_element_type=jnp.float32)

    order.mark(grad_one)
    cat_away = order(jnp.concatenate([rounded(cat_block(1)), rounded(cat_block(3))]))
    order.mark(cat_away)
    cat_got = swap_core(cat_away)
    dmod_sent = order(
        jnp.concatenate(
            [d_shift_one, d_scale_one, d_gate_one, d_shift_two, d_scale_two, held["d_gate_two"]]
        )
    )
    cols_here = w_mod.shape[1]

    def modulation_back():
        far, near = send(dmod_sent)
        yield
        far = order(far)
        order.mark(far)
        diagonal = swap_core(far)
        yield
        blocks = jnp.stack(order(dmod_sent, near, far, diagonal))
        blocks = reorder(blocks, [here ^ shard for shard in range(shards)])
        five = blocks[:, : 5 * own_cols].reshape(shards, 5, own_cols)
        five = jnp.swapaxes(five, 0, 1).reshape(5 * D)
        full = jnp.concatenate([five, jnp.sum(blocks[:, 5 * own_cols :], axis=0)])
        cols = part_at(full, here * cols_here, cols_here, 0)[None]
        order.mark(cols)
        for bit in images.bits:
            other = images.swap(cols, bit)
            yield
            cols = jnp.concatenate([cols, order(other)])
            order.mark(cols)
        rows = jnp.einsum(
            "nc,rc->nr",
            cols,
            wide(mod_low),
            precision=lax.Precision.HIGHEST,
            preferred_element_type=jnp.float32,
        )
        order.mark(rows)
        for bit in images.bits:
            split = rows.reshape((-1, 2, bit) + rows.shape[1:])
            other = images.swap(split[:, 1], bit)
            yield
            rows = jnp.stack([split[:, 0], order(other)], axis=1).reshape(rows.shape)
            order.mark(rows)
        for swap in (swap_core, swap_chip):
            other = swap(rows)
            yield
            rows = rows + order(other)
            order.mark(rows)
        return cols, rows

    def sum_of_all(own):
        order.mark(own)
        for swap in (swap_core, swap_chip):
            other = swap(own)
            yield
            own = own + order(other)
            order.mark(own)
        for bit in images.bits:
            other = images.swap(own, bit)
            yield
            own = own + order(other)
            order.mark(own)
        return own

    cond_chain = Chain(modulation_back())
    fc1_sum, fc2_sum = order(held["fc1"], held["fc2"])
    fc1_pieces, fc2_pieces = split_cols(fc1_sum, shards), split_cols(fc2_sum, shards)
    order.mark(fc1_pieces, fc2_pieces)
    cat_two = order(cat_block(2))
    cat_sent = rounded(cat_two + wide(order(cat_got)[tokens_here:]))
    order.mark(cat_sent)
    cat_far = swap_chip(cat_sent)
    cond_chain.tick()
    skip_grad = jnp.einsum(
        "tk,nt->kn", cat_low, order(grad_one), preferred_element_type=jnp.float32
    )
    held["skip"] = ScatterRing(images, [(rounded(skip_grad),)], [straight])
    order.step(held["skip"])
    order.step(held["qkv"])
    cond_chain.tick()
    grad_held, away_held, two_held = order(grad_one, cat_away, cat_two)
    cat_zero = jnp.einsum(
        "nt,kn->tk",
        part_at(grad_held, here * tokens_here, tokens_here, 1),
        skip_all,
        preferred_element_type=jnp.float32,
    )
    cat_parts = (cat_zero, away_held[:tokens_here], two_held, away_held[tokens_here:])
    d_skip_bias = sum(jnp.sum(wide(part), axis=0) for part in cat_parts)
    d_skip_gain = sum(
        jnp.sum(wide(part) * wide(pick(norm_rows, here ^ distance)), axis=0)
        for distance, part in enumerate(cat_parts)
    )
    cross_gains = lax.dynamic_update_index_in_dim(
        jnp.zeros((shards, 2 * own_cols), jnp.float32),
        jnp.concatenate([d_cross_gain, d_cross_bias]),
        here,
        0,
        allow_negative_indices=False,
    )
    gains = jnp.concatenate(
        [d_skip_gain, d_skip_bias, gain_terms.reshape(-1), cross_gains.reshape(-1)]
    )
    gain_chain = Chain(sum_of_all(gains))
    cond_chain.tick()
    order.step(held["skip"])
    order.step(held["small"])
    gain_chain.tick()
    cond_chain.tick()
    fc1_trade = trade_starts(order(fc1_pieces), here)
    fc2_trade = trade_starts(order(fc2_pieces), here)
    order.step(held["qkv"])
    cond_chain.tick()
    order.step(held["skip"])
    gain_chain.tick()
    text_pair, text_far, mlp_far = order(text_pair, text_far, mlp_far)
    grad_text = wide(text_pair + text_far)[None]
    mlp_rows = pick(held["mlp"], here) + wide(held["mlp_got"][0]) + wide(mlp_far)
    block_out = rounded(held["three"] + gate_two * mlp_rows)[None]
    order.mark(grad_text, block_out)
    cond_chain.tick()
    order.step(held["small"])
    gain_chain.tick()
    order.step(held["qkv"])
    cond_chain.tick()
    order.step(held["skip"])
    fc2_back = place(order(*fc2_trade), here)
    fc1_back = join_cols(place(order(*fc1_trade), here))
    grad_fc2 = wide(fc2_back).reshape(-1, own_cols)
    grad_fc1 = jnp.dot(fc1_back, unit_map.T, preferred_element_type=jnp.float32)
    order.mark(grad_fc1, grad_fc2)
    cond_chain.tick()
    gain_chain.tick()
    qkv_sum = split_cols(rounded(held["qkv"].result(order.last)), 3)
    qkv_sum = jnp.stack(
        [select(qkv_sum[part], column_maps[part].T) for part in range(3)]
    )
    order.mark(qkv_sum)
    stay = pick(qkv_sum, qkv_home[0])
    middle = swap_core(pick(qkv_sum, qkv_home[1]))
    other = swap_chip(pick(qkv_sum, qkv_home[2]))
    cond_chain.tick()
    small_sum = held["small"].result(order.last)
    grad_attn_out, grad_cross_q, grad_cross_out = jnp.split(small_sum[: 3 * rows_here], 3)
    grad_crosskv = jnp.stack(jnp.split(small_sum[3 * rows_here :], 2), axis=1)
    order.mark(small_sum)
    gain_chain.tick()
    cond_chain.tick()

    here_wide = wide(joined_here)
    here_mid, here_inv = norm_stats(here_wide, 1)
    here_norm = (here_wide - here_mid) * here_inv
    cat_rows = cat_zero + wide(cat_got[:tokens_here]) + wide(order(cat_far))
    cat_scaled = cat_rows * skip_gain
    grad_joined = here_inv * (
        cat_scaled
        - jnp.mean(cat_scaled, axis=-1, keepdims=True)
        - here_norm * jnp.mean(cat_scaled * here_norm, axis=-1, keepdims=True)
    )
    grad_hidden = grad_joined[:, :D][None]
    grad_skip = grad_joined[:, D:][None]
    order.mark(grad_hidden)
    grad_w_skip = held["skip"].result(order.last)
    order.mark(grad_w_skip)
    gains = gain_chain.finish()
    cross_gains = gains[4 * D + 2 * HD :].reshape(shards, 2, own_cols)
    cross_gains = jnp.swapaxes(cross_gains, 0, 1).reshape(2, D)
    dmod_cols, cond_sum = cond_chain.finish()
    grad_mod = jnp.einsum(
        "nr,nc->rc",
        wide(cond_rows),
        dmod_cols,
        precision=lax.Precision.HIGHEST,
        preferred_element_type=jnp.float32,
    )
    cond_grad = reorder(cond_sum, [images.here ^ image for image in range(count)]).reshape(D)
    grad_condition = jax.vjp(jax.nn.silu, cond_vec)[1](cond_grad)[0][None]
    middle, other = order(middle, other)
    low_end = jnp.where(odd == 1, other, stay)
    high_end = jnp.where(odd == 1, stay, other)
    grad_w_qkv = wide(jnp.concatenate([low_end, middle, high_end], axis=-1))

    return (
        block_out,
        grad_hidden,
        grad_skip,
        grad_text,
        grad_condition,
        gains[: 2 * D],
        gains[2 * D : 4 * D],
        grad_w_skip,
        grad_mod,
        gains[4 * D : 4 * D + HD],
        gains[4 * D + HD : 4 * D + 2 * HD],
        grad_w_qkv,
        grad_attn_out,
        cross_gains[0],
        cross_gains[1],
        grad_cross_q,
        grad_crosskv,
        grad_cross_out,
        grad_fc1,
        grad_fc2,
    )


def solution(mesh):
    in_specs = (
        P("img", "seq", None),
        P("img", "seq", None),
        P("img", None, None),
        P("img", None),
        P("img", "seq", None),
        P("img", "seq", None),
        P(),
        P(),
        P("img", "seq"),
        P("img", "seq"),
        P(),
        P(),
        P("img", "seq"),
        P("img", "seq"),
        P(),
        P(),
        P("img", "seq"),
        P("img", None, "seq"),
        P("img", "seq"),
        P("img", "seq"),
        P("img", "seq"),
    )
    out_specs = (
        P("img", "seq", None),
        P("img", "seq", None),
        P("img", "seq", None),
        P("img", None, None),
        P("img", None),
        P(),
        P(),
        P("img", "seq"),
        P("img", "seq"),
        P(),
        P(),
        P("img", "seq"),
        P("img", "seq"),
        P(),
        P(),
        P("img", "seq"),
        P("img", None, "seq"),
        P("img", "seq"),
        P("img", "seq"),
        P("img", "seq"),
    )
    return jax.shard_map(
        per_device, mesh=mesh, in_specs=in_specs, out_specs=out_specs, check_vma=False
    )
```

```python
import functools
import math

import jax
import jax.numpy as jnp
import numpy as np
from jax import lax
from jax.experimental import pallas as pl
from jax.experimental.pallas import tpu as pltpu
from jax.sharding import PartitionSpec as P

D = 1408
H = 16
HD = 88

norm_eps = 1e-06
shards = 4
own_cols = D // shards
own_heads = H // shards
head_rows = 96
half_rows = head_rows // 2
quarter = HD // 4
padded_cols = own_heads * head_rows
vmem_bytes = 56 * 1024 * 1024
gelu_root = math.sqrt(2.0 / math.pi)
gelu_cube = 0.044715
log2_scale = HD ** (-0.5) / math.log(2.0)

core_pairs = ((0, 1), (1, 0), (2, 3), (3, 2))
chip_pairs = ((0, 2), (2, 0), (1, 3), (3, 1))
cross_pairs = ((0, 3), (3, 0), (1, 2), (2, 1))


def rounded(tensor):
    return tensor.astype(jnp.bfloat16)


def wide(tensor):
    return tensor.astype(jnp.float32)


def weigh(weights, tensors):
    return sum(
        jnp.einsum("kn,kt->nt", weight, tensor, preferred_element_type=jnp.float32)
        for weight, tensor in zip(weights, tensors)
    )


def weigh_back(weight, grad):
    return jnp.einsum("kn,nt->kt", weight, grad, preferred_element_type=jnp.float32)


def contract(left, right):
    return rounded(jnp.einsum("kt,nt->kn", left, right, preferred_element_type=jnp.float32))


def contract_pair(lefts, right):
    return tuple(contract(left, right) for left in lefts)


def norm_stats(tensor, axis):
    middle = jnp.mean(tensor, axis=axis, keepdims=True)
    center = tensor - middle
    spread = jnp.mean(center * center, axis=axis, keepdims=True)
    return middle, lax.rsqrt(spread + norm_eps)


def by_heads(tensor):
    return tensor.reshape(own_heads, HD, tensor.shape[-1])


def attend(queries, keys, values):
    scores = jnp.einsum(
        "hdk,hdq->hkq", keys, queries, preferred_element_type=jnp.float32
    ) * HD ** (-0.5)
    peak = jnp.max(scores, axis=1, keepdims=True)
    exp_scores = jnp.exp(scores - peak)
    total = jnp.sum(exp_scores, axis=1, keepdims=True)
    attn_probs = exp_scores / total
    outputs = jnp.einsum(
        "hdk,hkq->hdq", values, rounded(attn_probs), preferred_element_type=jnp.float32
    )
    return outputs, peak + jnp.log(total)


def attend_back(queries, keys, values, lse, grad_out):
    inv_root = HD ** (-0.5)
    scores = (
        jnp.einsum("hdk,hdq->hkq", keys, queries, preferred_element_type=jnp.float32) * inv_root
    )
    attn_probs = jnp.exp(scores - lse)
    grad_probs = jnp.einsum("hdk,hdq->hkq", values, grad_out, preferred_element_type=jnp.float32)
    delta = jnp.sum(attn_probs * grad_probs, axis=1, keepdims=True)
    grad_scores = rounded(attn_probs * (grad_probs - delta))
    grad_query = (
        jnp.einsum("hdk,hkq->hdq", keys, grad_scores, preferred_element_type=jnp.float32) * inv_root
    )
    grad_key = (
        jnp.einsum("hdq,hkq->hdk", queries, grad_scores, preferred_element_type=jnp.float32)
        * inv_root
    )
    grad_value = jnp.einsum(
        "hdq,hkq->hdk", grad_out, rounded(attn_probs), preferred_element_type=jnp.float32
    )
    return grad_query, grad_key, grad_value


def turned_rows():
    entry = np.arange(HD)
    axis, place = entry // (2 * quarter), entry % (2 * quarter)
    return (place // quarter) * half_rows + axis * quarter + place % quarter


def column_map(rows_of_entry):
    spread = np.zeros((own_cols, padded_cols), np.float32)
    for head in range(own_heads):
        spread[head * HD + np.arange(HD), head * head_rows + rows_of_entry] = 1.0
    return jnp.asarray(spread, jnp.bfloat16)


def select(left, right):
    return rounded(jnp.dot(left, right, preferred_element_type=jnp.float32))


def dot_across(left, right):
    return jnp.dot(left, right, preferred_element_type=jnp.float32)


def turn_head(raw, gain, cosine, sine_part):
    row = lax.broadcasted_iota(jnp.int32, raw.shape, 0)
    used = jnp.where(row % half_rows < 2 * quarter, 1.0, 0.0)
    center = (raw - jnp.sum(raw, axis=0, keepdims=True) * (1.0 / HD)) * used
    spread = jnp.sum(center * center, axis=0, keepdims=True) * (1.0 / HD)
    inverse = lax.rsqrt(spread + norm_eps)
    normed = center * inverse
    scaled = normed * gain
    first, second = scaled[:half_rows], scaled[half_rows:]
    turned = jnp.concatenate(
        [first * cosine - second * sine_part, first * sine_part + second * cosine], axis=0
    )
    return turned, normed, inverse, used


def turn_head_back(grad, normed, inverse, used, gain, cosine, sine_part):
    first, second = grad[:half_rows], grad[half_rows:]
    straight = jnp.concatenate(
        [first * cosine + second * sine_part, second * cosine - first * sine_part], axis=0
    )
    gain_grad = jnp.sum(straight * normed, axis=1, keepdims=True)
    scaled = straight * gain
    middle = jnp.sum(scaled, axis=0, keepdims=True) * (1.0 / HD)
    along = jnp.sum(scaled * normed, axis=0, keepdims=True) * (1.0 / HD)
    return inverse * (scaled - middle - normed * along) * used, gain_grad


key_chunk = 256


def attend_body(raw_ref, gain_ref, cos_ref, sin_ref, out_ref, low_ref, total_ref):
    cosine, sine_part = cos_ref[...], sin_ref[...]
    query = rounded(turn_head(raw_ref[0, 0], gain_ref[0], cosine, sine_part)[0])
    key_wide = turn_head(raw_ref[1, 0], gain_ref[1], cosine, sine_part)[0]
    value = rounded(raw_ref[2, 0])
    low_ref[0, 0] = query
    low_ref[1, 0] = rounded(key_wide)
    low_ref[2, 0] = value
    key_rows = rounded(key_wide.T)
    tokens = query.shape[1]
    total = jnp.zeros((1, tokens), jnp.float32)
    output = jnp.zeros((head_rows, tokens), jnp.float32)
    for start in range(0, tokens, key_chunk):
        scores = dot_across(key_rows[start : start + key_chunk], query)
        weights = jnp.exp2(scores * log2_scale)
        total = total + jnp.sum(weights, axis=0, keepdims=True)
        output = output + dot_across(value[:, start : start + key_chunk], rounded(weights))
    inverse = 1.0 / total
    total_ref[0] = inverse
    out_ref[0] = rounded((output * inverse)[:HD])


def attend_heads(raw, gains, cosine, sine_part):
    tokens = raw.shape[-1]
    heads = raw.shape[1]
    whole = lambda head: (0, 0)
    return pl.pallas_call(
        attend_body,
        grid=(heads,),
        out_shape=[
            jax.ShapeDtypeStruct((heads, HD, tokens), jnp.bfloat16),
            jax.ShapeDtypeStruct(raw.shape, jnp.bfloat16),
            jax.ShapeDtypeStruct((heads, 1, tokens), jnp.float32),
        ],
        in_specs=[
            pl.BlockSpec((3, 1, head_rows, tokens), lambda head: (0, head, 0, 0)),
            pl.BlockSpec((2, head_rows, 1), lambda head: (0, 0, 0)),
            pl.BlockSpec((half_rows, tokens), whole),
            pl.BlockSpec((half_rows, tokens), whole),
        ],
        out_specs=[
            pl.BlockSpec((1, HD, tokens), lambda head: (head, 0, 0)),
            pl.BlockSpec((3, 1, head_rows, tokens), lambda head: (0, head, 0, 0)),
            pl.BlockSpec((1, 1, tokens), lambda head: (head, 0, 0)),
        ],
        compiler_params=pltpu.CompilerParams(vmem_limit_bytes=vmem_bytes),
        cost_estimate=pl.CostEstimate(
            flops=4 * heads * tokens * tokens * 256,
            bytes_accessed=heads * tokens * 2000,
            transcendentals=heads * tokens * tokens,
        ),
    )(raw, gains, cosine, sine_part)


def attend_back_body(
    raw_ref, low_ref, total_ref, grad_ref, gain_ref, cos_ref, sin_ref, back_ref, gains_ref
):
    cosine, sine_part = cos_ref[...], sin_ref[...]
    query, key, value = low_ref[0, 0], low_ref[1, 0], low_ref[2, 0]
    tokens = query.shape[1]
    inverse_total = total_ref[0]
    grad_wide = wide(grad_ref[0])
    grad_wide = jnp.concatenate(
        [grad_wide, jnp.zeros((head_rows - HD, tokens), jnp.float32)], axis=0
    )
    grad = rounded(grad_wide)
    query_rows = rounded(wide(query).T)
    key_rows = rounded(wide(key).T)
    value_rows = rounded(wide(value).T)
    grad_rows = rounded(grad_wide.T)
    query_back = jnp.zeros((head_rows, tokens), jnp.float32)
    key_back, value_back = [], []
    delta = jnp.zeros((1, tokens), jnp.float32)
    chunks = [slice(start, start + key_chunk) for start in range(0, tokens, key_chunk)]
    held = []
    for chunk in chunks:
        scores = dot_across(key_rows[chunk], query)
        probs = jnp.exp2(scores * log2_scale) * inverse_total
        grad_probs = dot_across(value_rows[chunk], grad)
        delta = delta + jnp.sum(probs * grad_probs, axis=0, keepdims=True)
        held.append((probs, grad_probs))
    for chunk, (probs, grad_probs) in zip(chunks, held):
        grad_scores = rounded(probs * (grad_probs - delta))
        query_back = query_back + dot_across(key[:, chunk], grad_scores)
        key_back.append(dot_across(grad_scores, query_rows))
        value_back.append(dot_across(rounded(probs), grad_rows))
    root = HD ** (-0.5)
    key_back = jnp.concatenate(key_back, axis=0).T * root
    value_back = jnp.concatenate(value_back, axis=0).T
    for index, turned in enumerate((query_back * root, key_back)):
        gain = gain_ref[index]
        _, normed, inverse, used = turn_head(raw_ref[index, 0], gain, cosine, sine_part)
        straight, gain_grad = turn_head_back(
            turned, normed, inverse, used, gain, cosine, sine_part
        )
        back_ref[index, 0] = rounded(straight)
        gains_ref[0, index] = gain_grad
    back_ref[2, 0] = rounded(value_back)


def attend_heads_back(raw, low, inverse_total, grad, gains, cosine, sine_part):
    heads, tokens = raw.shape[1], raw.shape[-1]
    three = pl.BlockSpec((3, 1, head_rows, tokens), lambda head: (0, head, 0, 0))
    one = lambda rows: pl.BlockSpec((1, rows, tokens), lambda head: (head, 0, 0))
    whole = pl.BlockSpec((half_rows, tokens), lambda head: (0, 0))
    return pl.pallas_call(
        attend_back_body,
        grid=(heads,),
        out_shape=[
            jax.ShapeDtypeStruct(raw.shape, jnp.bfloat16),
            jax.ShapeDtypeStruct((heads, 2, head_rows, 1), jnp.float32),
        ],
        in_specs=[
            three,
            three,
            one(1),
            one(HD),
            pl.BlockSpec((2, head_rows, 1), lambda head: (0, 0, 0)),
            whole,
            whole,
        ],
        out_specs=[three, pl.BlockSpec((1, 2, head_rows, 1), lambda head: (head, 0, 0, 0))],
        compiler_params=pltpu.CompilerParams(vmem_limit_bytes=vmem_bytes),
        cost_estimate=pl.CostEstimate(
            flops=10 * heads * tokens * tokens * 256,
            bytes_accessed=heads * tokens * 3000,
            transcendentals=heads * tokens * tokens,
        ),
    )(raw, low, inverse_total, grad, gains, cosine, sine_part)


def norm_body(scale_at, shift_at, *refs):
    blocks, (columns_ref, keep_ref, away_ref, mid_ref, inv_ref) = refs[:4], refs[4:]
    base = wide(blocks[0][0:1])
    total = jnp.zeros(base.shape, jnp.float32)
    square = jnp.zeros(base.shape, jnp.float32)
    for block in blocks:
        shifted = wide(block[...]) - base
        total = total + jnp.sum(shifted, axis=0, keepdims=True)
        square = square + jnp.sum(shifted * shifted, axis=0, keepdims=True)
    total = total * (1.0 / D)
    inverse = lax.rsqrt(square * (1.0 / D) - total * total + norm_eps)
    middle = base + total
    mid_ref[...] = middle
    inv_ref[...] = inverse
    for index, block in enumerate(blocks):
        target = (keep_ref, away_ref)[index // 2]
        inner = (index % 2) * own_cols
        rows = slice(index * own_cols, (index + 1) * own_cols)
        scale = columns_ref[rows, scale_at : scale_at + 1]
        shift = columns_ref[rows, shift_at : shift_at + 1]
        normed = (wide(block[...]) - middle) * inverse
        target[inner : inner + own_cols] = rounded(normed * scale + shift)


def norm_columns(blocks, columns, scale_at, shift_at):
    tokens = blocks[0].shape[1]
    tile = 512
    part = pl.BlockSpec((own_cols, tile), lambda step: (0, step))
    half = pl.BlockSpec((2 * own_cols, tile), lambda step: (0, step))
    row = pl.BlockSpec((1, tile), lambda step: (0, step))
    keep, away, middle, inverse = pl.pallas_call(
        functools.partial(norm_body, scale_at, shift_at),
        grid=(tokens // tile,),
        out_shape=[
            jax.ShapeDtypeStruct((2 * own_cols, tokens), jnp.bfloat16),
            jax.ShapeDtypeStruct((2 * own_cols, tokens), jnp.bfloat16),
            jax.ShapeDtypeStruct((1, tokens), jnp.float32),
            jax.ShapeDtypeStruct((1, tokens), jnp.float32),
        ],
        in_specs=[part] * 4 + [pl.BlockSpec(columns.shape, lambda step: (0, 0))],
        out_specs=[half, half, row, row],
        compiler_params=pltpu.CompilerParams(vmem_limit_bytes=vmem_bytes),
        cost_estimate=pl.CostEstimate(
            flops=10 * D * tokens, bytes_accessed=4 * D * tokens, transcendentals=0
        ),
    )(*blocks, columns)
    return (keep, away), middle, inverse


def joined_body(places_ref, *refs):
    blocks, (vectors_ref, cat_ref, norm_ref) = refs[:4], refs[4:]
    gain, bias = vectors_ref[0:1], vectors_ref[1:2]
    for index, block in enumerate(blocks):
        tensor = wide(block[...])
        center = tensor - jnp.mean(tensor, axis=1, keepdims=True)
        spread = jnp.mean(center * center, axis=1, keepdims=True)
        normed = center * lax.rsqrt(spread + norm_eps)
        norm_ref[places_ref[index]] = rounded(normed)
        cat_ref[places_ref[index]] = rounded(normed * gain + bias)


def norm_joined(blocks, places, vectors):
    rows, cols = blocks[0].shape
    tile = 64
    shape = jax.ShapeDtypeStruct((4, rows, cols), jnp.bfloat16)
    part = pl.BlockSpec((tile, cols), lambda step: (step, 0))
    vector = pl.BlockSpec((2, cols), lambda step: (0, 0))
    every = pl.BlockSpec((4, tile, cols), lambda step: (0, step, 0))
    cat_low, norm_low = pl.pallas_call(
        joined_body,
        grid=(rows // tile,),
        out_shape=[shape, shape],
        in_specs=[pl.BlockSpec(memory_space=pltpu.SMEM)] + [part] * 4 + [vector],
        out_specs=[every, every],
        compiler_params=pltpu.CompilerParams(vmem_limit_bytes=vmem_bytes),
        cost_estimate=pl.CostEstimate(
            flops=40 * rows * cols, bytes_accessed=24 * rows * cols, transcendentals=0
        ),
    )(places, *blocks, vectors)
    return cat_low.reshape(4 * rows, cols), norm_low.reshape(4 * rows, cols)


def swap_core(tensor):
    return lax.ppermute(tensor, "seq", core_pairs)


def swap_chip(tensor):
    return lax.ppermute(tensor, "seq", chip_pairs)


def pick(tensor, index):
    return lax.dynamic_index_in_dim(
        tensor, index, 0, keepdims=False, allow_negative_indices=False
    )


def part_at(tensor, start, size, axis):
    return lax.dynamic_slice_in_dim(tensor, start, size, axis, allow_negative_indices=False)


def in_pairs(blocks):
    return jnp.concatenate(blocks[:2]), jnp.concatenate(blocks[2:])


def spread_rows(own):
    far = swap_chip(own)
    near = swap_core(own)
    return own, far, near, swap_core(far)


def fold_features(grad, weights, work=None):
    half = own_cols
    away = weigh_back(weights[1], grad)
    got = swap_core(rounded(away))
    keep = weigh_back(weights[0], grad)
    sent = rounded(keep[half:] + wide(got[half:]))
    far = swap_chip(sent)
    if work is not None:
        far = after(far, work(sent))
    total = keep[:half] + wide(got[:half]) + wide(far)
    return total, keep, away


def place(blocks, here):
    places = here ^ jnp.arange(shards, dtype=jnp.int32)
    rows, cols = blocks[0].shape
    moves = [(index, 0, index, 0, rows, 0, 0, cols) for index in range(shards)]
    return move_blocks(blocks, moves, places, [((shards, rows, cols), False)])[0]


def reorder(tensor, order, axis=0):
    return jnp.concatenate([part_at(tensor, index, 1, axis) for index in order], axis=axis)


def split_cols(tensor, parts):
    size = tensor.shape[1] // parts
    return jnp.stack([tensor[:, part * size : (part + 1) * size] for part in range(parts)])


def join_cols(blocks):
    return jnp.concatenate([blocks[part] for part in range(blocks.shape[0])], axis=1)


def gather_small(own, here):
    far = swap_chip(own)
    near = swap_core(own)
    blocks = jnp.stack([own, near, far, swap_core(far)])
    return reorder(blocks, [here ^ shard for shard in range(shards)])


def sum_small(own):
    pair = own + swap_core(own)
    return pair + swap_chip(pair)


def trade_starts(pieces, here):
    return (
        pick(pieces, here),
        swap_core(pick(pieces, here ^ 1)),
        swap_chip(pick(pieces, here ^ 2)),
        lax.ppermute(pick(pieces, here ^ 3), "seq", cross_pairs),
    )


def ring_tables(count):
    order = [0] + list(range(1, count, 2)) + list(range(count - 2, 0, -2))
    spot = [order.index(index) for index in range(count)]
    up = tuple((order[step], order[(step + 1) % count]) for step in range(count))
    down = tuple((after, before) for before, after in up)
    return order, spot, up, down


def move_blocks(sources, moves, places, targets):
    def body(places_ref, *refs):
        outs, first = [], len(sources)
        for _, paired in targets:
            outs.append(refs[first : first + (2 if paired else 1)])
            first += len(outs[-1])
        for source, row, entry, inner, size, target, lane, width in moves:
            block = refs[source][pl.ds(row, size), pl.ds(0, width)]
            where = (pl.ds(inner, size), pl.ds(lane, width))
            spot = places_ref[entry]
            if len(outs[target]) == 1:
                outs[target][0][(spot,) + where] = block
                continue
            half = targets[target][0][0]

            @pl.when(spot < half)
            def store_first():
                outs[target][0][(spot,) + where] = block

            @pl.when(spot >= half)
            def store_second():
                outs[target][1][(spot - half,) + where] = block

    shapes = [
        jax.ShapeDtypeStruct(shape, sources[0].dtype)
        for shape, paired in targets
        for _ in range(2 if paired else 1)
    ]
    size = sum(math.prod(shape.shape) for shape in shapes)
    return pl.pallas_call(
        body,
        out_shape=shapes,
        in_specs=[pl.BlockSpec(memory_space=pltpu.SMEM)]
        + [pl.BlockSpec(memory_space=pltpu.VMEM)] * len(sources),
        out_specs=[pl.BlockSpec(memory_space=pltpu.VMEM)] * len(shapes),
        compiler_params=pltpu.CompilerParams(vmem_limit_bytes=vmem_bytes),
        cost_estimate=pl.CostEstimate(flops=0, bytes_accessed=4 * size, transcendentals=0),
    )(places, *sources)


def pick_blocks(source, table, paired_rows, plain_rows):
    count, _, cols = source.shape
    half = count // 2
    shapes = []
    for rows in paired_rows:
        shapes += [(half, rows, cols)] * 2
    shapes += [(count, rows, cols) for rows in plain_rows]

    def body(table_ref, source_ref, *targets):
        row = 0
        for part, rows in enumerate(paired_rows):
            for entry in range(count):
                target = targets[2 * part + entry // half]
                target[entry % half] = source_ref[table_ref[entry], pl.ds(row, rows)]
            row += rows
        for part, rows in enumerate(plain_rows):
            targets[2 * len(paired_rows) + part][...] = source_ref[:, pl.ds(row, rows)]
            row += rows

    picked = pl.pallas_call(
        body,
        out_shape=[jax.ShapeDtypeStruct(shape, source.dtype) for shape in shapes],
        in_specs=[
            pl.BlockSpec(memory_space=pltpu.SMEM),
            pl.BlockSpec(memory_space=pltpu.VMEM),
        ],
        out_specs=[pl.BlockSpec(memory_space=pltpu.VMEM)] * len(shapes),
        compiler_params=pltpu.CompilerParams(vmem_limit_bytes=vmem_bytes),
        cost_estimate=pl.CostEstimate(
            flops=0, bytes_accessed=4 * math.prod(source.shape), transcendentals=0
        ),
    )(table, source)
    picked = [piece.reshape(-1, cols) for piece in picked]
    first = 2 * len(paired_rows)
    return list(zip(picked[:first:2], picked[1:first:2])) + picked[first:]


def arrange_blocks(grads, tables, entries):
    rows = [grad[0].shape[1] for grad in grads]
    cols = max(grad[0].shape[2] for grad in grads)
    flat = [array for grad in grads for array in grad]

    def body(*refs):
        tables_refs, array_refs = refs[: len(grads)], refs[len(grads) : len(grads) + len(flat)]
        targets = refs[len(grads) + len(flat) :]
        base, first = 0, 0
        for grad, table_ref, size in zip(grads, tables_refs, rows):
            for entry, target in enumerate(targets):
                spot = table_ref[entry]
                begin = 0
                for index, array in enumerate(grad):
                    end = begin + array.shape[0]

                    @pl.when((spot >= begin) & (spot < end))
                    def store(index=index, begin=begin):
                        target[pl.ds(base, size)] = array_refs[first + index][spot - begin]

                    begin = end
            base, first = base + size, first + len(grad)

    shape = jax.ShapeDtypeStruct((sum(rows), cols), flat[0].dtype)
    return pl.pallas_call(
        body,
        out_shape=[shape] * entries,
        in_specs=[pl.BlockSpec(memory_space=pltpu.SMEM)] * len(grads)
        + [pl.BlockSpec(memory_space=pltpu.VMEM)] * len(flat),
        out_specs=[pl.BlockSpec(memory_space=pltpu.VMEM)] * entries,
        compiler_params=pltpu.CompilerParams(vmem_limit_bytes=vmem_bytes),
        cost_estimate=pl.CostEstimate(
            flops=0, bytes_accessed=4 * entries * math.prod(shape.shape), transcendentals=0
        ),
    )(*tables, *flat)


class Images:

    def __init__(self):
        self.count = lax.axis_size("img")
        self.here = lax.axis_index("img")
        self.bits = [1 << bit for bit in range((self.count - 1).bit_length())]
        self.direct = self.count != 8
        order, spot, self.up, self.down = ring_tables(self.count)
        self.order = order
        self.spot = spot


    def swap(self, tensor, bit):
        return lax.ppermute(
            tensor, "img", tuple((index, index ^ bit) for index in range(self.count))
        )

    def gather_small(self, own):
        held = own[None]
        for bit in self.bits:
            held = jnp.concatenate([held, self.swap(held, bit)])
        return held

    def scatter_small(self, terms):
        held = terms
        for bit in reversed(self.bits):
            held = held[:bit] + self.swap(held[bit:], bit)
        return held[0]

    def trade_small(self, rows):
        held = rows
        for bit in self.bits:
            split = held.reshape((-1, 2, bit) + rows.shape[1:])
            split = jnp.stack([split[:, 0], self.swap(split[:, 1], bit)], axis=1)
            held = split.reshape(rows.shape)
        return held

    def sum_small(self, own):
        for bit in self.bits:
            own = own + self.swap(own, bit)
        return own


    def table(self, entry_of, size):
        table = np.zeros((shards, self.count, size), np.int32)
        for shard in range(shards):
            for image in range(self.count):
                for entry in range(size):
                    table[shard, image, entry] = entry_of(shard, image, entry)
        table = jnp.asarray(table.reshape(shards * self.count, size))
        return pick(table, lax.axis_index("seq") * self.count + self.here)

    def places(self, slots, offsets):
        def entry_of(shard, image, entry):
            return slots(shard, self.order[(self.spot[image] + offsets[entry]) % self.count])

        return self.table(entry_of, len(offsets))


class GatherRing:
    def __init__(self, images, shard, halves=False):
        self.images = images
        self.shard = shard
        self.blocks, self.offsets, self.starts = [shard], [0], [0]
        self.halves = halves
        self.middle = (shard.shape[0] // 2 + 15) // 16 * 16
        self.upward = self.downward = shard
        self.step = 0
        self.reach = images.count // 2

    def advance(self, tie=()):
        images = self.images
        if images.direct:
            return self.shard
        self.step += 1
        upward, downward = after((self.upward, self.downward), tie)
        if self.step < self.reach:
            self.upward = lax.ppermute(upward, "img", images.up)
            self.downward = lax.ppermute(downward, "img", images.down)
            self.blocks += [self.upward, self.downward]
            self.offsets += [-self.step, self.step]
            self.starts += [0, 0]
        elif self.halves:
            self.upward = lax.ppermute(upward[: self.middle], "img", images.up)
            self.downward = lax.ppermute(downward[self.middle :], "img", images.down)
            self.blocks += [self.upward, self.downward]
            self.offsets += [-self.reach, -self.reach]
            self.starts += [0, self.middle]
        else:
            self.upward = lax.ppermute(upward, "img", images.up)
            self.blocks.append(self.upward)
            self.offsets.append(-self.reach)
            self.starts.append(0)
        return upward, downward

    def result(self, segments, targets):
        images = self.images
        count = images.count
        if images.direct:
            whole = lax.all_gather(self.shard, "img", axis=0)
            wholes = [[] for _ in targets]
            row = 0
            for rows, slots, target, _, width in segments:
                back = images.table(
                    lambda shard, image, entry: next(
                        other for other in range(count) if slots(shard, other) == entry
                    ),
                    count,
                )
                piece = jnp.take(whole[:, row : row + rows, :width], back, axis=0)
                wholes[target].append(piece.reshape(count * rows, width))
                row += rows
            wholes = [jnp.concatenate(pieces, axis=-1) for pieces in wholes]
            return [
                tuple(jnp.split(whole, 2)) if paired else whole
                for whole, (_, paired) in zip(wholes, targets)
            ]
        all_slots = []
        for _, slots, _, _, _ in segments:
            if slots not in all_slots:
                all_slots.append(slots)
        places = jnp.concatenate([images.places(slots, self.offsets) for slots in all_slots])
        moves = []
        for index, (block, start) in enumerate(zip(self.blocks, self.starts)):
            base = 0
            for rows, slots, target, lane, width in segments:
                low, high = max(base, start), min(base + rows, start + block.shape[0])
                if low < high:
                    entry = all_slots.index(slots) * len(self.offsets) + index
                    moves.append(
                        (index, low - start, entry, low - base, high - low, target, lane, width)
                    )
                base += rows
        placed = iter(move_blocks(self.blocks, moves, places, targets))
        results = []
        for _, paired in targets:
            pieces = tuple(next(placed) for _ in range(2 if paired else 1))
            pieces = tuple(piece.reshape(-1, piece.shape[-1]) for piece in pieces)
            results.append(pieces if paired else pieces[0])
        return results


class ScatterRing:
    def __init__(self, images, grads, slots):
        self.images = images
        count = images.count
        grads = [
            tuple(
                part.reshape(-1, sum(each.shape[0] for each in grad) // count, part.shape[1])
                for part in grad
            )
            for grad in grads
        ]
        self.grads, self.slots = grads, slots
        self.reach = count // 2
        self.step = 0
        if images.direct:
            return
        offsets = [self.reach]
        for step in range(2, self.reach + 1):
            offsets += [self.reach - step + 1, step - self.reach - 1]
        offsets.append(0)
        tables = [images.places(slots_of, offsets) for slots_of in slots]
        self.blocks = arrange_blocks(grads, tables, len(offsets))

    def advance(self, tie=()):
        images = self.images
        if images.direct:
            return self.grads
        self.step += 1
        blocks = self.blocks
        if self.step == 1:
            ahead = after(blocks[0], tie)
            self.upward = lax.ppermute(ahead, "img", images.up)
            return (ahead,)
        ahead, behind = blocks[2 * self.step - 3], blocks[2 * self.step - 2]
        if self.step == 2:
            upward, behind = after((self.upward, behind), tie)
        else:
            upward, downward = after((self.upward, self.downward), tie)
            behind = rounded(wide(behind) + wide(downward))
        ahead = rounded(wide(ahead) + wide(upward))
        self.upward = lax.ppermute(ahead, "img", images.up)
        self.downward = lax.ppermute(behind, "img", images.down)
        return ahead, behind

    def blocks_ready(self):
        return () if self.images.direct else self.blocks

    def result(self, tie=()):
        images = self.images
        if images.direct:
            count = images.count
            every = []
            cols = max(grad[0].shape[2] for grad in self.grads)
            for grad, slots in zip(self.grads, self.slots):
                order = images.table(lambda shard, image, entry: slots(shard, entry), count)
                block = jnp.take(jnp.concatenate(grad), order, axis=0)
                every.append(jnp.pad(block, ((0, 0), (0, 0), (0, cols - block.shape[2]))))
            every = wide(jnp.concatenate(every, axis=1))
            return lax.psum_scatter(every, "img", scatter_dimension=0, tiled=False)
        upward, downward = after((self.upward, self.downward), tie)
        return wide(self.blocks[-1]) + wide(upward) + wide(downward)


def after(tensor, mark):
    return lax.optimization_barrier((tensor, mark))[0]


class Order:
    def __init__(self):
        self.last = ()

    def __call__(self, *tensors):
        held = after(tensors, self.last)
        return held if len(tensors) > 1 else held[0]

    def mark(self, *tensors):
        self.last = tensors

    def step(self, ring):
        self.mark(ring.advance(self.last))


class Chain:
    def __init__(self, steps):
        self.steps = steps
        self.value = None
        self.running = True
        self.tick()

    def tick(self):
        if not self.running:
            return
        try:
            next(self.steps)
        except StopIteration as stop:
            self.value = stop.value
            self.running = False

    def finish(self):
        while self.running:
            self.tick()
        return self.value


def per_device(
    hidden_in,
    skip_in,
    text,
    condition,
    positions,
    out_grad,
    skip_gain,
    skip_bias,
    w_skip,
    w_mod,
    q_gain,
    k_gain,
    w_qkv,
    w_attn_out,
    cross_gain,
    cross_bias,
    w_cross_q,
    w_cross_kv,
    w_cross_out,
    w_fc1,
    w_fc2,
):
    here = lax.axis_index("seq")
    images = Images()
    count = images.count
    per_shard = count // shards
    rows_here = D // count
    text_rows = w_cross_kv.shape[0]
    hidden_units = w_fc2.shape[0] // shards
    tokens_here = hidden_in.shape[1]
    tokens = shards * tokens_here
    relative = [here, here ^ 2, here ^ 1, here ^ 3]

    def straight(shard, index):
        return index

    def turned(shard, index):
        return (0, 2, 1, 3)[(index // per_shard) ^ shard] * per_shard + index % per_shard

    order = Order()
    odd = here % 2
    places = here ^ jnp.arange(shards, dtype=jnp.int32)
    turn_map, plain_map = column_map(turned_rows()), column_map(np.arange(HD))
    column_maps = jnp.stack([turn_map, turn_map, plain_map])

    def send(own):
        order.mark(own)
        return swap_chip(own), swap_core(own)

    def receive(own, far, near):
        far = order(far)
        order.mark(far)
        return order(own, far, near, swap_core(far))

    skip_ring = GatherRing(images, rounded(w_skip))
    order.step(skip_ring)
    joined_here = order(jnp.concatenate([hidden_in[0], skip_in[0]], axis=-1))
    joined_far, joined_near = send(joined_here)
    cond_vec = wide(condition[0])
    cond_low = rounded(jax.nn.silu(cond_vec))
    mod_low = rounded(w_mod)

    def modulation():
        held = order(cond_low)[None]
        order.mark(held)
        for bit in images.bits:
            other = images.swap(held, bit)
            yield
            held = jnp.concatenate([held, order(other)])
            order.mark(held)
        rows = part_at(held, images.here * rows_here, rows_here, 1)
        held = jnp.dot(rows, mod_low, preferred_element_type=jnp.float32)
        order.mark(held)
        for bit in reversed(images.bits):
            other = images.swap(held[bit:], bit)
            yield
            held = held[:bit] + order(other)
            order.mark(held)
        own = held[0]
        far, near = swap_chip(own), swap_core(own)
        yield
        far = order(far)
        order.mark(far)
        diagonal = swap_core(far)
        yield
        blocks = jnp.stack(order(own, near, far, diagonal))
        vectors = reorder(blocks, [here ^ shard for shard in range(shards)]).reshape(6, D)
        order.mark(vectors)
        return rows, vectors

    mod_chain = Chain(modulation())
    qkv_here = rounded(order(w_qkv))
    qkv_parts = split_cols(qkv_here, 3)
    kept = jnp.where(odd == 1, qkv_parts[2], qkv_parts[0])
    sent = jnp.where(odd == 1, qkv_parts[0], qkv_parts[2])
    order.mark(kept, sent)
    qkv_mix = [kept, swap_core(qkv_parts[1]), swap_chip(sent)]
    grid_here = order(positions[0].T)
    grid_far, grid_near = send(grid_here)
    order.step(skip_ring)
    mod_chain.tick()
    mod_chain.tick()
    order.step(skip_ring)
    qkv_mix = jnp.stack(order(*qkv_mix))
    qkv_order = pick(np.array([[0, 1, 2], [1, 0, 2], [2, 0, 1], [2, 1, 0]], np.int32), here)
    qkv_home = pick(np.array([[0, 1, 2], [1, 0, 2], [1, 2, 0], [2, 1, 0]], np.int32), here)
    qkv_own = jnp.concatenate(
        [select(pick(qkv_mix, qkv_order[part]), column_maps[part]) for part in range(3)]
    )
    qkv_ring = GatherRing(images, qkv_own)
    order.mark(qkv_own)
    order.step(qkv_ring)
    mod_chain.tick()
    unit = np.arange(w_fc1.shape[1])
    image_of, inner = unit // (w_fc1.shape[1] // per_shard), unit % (w_fc1.shape[1] // per_shard)
    slot_of = (inner // hidden_units) * per_shard * hidden_units
    slot_of = slot_of + image_of * hidden_units + inner % hidden_units
    unit_map = np.zeros((w_fc1.shape[1], w_fc1.shape[1]), np.float32)
    unit_map[unit, slot_of] = 1.0
    unit_map = jnp.asarray(unit_map, jnp.bfloat16)
    later = order(w_fc1, w_fc2)
    fc1_pieces = split_cols(select(rounded(later[0]), unit_map), shards)
    fc2_pieces = rounded(later[1]).reshape(shards, hidden_units, own_cols)
    skip_rows = order(jnp.stack([skip_gain, skip_bias]))
    order.mark(fc1_pieces, fc2_pieces, skip_rows)
    grid = receive(grid_here, grid_far, grid_near)
    grid = jnp.stack([grid[0], grid[2], grid[1], grid[3]])
    grid = reorder(grid, [here ^ shard for shard in range(shards)])
    order.mark(grid)
    order.step(skip_ring)
    mod_chain.tick()
    order.step(qkv_ring)
    joined = receive(joined_here, joined_far, joined_near)
    joined = (joined[0], joined[2], joined[1], joined[3])
    cotangent_far = swap_chip(order(out_grad[0]))
    fc1_trade, fc2_trade = trade_starts(order(fc1_pieces), here), trade_starts(fc2_pieces, here)
    mod_chain.tick()
    (skip_all,) = skip_ring.result(
        [(2 * rows_here, straight, 0, 0, own_cols)], [((count, 2 * rows_here, own_cols), False)]
    )
    skip_all = order(skip_all)
    order.mark(skip_all)
    order.step(qkv_ring)
    mod_chain.tick()
    cond_rows, modul = mod_chain.finish()
    later = order(w_attn_out, w_cross_q, w_cross_out, w_cross_kv)
    crosskv = rounded(later[3])
    small = [rounded(weight) for weight in later[:3]] + [crosskv[:, 0], crosskv[:, 1]]
    small = jnp.concatenate(small)
    order.mark(small)
    small_ring = GatherRing(images, small)
    order.step(small_ring)
    cat_low, joined_norm = norm_joined(order(*joined), places, skip_rows)
    order.mark(cat_low)
    order.step(qkv_ring)
    one_own = jnp.einsum("kn,tk->nt", skip_all, order(cat_low), preferred_element_type=jnp.float32)
    one_low = rounded(one_own)
    order.mark(one_low)
    order.step(small_ring)
    cotangent_far, *trades = order(cotangent_far, *fc1_trade, *fc2_trade)
    one_low = after(one_low, (cotangent_far, trades))

    far, near = send(one_low)
    vectors = jnp.concatenate([order(modul), cross_gain[None], cross_bias[None]])
    one_plus = np.zeros((8, 1), np.float32)
    one_plus[[1, 4]] = 1.0
    columns = (vectors + one_plus).T
    columns = jnp.concatenate(
        [part_at(columns, index * own_cols, own_cols, 0) for index in relative]
    )
    shift_one, scale_one = columns[:, 0:1], columns[:, 1:2]
    shift_two, scale_two = columns[:, 3:4], columns[:, 4:5]
    cross_scale, cross_shift = columns[:, 6:7], columns[:, 7:8]
    gate_one = columns[:own_cols, 2:3]
    gate_two = modul[5]
    order.mark(columns)
    grid_pos = jnp.swapaxes(order(grid), 0, 1).reshape(2, 1, tokens).astype(jnp.float32)
    row = np.arange(half_rows)
    frequency = np.where(row < 2 * quarter, 10000.0 ** (-(row % quarter) / quarter), 0.0)
    frequency = jnp.asarray(frequency[:, None], jnp.float32)
    angles = jnp.where((row < quarter)[:, None], grid_pos[0], grid_pos[1]) * frequency
    cosine, sine_part = jnp.cos(angles), jnp.sin(angles)
    entry_rows = turned_rows()
    head_map = np.zeros((head_rows, HD), np.float32)
    head_map[entry_rows, np.arange(HD)] = 1.0
    gains_low = jnp.dot(
        jnp.stack([q_gain, k_gain]), head_map.T, precision=lax.Precision.HIGHEST
    )[:, :, None]
    order.mark(cosine, sine_part, gains_low)
    fc1_own = join_cols(place(order(*trades[:4]), here))
    fc2_own = join_cols(place(order(*trades[4:]), here))
    fc2_pad = jnp.zeros((hidden_units, w_fc1.shape[1] - D), jnp.bfloat16)
    fc_own = jnp.concatenate([fc1_own, jnp.concatenate([fc2_own, fc2_pad], axis=1)])
    order.mark(fc_own)
    fc_ring = GatherRing(images, fc_own, halves=True)
    (qkv_all,) = qkv_ring.result(
        [(rows_here, turned, 0, part * padded_cols, padded_cols) for part in range(3)],
        [((count // 2, rows_here, 3 * padded_cols), True)],
    )
    qkv_all = order(*qkv_all)
    order.mark(qkv_all)
    order.step(small_ring)
    one_blocks = receive(one_low, far, near)
    attn_in, one_mid, one_inv = norm_columns(one_blocks, columns, 1, 0)
    order.mark(attn_in)
    qkv_raw = weigh(qkv_all, order(*attn_in)).reshape(3, own_heads, head_rows, tokens)
    order.mark(qkv_raw)
    order.step(small_ring)
    attn_raw, qkv_low, attn_total = attend_heads(order(qkv_raw), gains_low, cosine, sine_part)
    attn_own = attn_raw.reshape(own_cols, tokens)

    far, near = send(attn_own)
    order.step(fc_ring)
    attn_out_all, cross_q_all, cross_out_all, *crosskv_all = small_ring.result(
        [(rows_here, turned, part, 0, own_cols) for part in range(3)]
        + [(text_rows, straight, part, 0, own_cols) for part in (3, 4)],
        [((count // 2, rows_here, own_cols), True)] * 3
        + [((count, text_rows, own_cols), False)] * 2,
    )
    crosskv_all = order(*crosskv_all)
    order.mark(crosskv_all)
    cotangent = (out_grad[0], swap_core(order(out_grad[0])), cotangent_far, swap_core(cotangent_far))
    attn_blocks = receive(attn_own, far, near)
    order.step(fc_ring)
    attn_low = in_pairs(order(*attn_blocks))
    branch_own = weigh(attn_out_all, attn_low)
    two_own = one_own + gate_one * branch_own
    two_low = rounded(two_own)

    far, near = send(two_low)
    text_keys, text_values = [
        by_heads(
            rounded(
                jnp.einsum("kn,tk->nt", weight, text[0], preferred_element_type=jnp.float32)
            )
        )
        for weight in order(*crosskv_all)
    ]
    order.mark(text_keys, text_values)
    cotangent = place(order(*cotangent), here).reshape(tokens, D)
    order.mark(cotangent)
    cot_wide = wide(order(cotangent))
    grad_mlp = rounded(cot_wide * gate_two)
    order.mark(grad_mlp)
    two_blocks = receive(two_low, far, near)
    order.step(fc_ring)
    two_blocks = order(*two_blocks)
    cross_in, two_mid, two_inv = norm_columns(two_blocks, columns, 6, 7)
    cross_query = by_heads(rounded(weigh(cross_q_all, cross_in)))
    cross_raw, cross_lse = attend(cross_query, text_keys, text_values)
    cross_own = rounded(cross_raw.reshape(own_cols, tokens))
    far, near = send(cross_own)
    order.step(fc_ring)
    cross_low = in_pairs(receive(cross_own, far, near))
    three_own = two_own + weigh(cross_out_all, cross_low)
    three_sent = rounded(three_own)

    far, near = send(three_sent)
    fc1_all, fc2_all = fc_ring.result(
        [
            (rows_here, turned, 0, 0, w_fc1.shape[1]),
            (hidden_units, straight, 1, 0, D),
        ],
        [
            ((count // 2, rows_here, w_fc1.shape[1]), True),
            ((count, hidden_units, D), False),
        ],
    )
    *fc1_all, fc2_all = order(*fc1_all, fc2_all)
    order.mark(fc2_all)
    three_low = receive(three_sent, far, near)
    mlp_in, three_mid, three_inv = norm_columns(three_low, columns, 4, 3)
    upper = weigh(fc1_all, mlp_in)
    bend = jnp.tanh(gelu_root * (upper + gelu_cube * upper * upper * upper))
    act_low = rounded(0.5 * upper * (1.0 + bend))
    slope = 0.5 * (1.0 + bend) + 0.5 * upper * (1.0 - bend * bend) * gelu_root * (
        1.0 + 3.0 * gelu_cube * upper * upper
    )
    act_low, slope = lax.optimization_barrier((act_low, slope))

    grad_act = jnp.einsum("uc,tc->ut", fc2_all, grad_mlp, preferred_element_type=jnp.float32)
    grad_upper = rounded(grad_act * slope)
    canonical = jnp.arange(D, dtype=jnp.int32)
    own_map = canonical[:, None] == here * own_cols + canonical[None, :own_cols]
    cot_own = jnp.einsum(
        "tc,cn->nt", cotangent, rounded(own_map), preferred_element_type=jnp.float32
    )
    held = {}

    def norm_back(grad, weights, gain_rel, normed, shift, norm_inv, own, work):
        total, keep, away = fold_features(grad, weights, work)
        half = D // 2
        kept = keep * gain_rel[:half]
        gone = away * gain_rel[half:]
        sums = jnp.stack(
            [
                jnp.sum(kept, axis=0) + jnp.sum(gone, axis=0),
                jnp.sum(keep * (wide(normed[0]) - shift[:half]), axis=0)
                + jnp.sum(away * (wide(normed[1]) - shift[half:]), axis=0),
            ]
        )
        means = sum_small(sums) * (1.0 / D)
        scaled = total * gain_rel[:own_cols]
        grad_in = norm_inv * (scaled - means[:1] - own * means[1:])
        return grad_in, jnp.sum(total * own, axis=1), jnp.sum(total, axis=1)

    def work_three(sent):
        fc2_grad = contract(after(act_low, sent), grad_mlp.T)
        fc1_grad = contract_pair(mlp_in, after(grad_upper, sent))
        held["fc1_pair"] = fc1_grad
        held["fc2"] = lax.psum_scatter(fc2_grad, "img", scatter_dimension=0, tiled=True)
        return fc2_grad, held["fc1_pair"]

    three_own_norm = (three_own - three_mid) * three_inv
    back_three, d_scale_two, d_shift_two = norm_back(
        grad_upper, fc1_all, scale_two, mlp_in, shift_two, three_inv, three_own_norm, work_three
    )
    grad_three = cot_own + back_three

    grad_cross = rounded(grad_three)

    def work_cross(sent):
        act_held = after(act_low, sent)
        mlp_part = jnp.einsum("ut,uc->tc", act_held, fc2_all, preferred_element_type=jnp.float32)
        held["mlp"] = mlp_part.reshape(shards, tokens_here, D)
        held["d_gate_two"] = jnp.sum(cot_wide * mlp_part, axis=0)
        held["cross_out"] = contract_pair(cross_low, after(grad_cross, sent))
        fc1_grad = move_blocks(
            after(held["fc1_pair"], sent),
            [
                (index // 2, (index % 2) * own_cols, index, 0, own_cols, 0, 0, w_fc1.shape[1])
                for index in range(shards)
            ],
            jnp.stack(relative),
            [((shards, own_cols, w_fc1.shape[1]), False)],
        )[0].reshape(D, -1)
        held["fc1"] = lax.psum_scatter(
            after(fc1_grad, held["fc2"]), "img", scatter_dimension=0, tiled=True
        )
        return held["d_gate_two"], held["cross_out"], fc1_grad

    grad_cross_attn = fold_features(grad_cross, cross_out_all, work_cross)[0]
    grad_cross_attn = by_heads(rounded(grad_cross_attn))
    cross_back = attend_back(cross_query, text_keys, text_values, cross_lse, grad_cross_attn)
    grad_cquery = rounded(cross_back[0].reshape(own_cols, tokens))
    text_grad = rounded(jnp.concatenate([cross_back[1], cross_back[2]])).reshape(2 * own_cols, -1)
    two_own_norm = (two_own - two_mid) * two_inv

    def work_two(sent):
        grad_held = after(text_grad, sent)
        kv_grads = [
            (rounded(jnp.einsum("tk,nt->kn", text[0], grad, preferred_element_type=jnp.float32)),)
            for grad in (grad_held[:own_cols], grad_held[own_cols:])
        ]
        held["kv"] = kv_grads
        text_part = sum(
            jnp.einsum("nt,kn->tk", grad, weight, preferred_element_type=jnp.float32)
            for grad, weight in zip((grad_held[:own_cols], grad_held[own_cols:]), crosskv_all)
        )
        held["text"] = rounded(text_part)
        held["text_got"] = swap_core(held["text"])
        held["cross_q"] = contract_pair(cross_in, after(grad_cquery, sent))
        three_here = jnp.concatenate(
            [part_at(block, here * tokens_here, tokens_here, 1) for block in after(three_low, sent)]
        )
        place_of = jnp.concatenate([index * own_cols + canonical[:own_cols] for index in relative])
        feature_map = rounded(place_of[:, None] == canonical[None, :])
        held["three"] = jnp.einsum(
            "kt,kc->tc", three_here, feature_map, preferred_element_type=jnp.float32
        )
        away = [rounded(pick(held["mlp"], here ^ distance)) for distance in (1, 3)]
        held["mlp_away"] = jnp.stack(away)
        held["mlp_got"] = swap_core(held["mlp_away"])
        return kv_grads, held["text"], held["cross_q"], held["mlp_away"], held["three"]

    back_two, d_cross_gain, d_cross_bias = norm_back(
        grad_cquery, cross_q_all, cross_scale, cross_in, cross_shift, two_inv, two_own_norm, work_two
    )
    grad_two = grad_three + back_two

    d_gate_one = jnp.sum(grad_two * branch_own, axis=1)
    grad_branch = rounded(grad_two * gate_one)

    def work_attn(sent):
        mlp_here = pick(held["mlp"], here ^ 2)
        held["mlp_sent"] = rounded(mlp_here + wide(held["mlp_got"][1]))
        held["text_pair"] = held["text"] + held["text_got"]
        attn_grads = contract_pair(attn_low, after(grad_branch, sent))
        held["small"] = ScatterRing(
            images,
            [attn_grads, held["cross_q"], held["cross_out"]] + held["kv"],
            [turned] * 3 + [straight] * 2,
        )
        return held["mlp_sent"], held["text_pair"], held["small"].blocks_ready(), held["fc2"]

    grad_attn = fold_features(grad_branch, attn_out_all, work_attn)[0]
    grad_attn = by_heads(rounded(grad_attn))
    mlp_sent, text_pair = after((held["mlp_sent"], held["text_pair"]), grad_attn)
    mlp_far = swap_chip(mlp_sent)
    grad_qkv, gain_terms = attend_heads_back(
        qkv_raw,
        qkv_low,
        attn_total,
        after(grad_attn, (mlp_sent, text_pair)),
        gains_low,
        cosine,
        sine_part,
    )
    grad_qkv = after(grad_qkv.reshape(3 * padded_cols, tokens), mlp_far)
    gain_terms = jnp.sum(gain_terms[..., 0], axis=0)
    gain_terms = jnp.dot(gain_terms, head_map, precision=lax.Precision.HIGHEST)
    one_own_norm = (one_own - one_mid) * one_inv


    def work_one(sent):
        qkv_grads = contract_pair(attn_in, after(grad_qkv, sent))
        held["qkv"] = ScatterRing(images, [qkv_grads], [turned])
        mlp_there = after(mlp_far, sent)
        mlp_rows = pick(held["mlp"], here) + wide(held["mlp_got"][0]) + wide(mlp_there)
        held["block_out"] = rounded(held["three"] + gate_two * mlp_rows)[None]
        return held["qkv"].advance(), held["block_out"]

    back_one, d_scale_one, d_shift_one = norm_back(
        grad_qkv, qkv_all, scale_one, attn_in, shift_one, one_inv, one_own_norm, work_one
    )
    grad_one = rounded(grad_two + back_one)

    norm_rows = joined_norm.reshape(shards, tokens_here, 2 * D)

    def cat_block(distance):
        rows = part_at(grad_one, (here ^ distance) * tokens_here, tokens_here, 1)
        return jnp.einsum("nt,kn->tk", rows, skip_all, preferred_element_type=jnp.float32)

    order.mark(grad_one)
    cat_away = order(jnp.concatenate([rounded(cat_block(1)), rounded(cat_block(3))]))
    order.mark(cat_away)
    cat_got = swap_core(cat_away)
    dmod_sent = order(
        jnp.concatenate(
            [d_shift_one, d_scale_one, d_gate_one, d_shift_two, d_scale_two, held["d_gate_two"]]
        )
    )
    cols_here = w_mod.shape[1]

    def modulation_back():
        far, near = send(dmod_sent)
        yield
        far = order(far)
        order.mark(far)
        diagonal = swap_core(far)
        yield
        blocks = jnp.stack(order(dmod_sent, near, far, diagonal))
        blocks = reorder(blocks, [here ^ shard for shard in range(shards)])
        five = blocks[:, : 5 * own_cols].reshape(shards, 5, own_cols)
        five = jnp.swapaxes(five, 0, 1).reshape(5 * D)
        full = jnp.concatenate([five, jnp.sum(blocks[:, 5 * own_cols :], axis=0)])
        cols = part_at(full, here * cols_here, cols_here, 0)[None]
        order.mark(cols)
        for bit in images.bits:
            other = images.swap(cols, bit)
            yield
            cols = jnp.concatenate([cols, order(other)])
            order.mark(cols)
        rows = jnp.einsum(
            "nc,rc->nr",
            cols,
            wide(mod_low),
            precision=lax.Precision.HIGHEST,
            preferred_element_type=jnp.float32,
        )
        order.mark(rows)
        for bit in images.bits:
            split = rows.reshape((-1, 2, bit) + rows.shape[1:])
            other = images.swap(split[:, 1], bit)
            yield
            rows = jnp.stack([split[:, 0], order(other)], axis=1).reshape(rows.shape)
            order.mark(rows)
        for swap in (swap_core, swap_chip):
            other = swap(rows)
            yield
            rows = rows + order(other)
            order.mark(rows)
        return cols, rows

    def sum_of_all(own):
        order.mark(own)
        for swap in (swap_core, swap_chip):
            other = swap(own)
            yield
            own = own + order(other)
            order.mark(own)
        for bit in images.bits:
            other = images.swap(own, bit)
            yield
            own = own + order(other)
            order.mark(own)
        return own

    cond_chain = Chain(modulation_back())
    cat_two = order(cat_block(2))
    cat_sent = rounded(cat_two + wide(order(cat_got)[tokens_here:]))
    order.mark(cat_sent)
    cat_far = swap_chip(cat_sent)
    text_far = swap_chip(order(text_pair))
    fc1_sum, fc2_sum = order(held["fc1"], held["fc2"])
    fc1_pieces, fc2_pieces = split_cols(fc1_sum, shards), split_cols(fc2_sum, shards)
    order.mark(fc1_pieces, fc2_pieces)
    order.step(held["small"])
    cond_chain.tick()
    skip_grad = jnp.einsum(
        "tk,nt->kn", cat_low, order(grad_one), preferred_element_type=jnp.float32
    )
    held["skip"] = ScatterRing(images, [(rounded(skip_grad),)], [straight])
    order.step(held["skip"])
    order.step(held["qkv"])
    cond_chain.tick()
    grad_held, away_held, two_held = order(grad_one, cat_away, cat_two)
    cat_zero = jnp.einsum(
        "nt,kn->tk",
        part_at(grad_held, here * tokens_here, tokens_here, 1),
        skip_all,
        preferred_element_type=jnp.float32,
    )
    cat_parts = (cat_zero, away_held[:tokens_here], two_held, away_held[tokens_here:])
    d_skip_bias = sum(jnp.sum(wide(part), axis=0) for part in cat_parts)
    d_skip_gain = sum(
        jnp.sum(wide(part) * wide(pick(norm_rows, here ^ distance)), axis=0)
        for distance, part in enumerate(cat_parts)
    )
    cross_gains = lax.dynamic_update_index_in_dim(
        jnp.zeros((shards, 2 * own_cols), jnp.float32),
        jnp.concatenate([d_cross_gain, d_cross_bias]),
        here,
        0,
        allow_negative_indices=False,
    )
    gains = jnp.concatenate(
        [d_skip_gain, d_skip_bias, gain_terms.reshape(-1), cross_gains.reshape(-1)]
    )
    gain_chain = Chain(sum_of_all(gains))
    cond_chain.tick()
    order.step(held["skip"])
    order.step(held["small"])
    gain_chain.tick()
    cond_chain.tick()
    grad_text = wide(text_pair + order(text_far))[None]
    order.mark(grad_text)
    fc1_trade = trade_starts(order(fc1_pieces), here)
    fc2_trade = trade_starts(order(fc2_pieces), here)
    order.step(held["qkv"])
    cond_chain.tick()
    order.step(held["skip"])
    gain_chain.tick()
    cond_chain.tick()
    order.step(held["small"])
    gain_chain.tick()
    order.step(held["qkv"])
    cond_chain.tick()
    order.step(held["skip"])
    order.step(held["small"])
    fc2_back = place(order(*fc2_trade), here)
    fc1_back = join_cols(place(order(*fc1_trade), here))
    grad_fc2 = wide(fc2_back).reshape(-1, own_cols)
    grad_fc1 = jnp.dot(fc1_back, unit_map.T, preferred_element_type=jnp.float32)
    order.mark(grad_fc1, grad_fc2)
    cond_chain.tick()
    gain_chain.tick()
    qkv_sum = split_cols(rounded(held["qkv"].result(order.last)), 3)
    qkv_sum = jnp.stack(
        [select(qkv_sum[part], column_maps[part].T) for part in range(3)]
    )
    order.mark(qkv_sum)
    stay = pick(qkv_sum, qkv_home[0])
    middle = swap_core(pick(qkv_sum, qkv_home[1]))
    other = swap_chip(pick(qkv_sum, qkv_home[2]))
    cond_chain.tick()
    small_sum = held["small"].result(order.last)
    grad_attn_out, grad_cross_q, grad_cross_out = jnp.split(small_sum[: 3 * rows_here], 3)
    grad_crosskv = jnp.stack(jnp.split(small_sum[3 * rows_here :], 2), axis=1)
    order.mark(small_sum)
    gain_chain.tick()
    cond_chain.tick()

    here_wide = wide(joined_here)
    here_mid, here_inv = norm_stats(here_wide, 1)
    here_norm = (here_wide - here_mid) * here_inv
    cat_rows = cat_zero + wide(cat_got[:tokens_here]) + wide(order(cat_far))
    cat_scaled = cat_rows * skip_gain
    grad_joined = here_inv * (
        cat_scaled
        - jnp.mean(cat_scaled, axis=-1, keepdims=True)
        - here_norm * jnp.mean(cat_scaled * here_norm, axis=-1, keepdims=True)
    )
    grad_hidden = grad_joined[:, :D][None]
    grad_skip = grad_joined[:, D:][None]
    order.mark(grad_hidden)
    grad_w_skip = held["skip"].result(order.last)
    order.mark(grad_w_skip)
    gains = gain_chain.finish()
    cross_gains = gains[4 * D + 2 * HD :].reshape(shards, 2, own_cols)
    cross_gains = jnp.swapaxes(cross_gains, 0, 1).reshape(2, D)
    dmod_cols, cond_sum = cond_chain.finish()
    grad_mod = jnp.einsum(
        "nr,nc->rc",
        wide(cond_rows),
        dmod_cols,
        precision=lax.Precision.HIGHEST,
        preferred_element_type=jnp.float32,
    )
    cond_grad = reorder(cond_sum, [images.here ^ image for image in range(count)]).reshape(D)
    grad_condition = jax.vjp(jax.nn.silu, cond_vec)[1](cond_grad)[0][None]
    middle, other = order(middle, other)
    low_end = jnp.where(odd == 1, other, stay)
    high_end = jnp.where(odd == 1, stay, other)
    grad_w_qkv = wide(jnp.concatenate([low_end, middle, high_end], axis=-1))

    return (
        held["block_out"],
        grad_hidden,
        grad_skip,
        grad_text,
        grad_condition,
        gains[: 2 * D],
        gains[2 * D : 4 * D],
        grad_w_skip,
        grad_mod,
        gains[4 * D : 4 * D + HD],
        gains[4 * D + HD : 4 * D + 2 * HD],
        grad_w_qkv,
        grad_attn_out,
        cross_gains[0],
        cross_gains[1],
        grad_cross_q,
        grad_crosskv,
        grad_cross_out,
        grad_fc1,
        grad_fc2,
    )


def solution(mesh):
    in_specs = (
        P("img", "seq", None),
        P("img", "seq", None),
        P("img", None, None),
        P("img", None),
        P("img", "seq", None),
        P("img", "seq", None),
        P(),
        P(),
        P("img", "seq"),
        P("img", "seq"),
        P(),
        P(),
        P("img", "seq"),
        P("img", "seq"),
        P(),
        P(),
        P("img", "seq"),
        P("img", None, "seq"),
        P("img", "seq"),
        P("img", "seq"),
        P("img", "seq"),
    )
    out_specs = (
        P("img", "seq", None),
        P("img", "seq", None),
        P("img", "seq", None),
        P("img", None, None),
        P("img", None),
        P(),
        P(),
        P("img", "seq"),
        P("img", "seq"),
        P(),
        P(),
        P("img", "seq"),
        P("img", "seq"),
        P(),
        P(),
        P("img", "seq"),
        P("img", None, "seq"),
        P("img", "seq"),
        P("img", "seq"),
        P("img", "seq"),
    )
    return jax.shard_map(
        per_device, mesh=mesh, in_specs=in_specs, out_specs=out_specs, check_vma=False
    )
```

```python
import functools
import math

import jax
import jax.numpy as jnp
import numpy as np
from jax import lax
from jax.experimental import pallas as pl
from jax.experimental.pallas import tpu as pltpu
from jax.sharding import PartitionSpec as P

D = 1408
H = 16
HD = 88

norm_eps = 1e-06
shards = 4
own_cols = D // shards
own_heads = H // shards
head_rows = 96
half_rows = head_rows // 2
quarter = HD // 4
padded_cols = own_heads * head_rows
vmem_bytes = 56 * 1024 * 1024
gelu_root = math.sqrt(2.0 / math.pi)
gelu_cube = 0.044715
log2_scale = HD ** (-0.5) / math.log(2.0)

core_pairs = ((0, 1), (1, 0), (2, 3), (3, 2))
chip_pairs = ((0, 2), (2, 0), (1, 3), (3, 1))
cross_pairs = ((0, 3), (3, 0), (1, 2), (2, 1))


def rounded(tensor):
    return tensor.astype(jnp.bfloat16)


def wide(tensor):
    return tensor.astype(jnp.float32)


def weigh(weights, tensors):
    return sum(
        jnp.einsum("kn,kt->nt", weight, tensor, preferred_element_type=jnp.float32)
        for weight, tensor in zip(weights, tensors)
    )


def weigh_back(weight, grad):
    return jnp.einsum("kn,nt->kt", weight, grad, preferred_element_type=jnp.float32)


def contract(left, right):
    return rounded(jnp.einsum("kt,nt->kn", left, right, preferred_element_type=jnp.float32))


def contract_pair(lefts, right):
    return tuple(contract(left, right) for left in lefts)


def norm_stats(tensor, axis):
    middle = jnp.mean(tensor, axis=axis, keepdims=True)
    center = tensor - middle
    spread = jnp.mean(center * center, axis=axis, keepdims=True)
    return middle, lax.rsqrt(spread + norm_eps)


def by_heads(tensor):
    return tensor.reshape(own_heads, HD, tensor.shape[-1])


def attend(queries, keys, values):
    scores = jnp.einsum(
        "hdk,hdq->hkq", keys, queries, preferred_element_type=jnp.float32
    ) * HD ** (-0.5)
    peak = jnp.max(scores, axis=1, keepdims=True)
    exp_scores = jnp.exp(scores - peak)
    total = jnp.sum(exp_scores, axis=1, keepdims=True)
    attn_probs = exp_scores / total
    outputs = jnp.einsum(
        "hdk,hkq->hdq", values, rounded(attn_probs), preferred_element_type=jnp.float32
    )
    return outputs, peak + jnp.log(total)


def attend_back(queries, keys, values, lse, grad_out):
    inv_root = HD ** (-0.5)
    scores = (
        jnp.einsum("hdk,hdq->hkq", keys, queries, preferred_element_type=jnp.float32) * inv_root
    )
    attn_probs = jnp.exp(scores - lse)
    grad_probs = jnp.einsum("hdk,hdq->hkq", values, grad_out, preferred_element_type=jnp.float32)
    delta = jnp.sum(attn_probs * grad_probs, axis=1, keepdims=True)
    grad_scores = rounded(attn_probs * (grad_probs - delta))
    grad_query = (
        jnp.einsum("hdk,hkq->hdq", keys, grad_scores, preferred_element_type=jnp.float32) * inv_root
    )
    grad_key = (
        jnp.einsum("hdq,hkq->hdk", queries, grad_scores, preferred_element_type=jnp.float32)
        * inv_root
    )
    grad_value = jnp.einsum(
        "hdq,hkq->hdk", grad_out, rounded(attn_probs), preferred_element_type=jnp.float32
    )
    return grad_query, grad_key, grad_value


def turned_rows():
    entry = np.arange(HD)
    axis, place = entry // (2 * quarter), entry % (2 * quarter)
    return (place // quarter) * half_rows + axis * quarter + place % quarter


def column_map(rows_of_entry):
    spread = np.zeros((own_cols, padded_cols), np.float32)
    for head in range(own_heads):
        spread[head * HD + np.arange(HD), head * head_rows + rows_of_entry] = 1.0
    return jnp.asarray(spread, jnp.bfloat16)


def select(left, right):
    return rounded(jnp.dot(left, right, preferred_element_type=jnp.float32))


def dot_across(left, right):
    return jnp.dot(left, right, preferred_element_type=jnp.float32)


def turn_head(raw, gain, cosine, sine_part):
    row = lax.broadcasted_iota(jnp.int32, raw.shape, 0)
    used = jnp.where(row % half_rows < 2 * quarter, 1.0, 0.0)
    center = (raw - jnp.sum(raw, axis=0, keepdims=True) * (1.0 / HD)) * used
    spread = jnp.sum(center * center, axis=0, keepdims=True) * (1.0 / HD)
    inverse = lax.rsqrt(spread + norm_eps)
    normed = center * inverse
    scaled = normed * gain
    first, second = scaled[:half_rows], scaled[half_rows:]
    turned = jnp.concatenate(
        [first * cosine - second * sine_part, first * sine_part + second * cosine], axis=0
    )
    return turned, normed, inverse, used


def turn_head_back(grad, normed, inverse, used, gain, cosine, sine_part):
    first, second = grad[:half_rows], grad[half_rows:]
    straight = jnp.concatenate(
        [first * cosine + second * sine_part, second * cosine - first * sine_part], axis=0
    )
    gain_grad = jnp.sum(straight * normed, axis=1, keepdims=True)
    scaled = straight * gain
    middle = jnp.sum(scaled, axis=0, keepdims=True) * (1.0 / HD)
    along = jnp.sum(scaled * normed, axis=0, keepdims=True) * (1.0 / HD)
    return inverse * (scaled - middle - normed * along) * used, gain_grad


key_chunk = 256


def attend_body(raw_ref, gain_ref, cos_ref, sin_ref, out_ref, low_ref, total_ref):
    cosine, sine_part = cos_ref[...], sin_ref[...]
    query = rounded(turn_head(raw_ref[0, 0], gain_ref[0], cosine, sine_part)[0])
    key_wide = turn_head(raw_ref[1, 0], gain_ref[1], cosine, sine_part)[0]
    value = rounded(raw_ref[2, 0])
    low_ref[0, 0] = query
    low_ref[1, 0] = rounded(key_wide)
    low_ref[2, 0] = value
    key_rows = rounded(key_wide.T)
    tokens = query.shape[1]
    total = jnp.zeros((1, tokens), jnp.float32)
    output = jnp.zeros((head_rows, tokens), jnp.float32)
    for start in range(0, tokens, key_chunk):
        scores = dot_across(key_rows[start : start + key_chunk], query)
        weights = jnp.exp2(scores * log2_scale)
        total = total + jnp.sum(weights, axis=0, keepdims=True)
        output = output + dot_across(value[:, start : start + key_chunk], rounded(weights))
    inverse = 1.0 / total
    total_ref[0] = inverse
    out_ref[0] = rounded((output * inverse)[:HD])


def attend_heads(raw, gains, cosine, sine_part):
    tokens = raw.shape[-1]
    heads = raw.shape[1]
    whole = lambda head: (0, 0)
    return pl.pallas_call(
        attend_body,
        grid=(heads,),
        out_shape=[
            jax.ShapeDtypeStruct((heads, HD, tokens), jnp.bfloat16),
            jax.ShapeDtypeStruct(raw.shape, jnp.bfloat16),
            jax.ShapeDtypeStruct((heads, 1, tokens), jnp.float32),
        ],
        in_specs=[
            pl.BlockSpec((3, 1, head_rows, tokens), lambda head: (0, head, 0, 0)),
            pl.BlockSpec((2, head_rows, 1), lambda head: (0, 0, 0)),
            pl.BlockSpec((half_rows, tokens), whole),
            pl.BlockSpec((half_rows, tokens), whole),
        ],
        out_specs=[
            pl.BlockSpec((1, HD, tokens), lambda head: (head, 0, 0)),
            pl.BlockSpec((3, 1, head_rows, tokens), lambda head: (0, head, 0, 0)),
            pl.BlockSpec((1, 1, tokens), lambda head: (head, 0, 0)),
        ],
        compiler_params=pltpu.CompilerParams(vmem_limit_bytes=vmem_bytes),
        cost_estimate=pl.CostEstimate(
            flops=4 * heads * tokens * tokens * 256,
            bytes_accessed=heads * tokens * 2000,
            transcendentals=heads * tokens * tokens,
        ),
    )(raw, gains, cosine, sine_part)


def attend_back_body(
    raw_ref, low_ref, total_ref, grad_ref, gain_ref, cos_ref, sin_ref, back_ref, gains_ref
):
    cosine, sine_part = cos_ref[...], sin_ref[...]
    query, key, value = low_ref[0, 0], low_ref[1, 0], low_ref[2, 0]
    tokens = query.shape[1]
    inverse_total = total_ref[0]
    grad_wide = wide(grad_ref[0])
    grad_wide = jnp.concatenate(
        [grad_wide, jnp.zeros((head_rows - HD, tokens), jnp.float32)], axis=0
    )
    grad = rounded(grad_wide)
    query_rows = rounded(wide(query).T)
    key_rows = rounded(wide(key).T)
    value_rows = rounded(wide(value).T)
    grad_rows = rounded(grad_wide.T)
    query_back = jnp.zeros((head_rows, tokens), jnp.float32)
    key_back, value_back = [], []
    delta = jnp.zeros((1, tokens), jnp.float32)
    chunks = [slice(start, start + key_chunk) for start in range(0, tokens, key_chunk)]
    held = []
    for chunk in chunks:
        scores = dot_across(key_rows[chunk], query)
        probs = jnp.exp2(scores * log2_scale) * inverse_total
        grad_probs = dot_across(value_rows[chunk], grad)
        delta = delta + jnp.sum(probs * grad_probs, axis=0, keepdims=True)
        held.append((probs, grad_probs))
    for chunk, (probs, grad_probs) in zip(chunks, held):
        grad_scores = rounded(probs * (grad_probs - delta))
        query_back = query_back + dot_across(key[:, chunk], grad_scores)
        key_back.append(dot_across(grad_scores, query_rows))
        value_back.append(dot_across(rounded(probs), grad_rows))
    root = HD ** (-0.5)
    key_back = jnp.concatenate(key_back, axis=0).T * root
    value_back = jnp.concatenate(value_back, axis=0).T
    for index, turned in enumerate((query_back * root, key_back)):
        gain = gain_ref[index]
        _, normed, inverse, used = turn_head(raw_ref[index, 0], gain, cosine, sine_part)
        straight, gain_grad = turn_head_back(
            turned, normed, inverse, used, gain, cosine, sine_part
        )
        back_ref[index, 0] = rounded(straight)
        gains_ref[0, index] = gain_grad
    back_ref[2, 0] = rounded(value_back)


def attend_heads_back(raw, low, inverse_total, grad, gains, cosine, sine_part):
    heads, tokens = raw.shape[1], raw.shape[-1]
    three = pl.BlockSpec((3, 1, head_rows, tokens), lambda head: (0, head, 0, 0))
    one = lambda rows: pl.BlockSpec((1, rows, tokens), lambda head: (head, 0, 0))
    whole = pl.BlockSpec((half_rows, tokens), lambda head: (0, 0))
    return pl.pallas_call(
        attend_back_body,
        grid=(heads,),
        out_shape=[
            jax.ShapeDtypeStruct(raw.shape, jnp.bfloat16),
            jax.ShapeDtypeStruct((heads, 2, head_rows, 1), jnp.float32),
        ],
        in_specs=[
            three,
            three,
            one(1),
            one(HD),
            pl.BlockSpec((2, head_rows, 1), lambda head: (0, 0, 0)),
            whole,
            whole,
        ],
        out_specs=[three, pl.BlockSpec((1, 2, head_rows, 1), lambda head: (head, 0, 0, 0))],
        compiler_params=pltpu.CompilerParams(vmem_limit_bytes=vmem_bytes),
        cost_estimate=pl.CostEstimate(
            flops=10 * heads * tokens * tokens * 256,
            bytes_accessed=heads * tokens * 3000,
            transcendentals=heads * tokens * tokens,
        ),
    )(raw, low, inverse_total, grad, gains, cosine, sine_part)


def norm_body(scale_at, shift_at, *refs):
    blocks, (columns_ref, keep_ref, away_ref, mid_ref, inv_ref) = refs[:4], refs[4:]
    base = wide(blocks[0][0:1])
    total = jnp.zeros(base.shape, jnp.float32)
    square = jnp.zeros(base.shape, jnp.float32)
    for block in blocks:
        shifted = wide(block[...]) - base
        total = total + jnp.sum(shifted, axis=0, keepdims=True)
        square = square + jnp.sum(shifted * shifted, axis=0, keepdims=True)
    total = total * (1.0 / D)
    inverse = lax.rsqrt(square * (1.0 / D) - total * total + norm_eps)
    middle = base + total
    mid_ref[...] = middle
    inv_ref[...] = inverse
    for index, block in enumerate(blocks):
        target = (keep_ref, away_ref)[index // 2]
        inner = (index % 2) * own_cols
        rows = slice(index * own_cols, (index + 1) * own_cols)
        scale = columns_ref[rows, scale_at : scale_at + 1]
        shift = columns_ref[rows, shift_at : shift_at + 1]
        normed = (wide(block[...]) - middle) * inverse
        target[inner : inner + own_cols] = rounded(normed * scale + shift)


def norm_columns(blocks, columns, scale_at, shift_at):
    tokens = blocks[0].shape[1]
    tile = 512
    part = pl.BlockSpec((own_cols, tile), lambda step: (0, step))
    half = pl.BlockSpec((2 * own_cols, tile), lambda step: (0, step))
    row = pl.BlockSpec((1, tile), lambda step: (0, step))
    keep, away, middle, inverse = pl.pallas_call(
        functools.partial(norm_body, scale_at, shift_at),
        grid=(tokens // tile,),
        out_shape=[
            jax.ShapeDtypeStruct((2 * own_cols, tokens), jnp.bfloat16),
            jax.ShapeDtypeStruct((2 * own_cols, tokens), jnp.bfloat16),
            jax.ShapeDtypeStruct((1, tokens), jnp.float32),
            jax.ShapeDtypeStruct((1, tokens), jnp.float32),
        ],
        in_specs=[part] * 4 + [pl.BlockSpec(columns.shape, lambda step: (0, 0))],
        out_specs=[half, half, row, row],
        compiler_params=pltpu.CompilerParams(vmem_limit_bytes=vmem_bytes),
        cost_estimate=pl.CostEstimate(
            flops=10 * D * tokens, bytes_accessed=4 * D * tokens, transcendentals=0
        ),
    )(*blocks, columns)
    return (keep, away), middle, inverse


def joined_body(places_ref, *refs):
    blocks, (vectors_ref, cat_ref, norm_ref) = refs[:4], refs[4:]
    gain, bias = vectors_ref[0:1], vectors_ref[1:2]
    for index, block in enumerate(blocks):
        tensor = wide(block[...])
        center = tensor - jnp.mean(tensor, axis=1, keepdims=True)
        spread = jnp.mean(center * center, axis=1, keepdims=True)
        normed = center * lax.rsqrt(spread + norm_eps)
        norm_ref[places_ref[index]] = rounded(normed)
        cat_ref[places_ref[index]] = rounded(normed * gain + bias)


def norm_joined(blocks, places, vectors):
    rows, cols = blocks[0].shape
    tile = 64
    shape = jax.ShapeDtypeStruct((4, rows, cols), jnp.bfloat16)
    part = pl.BlockSpec((tile, cols), lambda step: (step, 0))
    vector = pl.BlockSpec((2, cols), lambda step: (0, 0))
    every = pl.BlockSpec((4, tile, cols), lambda step: (0, step, 0))
    cat_low, norm_low = pl.pallas_call(
        joined_body,
        grid=(rows // tile,),
        out_shape=[shape, shape],
        in_specs=[pl.BlockSpec(memory_space=pltpu.SMEM)] + [part] * 4 + [vector],
        out_specs=[every, every],
        compiler_params=pltpu.CompilerParams(vmem_limit_bytes=vmem_bytes),
        cost_estimate=pl.CostEstimate(
            flops=40 * rows * cols, bytes_accessed=24 * rows * cols, transcendentals=0
        ),
    )(places, *blocks, vectors)
    return cat_low.reshape(4 * rows, cols), norm_low.reshape(4 * rows, cols)


def swap_core(tensor):
    return lax.ppermute(tensor, "seq", core_pairs)


def swap_chip(tensor):
    return lax.ppermute(tensor, "seq", chip_pairs)


def pick(tensor, index):
    return lax.dynamic_index_in_dim(
        tensor, index, 0, keepdims=False, allow_negative_indices=False
    )


def part_at(tensor, start, size, axis):
    return lax.dynamic_slice_in_dim(tensor, start, size, axis, allow_negative_indices=False)


def in_pairs(blocks):
    return jnp.concatenate(blocks[:2]), jnp.concatenate(blocks[2:])


def spread_rows(own):
    far = swap_chip(own)
    near = swap_core(own)
    return own, far, near, swap_core(far)


def fold_features(grad, weights, work=None):
    half = own_cols
    away = weigh_back(weights[1], grad)
    got = swap_core(rounded(away))
    keep = weigh_back(weights[0], grad)
    sent = rounded(keep[half:] + wide(got[half:]))
    far = swap_chip(sent)
    if work is not None:
        far = after(far, work(sent))
    total = keep[:half] + wide(got[:half]) + wide(far)
    return total, keep, away, sent


def place(blocks, here):
    places = here ^ jnp.arange(shards, dtype=jnp.int32)
    rows, cols = blocks[0].shape
    moves = [(index, 0, index, 0, rows, 0, 0, cols) for index in range(shards)]
    return move_blocks(blocks, moves, places, [((shards, rows, cols), False)])[0]


def reorder(tensor, order, axis=0):
    return jnp.concatenate([part_at(tensor, index, 1, axis) for index in order], axis=axis)


def split_cols(tensor, parts):
    size = tensor.shape[1] // parts
    return jnp.stack([tensor[:, part * size : (part + 1) * size] for part in range(parts)])


def join_cols(blocks):
    return jnp.concatenate([blocks[part] for part in range(blocks.shape[0])], axis=1)


def gather_small(own, here):
    far = swap_chip(own)
    near = swap_core(own)
    blocks = jnp.stack([own, near, far, swap_core(far)])
    return reorder(blocks, [here ^ shard for shard in range(shards)])


def sum_small(own):
    pair = own + swap_core(own)
    return pair + swap_chip(pair)


def trade_starts(pieces, here):
    return (
        pick(pieces, here),
        swap_core(pick(pieces, here ^ 1)),
        swap_chip(pick(pieces, here ^ 2)),
        lax.ppermute(pick(pieces, here ^ 3), "seq", cross_pairs),
    )


def ring_tables(count):
    order = [0] + list(range(1, count, 2)) + list(range(count - 2, 0, -2))
    spot = [order.index(index) for index in range(count)]
    up = tuple((order[step], order[(step + 1) % count]) for step in range(count))
    down = tuple((after, before) for before, after in up)
    return order, spot, up, down


def move_blocks(sources, moves, places, targets):
    def body(places_ref, *refs):
        outs, first = [], len(sources)
        for _, paired in targets:
            outs.append(refs[first : first + (2 if paired else 1)])
            first += len(outs[-1])
        for source, row, entry, inner, size, target, lane, width in moves:
            block = refs[source][pl.ds(row, size), pl.ds(0, width)]
            where = (pl.ds(inner, size), pl.ds(lane, width))
            spot = places_ref[entry]
            if len(outs[target]) == 1:
                outs[target][0][(spot,) + where] = block
                continue
            half = targets[target][0][0]

            @pl.when(spot < half)
            def store_first():
                outs[target][0][(spot,) + where] = block

            @pl.when(spot >= half)
            def store_second():
                outs[target][1][(spot - half,) + where] = block

    shapes = [
        jax.ShapeDtypeStruct(shape, sources[0].dtype)
        for shape, paired in targets
        for _ in range(2 if paired else 1)
    ]
    size = sum(math.prod(shape.shape) for shape in shapes)
    return pl.pallas_call(
        body,
        out_shape=shapes,
        in_specs=[pl.BlockSpec(memory_space=pltpu.SMEM)]
        + [pl.BlockSpec(memory_space=pltpu.VMEM)] * len(sources),
        out_specs=[pl.BlockSpec(memory_space=pltpu.VMEM)] * len(shapes),
        compiler_params=pltpu.CompilerParams(vmem_limit_bytes=vmem_bytes),
        cost_estimate=pl.CostEstimate(flops=0, bytes_accessed=4 * size, transcendentals=0),
    )(places, *sources)


def pick_blocks(source, table, paired_rows, plain_rows):
    count, _, cols = source.shape
    half = count // 2
    shapes = []
    for rows in paired_rows:
        shapes += [(half, rows, cols)] * 2
    shapes += [(count, rows, cols) for rows in plain_rows]

    def body(table_ref, source_ref, *targets):
        row = 0
        for part, rows in enumerate(paired_rows):
            for entry in range(count):
                target = targets[2 * part + entry // half]
                target[entry % half] = source_ref[table_ref[entry], pl.ds(row, rows)]
            row += rows
        for part, rows in enumerate(plain_rows):
            targets[2 * len(paired_rows) + part][...] = source_ref[:, pl.ds(row, rows)]
            row += rows

    picked = pl.pallas_call(
        body,
        out_shape=[jax.ShapeDtypeStruct(shape, source.dtype) for shape in shapes],
        in_specs=[
            pl.BlockSpec(memory_space=pltpu.SMEM),
            pl.BlockSpec(memory_space=pltpu.VMEM),
        ],
        out_specs=[pl.BlockSpec(memory_space=pltpu.VMEM)] * len(shapes),
        compiler_params=pltpu.CompilerParams(vmem_limit_bytes=vmem_bytes),
        cost_estimate=pl.CostEstimate(
            flops=0, bytes_accessed=4 * math.prod(source.shape), transcendentals=0
        ),
    )(table, source)
    picked = [piece.reshape(-1, cols) for piece in picked]
    first = 2 * len(paired_rows)
    return list(zip(picked[:first:2], picked[1:first:2])) + picked[first:]


def arrange_blocks(grads, tables, entries):
    rows = [grad[0].shape[1] for grad in grads]
    cols = max(grad[0].shape[2] for grad in grads)
    flat = [array for grad in grads for array in grad]

    def body(*refs):
        tables_refs, array_refs = refs[: len(grads)], refs[len(grads) : len(grads) + len(flat)]
        targets = refs[len(grads) + len(flat) :]
        base, first = 0, 0
        for grad, table_ref, size in zip(grads, tables_refs, rows):
            for entry, target in enumerate(targets):
                spot = table_ref[entry]
                begin = 0
                for index, array in enumerate(grad):
                    end = begin + array.shape[0]

                    @pl.when((spot >= begin) & (spot < end))
                    def store(index=index, begin=begin):
                        target[pl.ds(base, size)] = array_refs[first + index][spot - begin]

                    begin = end
            base, first = base + size, first + len(grad)

    shape = jax.ShapeDtypeStruct((sum(rows), cols), flat[0].dtype)
    return pl.pallas_call(
        body,
        out_shape=[shape] * entries,
        in_specs=[pl.BlockSpec(memory_space=pltpu.SMEM)] * len(grads)
        + [pl.BlockSpec(memory_space=pltpu.VMEM)] * len(flat),
        out_specs=[pl.BlockSpec(memory_space=pltpu.VMEM)] * entries,
        compiler_params=pltpu.CompilerParams(vmem_limit_bytes=vmem_bytes),
        cost_estimate=pl.CostEstimate(
            flops=0, bytes_accessed=4 * entries * math.prod(shape.shape), transcendentals=0
        ),
    )(*tables, *flat)


class Images:

    def __init__(self):
        self.count = lax.axis_size("img")
        self.here = lax.axis_index("img")
        self.bits = [1 << bit for bit in range((self.count - 1).bit_length())]
        self.direct = self.count != 8
        order, spot, self.up, self.down = ring_tables(self.count)
        self.order = order
        self.spot = spot


    def swap(self, tensor, bit):
        return lax.ppermute(
            tensor, "img", tuple((index, index ^ bit) for index in range(self.count))
        )

    def gather_small(self, own):
        held = own[None]
        for bit in self.bits:
            held = jnp.concatenate([held, self.swap(held, bit)])
        return held

    def scatter_small(self, terms):
        held = terms
        for bit in reversed(self.bits):
            held = held[:bit] + self.swap(held[bit:], bit)
        return held[0]

    def trade_small(self, rows):
        held = rows
        for bit in self.bits:
            split = held.reshape((-1, 2, bit) + rows.shape[1:])
            split = jnp.stack([split[:, 0], self.swap(split[:, 1], bit)], axis=1)
            held = split.reshape(rows.shape)
        return held

    def sum_small(self, own):
        for bit in self.bits:
            own = own + self.swap(own, bit)
        return own


    def table(self, entry_of, size):
        table = np.zeros((shards, self.count, size), np.int32)
        for shard in range(shards):
            for image in range(self.count):
                for entry in range(size):
                    table[shard, image, entry] = entry_of(shard, image, entry)
        table = jnp.asarray(table.reshape(shards * self.count, size))
        return pick(table, lax.axis_index("seq") * self.count + self.here)

    def places(self, slots, offsets):
        def entry_of(shard, image, entry):
            return slots(shard, self.order[(self.spot[image] + offsets[entry]) % self.count])

        return self.table(entry_of, len(offsets))


class GatherRing:
    def __init__(self, images, shard, halves=False):
        self.images = images
        self.shard = shard
        self.blocks, self.offsets, self.starts = [shard], [0], [0]
        self.halves = halves
        self.middle = (shard.shape[0] // 2 + 15) // 16 * 16
        self.upward = self.downward = shard
        self.step = 0
        self.reach = images.count // 2

    def advance(self, tie=()):
        images = self.images
        if images.direct:
            return self.shard
        self.step += 1
        upward, downward = after((self.upward, self.downward), tie)
        if self.step < self.reach:
            self.upward = lax.ppermute(upward, "img", images.up)
            self.downward = lax.ppermute(downward, "img", images.down)
            self.blocks += [self.upward, self.downward]
            self.offsets += [-self.step, self.step]
            self.starts += [0, 0]
        elif self.halves:
            self.upward = lax.ppermute(upward[: self.middle], "img", images.up)
            self.downward = lax.ppermute(downward[self.middle :], "img", images.down)
            self.blocks += [self.upward, self.downward]
            self.offsets += [-self.reach, -self.reach]
            self.starts += [0, self.middle]
        else:
            self.upward = lax.ppermute(upward, "img", images.up)
            self.blocks.append(self.upward)
            self.offsets.append(-self.reach)
            self.starts.append(0)
        return upward, downward

    def result(self, segments, targets):
        images = self.images
        count = images.count
        if images.direct:
            whole = lax.all_gather(self.shard, "img", axis=0)
            wholes = [[] for _ in targets]
            row = 0
            for rows, slots, target, _, width in segments:
                back = images.table(
                    lambda shard, image, entry: next(
                        other for other in range(count) if slots(shard, other) == entry
                    ),
                    count,
                )
                piece = jnp.take(whole[:, row : row + rows, :width], back, axis=0)
                wholes[target].append(piece.reshape(count * rows, width))
                row += rows
            wholes = [jnp.concatenate(pieces, axis=-1) for pieces in wholes]
            return [
                tuple(jnp.split(whole, 2)) if paired else whole
                for whole, (_, paired) in zip(wholes, targets)
            ]
        all_slots = []
        for _, slots, _, _, _ in segments:
            if slots not in all_slots:
                all_slots.append(slots)
        places = jnp.concatenate([images.places(slots, self.offsets) for slots in all_slots])
        moves = []
        for index, (block, start) in enumerate(zip(self.blocks, self.starts)):
            base = 0
            for rows, slots, target, lane, width in segments:
                low, high = max(base, start), min(base + rows, start + block.shape[0])
                if low < high:
                    entry = all_slots.index(slots) * len(self.offsets) + index
                    moves.append(
                        (index, low - start, entry, low - base, high - low, target, lane, width)
                    )
                base += rows
        placed = iter(move_blocks(self.blocks, moves, places, targets))
        results = []
        for _, paired in targets:
            pieces = tuple(next(placed) for _ in range(2 if paired else 1))
            pieces = tuple(piece.reshape(-1, piece.shape[-1]) for piece in pieces)
            results.append(pieces if paired else pieces[0])
        return results


class ScatterRing:
    def __init__(self, images, grads, slots):
        self.images = images
        count = images.count
        grads = [
            tuple(
                part.reshape(-1, sum(each.shape[0] for each in grad) // count, part.shape[1])
                for part in grad
            )
            for grad in grads
        ]
        self.grads, self.slots = grads, slots
        self.reach = count // 2
        self.step = 0
        if images.direct:
            return
        offsets = [self.reach]
        for step in range(2, self.reach + 1):
            offsets += [self.reach - step + 1, step - self.reach - 1]
        offsets.append(0)
        tables = [images.places(slots_of, offsets) for slots_of in slots]
        self.blocks = arrange_blocks(grads, tables, len(offsets))

    def advance(self, tie=()):
        images = self.images
        if images.direct:
            return self.grads
        self.step += 1
        blocks = self.blocks
        if self.step == 1:
            ahead = after(blocks[0], tie)
            self.upward = lax.ppermute(ahead, "img", images.up)
            return (ahead,)
        ahead, behind = blocks[2 * self.step - 3], blocks[2 * self.step - 2]
        if self.step == 2:
            upward, behind = after((self.upward, behind), tie)
        else:
            upward, downward = after((self.upward, self.downward), tie)
            behind = rounded(wide(behind) + wide(downward))
        ahead = rounded(wide(ahead) + wide(upward))
        self.upward = lax.ppermute(ahead, "img", images.up)
        self.downward = lax.ppermute(behind, "img", images.down)
        return ahead, behind

    def blocks_ready(self):
        return () if self.images.direct else self.blocks

    def result(self, tie=()):
        images = self.images
        if images.direct:
            count = images.count
            every = []
            cols = max(grad[0].shape[2] for grad in self.grads)
            for grad, slots in zip(self.grads, self.slots):
                order = images.table(lambda shard, image, entry: slots(shard, entry), count)
                block = jnp.take(jnp.concatenate(grad), order, axis=0)
                every.append(jnp.pad(block, ((0, 0), (0, 0), (0, cols - block.shape[2]))))
            every = wide(jnp.concatenate(every, axis=1))
            return lax.psum_scatter(every, "img", scatter_dimension=0, tiled=False)
        upward, downward = after((self.upward, self.downward), tie)
        return wide(self.blocks[-1]) + wide(upward) + wide(downward)


def after(tensor, mark):
    return lax.optimization_barrier((tensor, mark))[0]


class Order:
    def __init__(self):
        self.last = ()

    def __call__(self, *tensors):
        held = after(tensors, self.last)
        return held if len(tensors) > 1 else held[0]

    def mark(self, *tensors):
        self.last = tensors

    def step(self, ring):
        self.mark(ring.advance(self.last))


class Chain:
    def __init__(self, steps):
        self.steps = steps
        self.value = None
        self.running = True
        self.tick()

    def tick(self):
        if not self.running:
            return
        try:
            next(self.steps)
        except StopIteration as stop:
            self.value = stop.value
            self.running = False

    def finish(self):
        while self.running:
            self.tick()
        return self.value


def per_device(
    hidden_in,
    skip_in,
    text,
    condition,
    positions,
    out_grad,
    skip_gain,
    skip_bias,
    w_skip,
    w_mod,
    q_gain,
    k_gain,
    w_qkv,
    w_attn_out,
    cross_gain,
    cross_bias,
    w_cross_q,
    w_cross_kv,
    w_cross_out,
    w_fc1,
    w_fc2,
):
    here = lax.axis_index("seq")
    images = Images()
    count = images.count
    per_shard = count // shards
    rows_here = D // count
    text_rows = w_cross_kv.shape[0]
    hidden_units = w_fc2.shape[0] // shards
    tokens_here = hidden_in.shape[1]
    tokens = shards * tokens_here
    relative = [here, here ^ 2, here ^ 1, here ^ 3]

    def straight(shard, index):
        return index

    def turned(shard, index):
        return (0, 2, 1, 3)[(index // per_shard) ^ shard] * per_shard + index % per_shard

    order = Order()
    odd = here % 2
    places = here ^ jnp.arange(shards, dtype=jnp.int32)
    turn_map, plain_map = column_map(turned_rows()), column_map(np.arange(HD))
    column_maps = jnp.stack([turn_map, turn_map, plain_map])

    def send(own):
        order.mark(own)
        return swap_chip(own), swap_core(own)

    def receive(own, far, near):
        far = order(far)
        order.mark(far)
        return order(own, far, near, swap_core(far))

    skip_ring = GatherRing(images, rounded(w_skip))
    order.step(skip_ring)
    joined_here = order(jnp.concatenate([hidden_in[0], skip_in[0]], axis=-1))
    joined_far, joined_near = send(joined_here)
    cond_vec = wide(condition[0])
    cond_low = rounded(jax.nn.silu(cond_vec))
    mod_low = rounded(w_mod)

    def modulation():
        held = order(cond_low)[None]
        order.mark(held)
        for bit in images.bits:
            other = images.swap(held, bit)
            yield
            held = jnp.concatenate([held, order(other)])
            order.mark(held)
        rows = part_at(held, images.here * rows_here, rows_here, 1)
        held = jnp.dot(rows, mod_low, preferred_element_type=jnp.float32)
        order.mark(held)
        for bit in reversed(images.bits):
            other = images.swap(held[bit:], bit)
            yield
            held = held[:bit] + order(other)
            order.mark(held)
        own = held[0]
        far, near = swap_chip(own), swap_core(own)
        yield
        far = order(far)
        order.mark(far)
        diagonal = swap_core(far)
        yield
        blocks = jnp.stack(order(own, near, far, diagonal))
        vectors = reorder(blocks, [here ^ shard for shard in range(shards)]).reshape(6, D)
        order.mark(vectors)
        return rows, vectors

    mod_chain = Chain(modulation())
    qkv_here = rounded(order(w_qkv))
    qkv_parts = split_cols(qkv_here, 3)
    kept = jnp.where(odd == 1, qkv_parts[2], qkv_parts[0])
    sent = jnp.where(odd == 1, qkv_parts[0], qkv_parts[2])
    order.mark(kept, sent)
    qkv_mix = [kept, swap_core(qkv_parts[1]), swap_chip(sent)]
    grid_here = order(positions[0].T)
    grid_far, grid_near = send(grid_here)
    order.step(skip_ring)
    mod_chain.tick()
    mod_chain.tick()
    order.step(skip_ring)
    qkv_mix = jnp.stack(order(*qkv_mix))
    qkv_order = pick(np.array([[0, 1, 2], [1, 0, 2], [2, 0, 1], [2, 1, 0]], np.int32), here)
    qkv_home = pick(np.array([[0, 1, 2], [1, 0, 2], [1, 2, 0], [2, 1, 0]], np.int32), here)
    qkv_own = jnp.concatenate(
        [select(pick(qkv_mix, qkv_order[part]), column_maps[part]) for part in range(3)]
    )
    qkv_ring = GatherRing(images, qkv_own)
    order.mark(qkv_own)
    order.step(qkv_ring)
    mod_chain.tick()
    unit = np.arange(w_fc1.shape[1])
    image_of, inner = unit // (w_fc1.shape[1] // per_shard), unit % (w_fc1.shape[1] // per_shard)
    slot_of = (inner // hidden_units) * per_shard * hidden_units
    slot_of = slot_of + image_of * hidden_units + inner % hidden_units
    unit_map = np.zeros((w_fc1.shape[1], w_fc1.shape[1]), np.float32)
    unit_map[unit, slot_of] = 1.0
    unit_map = jnp.asarray(unit_map, jnp.bfloat16)
    later = order(w_fc1, w_fc2)
    fc1_pieces = split_cols(select(rounded(later[0]), unit_map), shards)
    fc2_pieces = rounded(later[1]).reshape(shards, hidden_units, own_cols)
    skip_rows = order(jnp.stack([skip_gain, skip_bias]))
    order.mark(fc1_pieces, fc2_pieces, skip_rows)
    grid = receive(grid_here, grid_far, grid_near)
    grid = jnp.stack([grid[0], grid[2], grid[1], grid[3]])
    grid = reorder(grid, [here ^ shard for shard in range(shards)])
    order.mark(grid)
    order.step(skip_ring)
    mod_chain.tick()
    order.step(qkv_ring)
    joined = receive(joined_here, joined_far, joined_near)
    joined = (joined[0], joined[2], joined[1], joined[3])
    cotangent_far = swap_chip(order(out_grad[0]))
    fc1_trade, fc2_trade = trade_starts(order(fc1_pieces), here), trade_starts(fc2_pieces, here)
    mod_chain.tick()
    (skip_all,) = skip_ring.result(
        [(2 * rows_here, straight, 0, 0, own_cols)], [((count, 2 * rows_here, own_cols), False)]
    )
    skip_all = order(skip_all)
    order.mark(skip_all)
    order.step(qkv_ring)
    mod_chain.tick()
    cond_rows, modul = mod_chain.finish()
    later = order(w_attn_out, w_cross_q, w_cross_out, w_cross_kv)
    crosskv = rounded(later[3])
    small = [rounded(weight) for weight in later[:3]] + [crosskv[:, 0], crosskv[:, 1]]
    small = jnp.concatenate(small)
    order.mark(small)
    small_ring = GatherRing(images, small)
    order.step(small_ring)
    cat_low, joined_norm = norm_joined(order(*joined), places, skip_rows)
    order.mark(cat_low)
    order.step(qkv_ring)
    one_own = jnp.einsum("kn,tk->nt", skip_all, order(cat_low), preferred_element_type=jnp.float32)
    one_low = rounded(one_own)
    order.mark(one_low)
    order.step(small_ring)
    cotangent_far, *trades = order(cotangent_far, *fc1_trade, *fc2_trade)
    one_low = after(one_low, (cotangent_far, trades))

    far, near = send(one_low)
    vectors = jnp.concatenate([order(modul), cross_gain[None], cross_bias[None]])
    one_plus = np.zeros((8, 1), np.float32)
    one_plus[[1, 4]] = 1.0
    columns = (vectors + one_plus).T
    columns = jnp.concatenate(
        [part_at(columns, index * own_cols, own_cols, 0) for index in relative]
    )
    shift_one, scale_one = columns[:, 0:1], columns[:, 1:2]
    shift_two, scale_two = columns[:, 3:4], columns[:, 4:5]
    cross_scale, cross_shift = columns[:, 6:7], columns[:, 7:8]
    gate_one = columns[:own_cols, 2:3]
    gate_two = modul[5]
    order.mark(columns)
    grid_pos = jnp.swapaxes(order(grid), 0, 1).reshape(2, 1, tokens).astype(jnp.float32)
    row = np.arange(half_rows)
    frequency = np.where(row < 2 * quarter, 10000.0 ** (-(row % quarter) / quarter), 0.0)
    frequency = jnp.asarray(frequency[:, None], jnp.float32)
    angles = jnp.where((row < quarter)[:, None], grid_pos[0], grid_pos[1]) * frequency
    cosine, sine_part = jnp.cos(angles), jnp.sin(angles)
    entry_rows = turned_rows()
    head_map = np.zeros((head_rows, HD), np.float32)
    head_map[entry_rows, np.arange(HD)] = 1.0
    gains_low = jnp.dot(
        jnp.stack([q_gain, k_gain]), head_map.T, precision=lax.Precision.HIGHEST
    )[:, :, None]
    order.mark(cosine, sine_part, gains_low)
    fc1_own = join_cols(place(order(*trades[:4]), here))
    fc2_own = join_cols(place(order(*trades[4:]), here))
    fc2_pad = jnp.zeros((hidden_units, w_fc1.shape[1] - D), jnp.bfloat16)
    fc_own = jnp.concatenate([fc1_own, jnp.concatenate([fc2_own, fc2_pad], axis=1)])
    order.mark(fc_own)
    fc_ring = GatherRing(images, fc_own, halves=True)
    (qkv_all,) = qkv_ring.result(
        [(rows_here, turned, 0, part * padded_cols, padded_cols) for part in range(3)],
        [((count // 2, rows_here, 3 * padded_cols), True)],
    )
    qkv_all = order(*qkv_all)
    order.mark(qkv_all)
    order.step(small_ring)
    one_blocks = receive(one_low, far, near)
    attn_in, one_mid, one_inv = norm_columns(one_blocks, columns, 1, 0)
    order.mark(attn_in)
    qkv_raw = weigh(qkv_all, order(*attn_in)).reshape(3, own_heads, head_rows, tokens)
    order.mark(qkv_raw)
    order.step(small_ring)
    attn_raw, qkv_low, attn_total = attend_heads(order(qkv_raw), gains_low, cosine, sine_part)
    attn_own = attn_raw.reshape(own_cols, tokens)

    far, near = send(attn_own)
    order.step(fc_ring)
    attn_out_all, cross_q_all, cross_out_all, *crosskv_all = small_ring.result(
        [(rows_here, turned, part, 0, own_cols) for part in range(3)]
        + [(text_rows, straight, part, 0, own_cols) for part in (3, 4)],
        [((count // 2, rows_here, own_cols), True)] * 3
        + [((count, text_rows, own_cols), False)] * 2,
    )
    crosskv_all = order(*crosskv_all)
    order.mark(crosskv_all)
    cotangent = (out_grad[0], swap_core(order(out_grad[0])), cotangent_far, swap_core(cotangent_far))
    attn_blocks = receive(attn_own, far, near)
    order.step(fc_ring)
    attn_low = in_pairs(order(*attn_blocks))
    branch_own = weigh(attn_out_all, attn_low)
    two_own = one_own + gate_one * branch_own
    two_low = rounded(two_own)

    far, near = send(two_low)
    text_keys, text_values = [
        by_heads(
            rounded(
                jnp.einsum("kn,tk->nt", weight, text[0], preferred_element_type=jnp.float32)
            )
        )
        for weight in order(*crosskv_all)
    ]
    order.mark(text_keys, text_values)
    cotangent = place(order(*cotangent), here).reshape(tokens, D)
    order.mark(cotangent)
    cot_wide = wide(order(cotangent))
    grad_mlp = rounded(cot_wide * gate_two)
    order.mark(grad_mlp)
    two_blocks = receive(two_low, far, near)
    order.step(fc_ring)
    two_blocks = order(*two_blocks)
    cross_in, two_mid, two_inv = norm_columns(two_blocks, columns, 6, 7)
    cross_query = by_heads(rounded(weigh(cross_q_all, cross_in)))
    cross_raw, cross_lse = attend(cross_query, text_keys, text_values)
    cross_own = rounded(cross_raw.reshape(own_cols, tokens))
    far, near = send(cross_own)
    order.step(fc_ring)
    cross_low = in_pairs(receive(cross_own, far, near))
    three_own = two_own + weigh(cross_out_all, cross_low)
    three_sent = rounded(three_own)

    far, near = send(three_sent)
    fc1_all, fc2_all = fc_ring.result(
        [
            (rows_here, turned, 0, 0, w_fc1.shape[1]),
            (hidden_units, straight, 1, 0, D),
        ],
        [
            ((count // 2, rows_here, w_fc1.shape[1]), True),
            ((count, hidden_units, D), False),
        ],
    )
    *fc1_all, fc2_all = order(*fc1_all, fc2_all)
    order.mark(fc2_all)
    three_low = receive(three_sent, far, near)
    mlp_in, three_mid, three_inv = norm_columns(three_low, columns, 4, 3)
    upper = weigh(fc1_all, mlp_in)
    bend = jnp.tanh(gelu_root * (upper + gelu_cube * upper * upper * upper))
    act_low = rounded(0.5 * upper * (1.0 + bend))
    slope = 0.5 * (1.0 + bend) + 0.5 * upper * (1.0 - bend * bend) * gelu_root * (
        1.0 + 3.0 * gelu_cube * upper * upper
    )
    act_low, slope = lax.optimization_barrier((act_low, slope))

    grad_act = jnp.einsum("uc,tc->ut", fc2_all, grad_mlp, preferred_element_type=jnp.float32)
    grad_upper = rounded(grad_act * slope)
    canonical = jnp.arange(D, dtype=jnp.int32)
    held = {}

    def norm_back(grad, weights, gain_rel, normed, shift, norm_inv, own, work, late=True):
        total, keep, away, sent = fold_features(grad, weights, work)
        half = D // 2
        kept = keep * gain_rel[:half]
        gone = away * gain_rel[half:]
        sums = jnp.stack(
            [
                jnp.sum(kept, axis=0) + jnp.sum(gone, axis=0),
                jnp.sum(keep * (wide(normed[0]) - shift[:half]), axis=0)
                + jnp.sum(away * (wide(normed[1]) - shift[half:]), axis=0),
            ]
        )
        means = sum_small(after(sums, sent if late else ())) * (1.0 / D)
        scaled = total * gain_rel[:own_cols]
        grad_in = norm_inv * (scaled - means[:1] - own * means[1:])
        return grad_in, jnp.sum(total * own, axis=1), jnp.sum(total, axis=1)

    def work_three(sent):
        own_map = canonical[:, None] == here * own_cols + canonical[None, :own_cols]
        fc2_grad = contract(after(act_low, sent), grad_mlp.T)
        fc1_grad = contract_pair(mlp_in, after(grad_upper, sent))
        held["fc1_pair"] = fc1_grad
        held["fc2"] = lax.psum_scatter(fc2_grad, "img", scatter_dimension=0, tiled=True)
        held["cot_own"] = jnp.einsum(
            "tc,cn->nt",
            after(cotangent, fc1_grad),
            rounded(own_map),
            preferred_element_type=jnp.float32,
        )
        return fc2_grad, held["fc1_pair"], held["cot_own"]

    three_own_norm = (three_own - three_mid) * three_inv
    back_three, d_scale_two, d_shift_two = norm_back(
        grad_upper, fc1_all, scale_two, mlp_in, shift_two, three_inv, three_own_norm, work_three
    )
    grad_three = held["cot_own"] + back_three

    grad_cross = rounded(grad_three)

    def work_cross(sent):
        act_held = after(act_low, sent)
        mlp_part = jnp.einsum("ut,uc->tc", act_held, fc2_all, preferred_element_type=jnp.float32)
        held["mlp"] = mlp_part.reshape(shards, tokens_here, D)
        held["d_gate_two"] = jnp.sum(cot_wide * mlp_part, axis=0)
        held["cross_out"] = contract_pair(cross_low, after(grad_cross, sent))
        fc1_grad = move_blocks(
            after(held["fc1_pair"], sent),
            [
                (index // 2, (index % 2) * own_cols, index, 0, own_cols, 0, 0, w_fc1.shape[1])
                for index in range(shards)
            ],
            jnp.stack(relative),
            [((shards, own_cols, w_fc1.shape[1]), False)],
        )[0].reshape(D, -1)
        held["fc1"] = lax.psum_scatter(
            after(fc1_grad, held["fc2"]), "img", scatter_dimension=0, tiled=True
        )
        return held["d_gate_two"], held["cross_out"], fc1_grad

    grad_cross_attn = fold_features(grad_cross, cross_out_all, work_cross)[0]
    grad_cross_attn = by_heads(rounded(grad_cross_attn))
    cross_back = attend_back(cross_query, text_keys, text_values, cross_lse, grad_cross_attn)
    grad_cquery = rounded(cross_back[0].reshape(own_cols, tokens))
    text_grad = rounded(jnp.concatenate([cross_back[1], cross_back[2]])).reshape(2 * own_cols, -1)
    two_own_norm = (two_own - two_mid) * two_inv

    def work_two(sent):
        grad_held = after(text_grad, sent)
        kv_grads = [
            (rounded(jnp.einsum("tk,nt->kn", text[0], grad, preferred_element_type=jnp.float32)),)
            for grad in (grad_held[:own_cols], grad_held[own_cols:])
        ]
        held["kv"] = kv_grads
        text_part = sum(
            jnp.einsum("nt,kn->tk", grad, weight, preferred_element_type=jnp.float32)
            for grad, weight in zip((grad_held[:own_cols], grad_held[own_cols:]), crosskv_all)
        )
        held["text"] = rounded(text_part)
        held["text_got"] = swap_core(held["text"])
        held["cross_q"] = contract_pair(cross_in, after(grad_cquery, sent))
        three_here = jnp.concatenate(
            [part_at(block, here * tokens_here, tokens_here, 1) for block in after(three_low, sent)]
        )
        place_of = jnp.concatenate([index * own_cols + canonical[:own_cols] for index in relative])
        feature_map = rounded(place_of[:, None] == canonical[None, :])
        held["three"] = jnp.einsum(
            "kt,kc->tc", three_here, feature_map, preferred_element_type=jnp.float32
        )
        away = [rounded(pick(held["mlp"], here ^ distance)) for distance in (1, 3)]
        held["mlp_away"] = jnp.stack(away)
        held["mlp_got"] = swap_core(held["mlp_away"])
        return kv_grads, held["text"], held["cross_q"], held["mlp_away"], held["three"]

    back_two, d_cross_gain, d_cross_bias = norm_back(
        grad_cquery, cross_q_all, cross_scale, cross_in, cross_shift, two_inv, two_own_norm, work_two
    )
    grad_two = grad_three + back_two

    d_gate_one = jnp.sum(grad_two * branch_own, axis=1)
    grad_branch = rounded(grad_two * gate_one)

    def work_attn(sent):
        mlp_here = pick(held["mlp"], here ^ 2)
        held["mlp_sent"] = rounded(mlp_here + wide(held["mlp_got"][1]))
        held["text_pair"] = held["text"] + held["text_got"]
        attn_grads = contract_pair(attn_low, after(grad_branch, sent))
        held["small"] = ScatterRing(
            images,
            [attn_grads, held["cross_q"], held["cross_out"]] + held["kv"],
            [turned] * 3 + [straight] * 2,
        )
        return held["mlp_sent"], held["text_pair"], held["small"].blocks_ready(), held["fc2"]

    grad_attn = fold_features(grad_branch, attn_out_all, work_attn)[0]
    grad_attn = by_heads(rounded(grad_attn))
    mlp_sent, text_pair = after((held["mlp_sent"], held["text_pair"]), grad_attn)
    mlp_far = swap_chip(mlp_sent)
    grad_qkv, gain_terms = attend_heads_back(
        qkv_raw,
        qkv_low,
        attn_total,
        after(grad_attn, (mlp_sent, text_pair)),
        gains_low,
        cosine,
        sine_part,
    )
    grad_qkv = after(grad_qkv.reshape(3 * padded_cols, tokens), mlp_far)
    gain_terms = jnp.sum(gain_terms[..., 0], axis=0)
    gain_terms = jnp.dot(gain_terms, head_map, precision=lax.Precision.HIGHEST)
    one_own_norm = (one_own - one_mid) * one_inv


    def work_one(sent):
        qkv_grads = contract_pair(attn_in, after(grad_qkv, sent))
        held["qkv"] = ScatterRing(images, [qkv_grads], [turned])
        mlp_there = after(mlp_far, sent)
        mlp_rows = pick(held["mlp"], here) + wide(held["mlp_got"][0]) + wide(mlp_there)
        held["block_out"] = rounded(held["three"] + gate_two * mlp_rows)[None]
        return held["qkv"].advance(), held["block_out"]

    back_one, d_scale_one, d_shift_one = norm_back(
        grad_qkv, qkv_all, scale_one, attn_in, shift_one, one_inv, one_own_norm, work_one, False
    )
    grad_one = rounded(grad_two + back_one)

    norm_rows = joined_norm.reshape(shards, tokens_here, 2 * D)

    def cat_block(distance):
        rows = part_at(grad_one, (here ^ distance) * tokens_here, tokens_here, 1)
        return jnp.einsum("nt,kn->tk", rows, skip_all, preferred_element_type=jnp.float32)

    order.mark(grad_one)
    cat_away = order(jnp.concatenate([rounded(cat_block(1)), rounded(cat_block(3))]))
    order.mark(cat_away)
    cat_got = swap_core(cat_away)
    dmod_sent = order(
        jnp.concatenate(
            [d_shift_one, d_scale_one, d_gate_one, d_shift_two, d_scale_two, held["d_gate_two"]]
        )
    )
    cols_here = w_mod.shape[1]

    def modulation_back():
        far, near = send(dmod_sent)
        yield
        far = order(far)
        order.mark(far)
        diagonal = swap_core(far)
        yield
        blocks = jnp.stack(order(dmod_sent, near, far, diagonal))
        blocks = reorder(blocks, [here ^ shard for shard in range(shards)])
        five = blocks[:, : 5 * own_cols].reshape(shards, 5, own_cols)
        five = jnp.swapaxes(five, 0, 1).reshape(5 * D)
        full = jnp.concatenate([five, jnp.sum(blocks[:, 5 * own_cols :], axis=0)])
        cols = part_at(full, here * cols_here, cols_here, 0)[None]
        order.mark(cols)
        for bit in images.bits:
            other = images.swap(cols, bit)
            yield
            cols = jnp.concatenate([cols, order(other)])
            order.mark(cols)
        rows = jnp.einsum(
            "nc,rc->nr",
            cols,
            wide(mod_low),
            precision=lax.Precision.HIGHEST,
            preferred_element_type=jnp.float32,
        )
        order.mark(rows)
        for bit in images.bits:
            split = rows.reshape((-1, 2, bit) + rows.shape[1:])
            other = images.swap(split[:, 1], bit)
            yield
            rows = jnp.stack([split[:, 0], order(other)], axis=1).reshape(rows.shape)
            order.mark(rows)
        for swap in (swap_core, swap_chip):
            other = swap(rows)
            yield
            rows = rows + order(other)
            order.mark(rows)
        return cols, rows

    def sum_of_all(own):
        order.mark(own)
        for swap in (swap_core, swap_chip):
            other = swap(own)
            yield
            own = own + order(other)
            order.mark(own)
        for bit in images.bits:
            other = images.swap(own, bit)
            yield
            own = own + order(other)
            order.mark(own)
        return own

    cond_chain = Chain(modulation_back())
    cat_two = order(cat_block(2))
    cat_sent = rounded(cat_two + wide(order(cat_got)[tokens_here:]))
    order.mark(cat_sent)
    cat_far = swap_chip(cat_sent)
    text_far = swap_chip(order(text_pair))
    fc1_sum, fc2_sum = order(held["fc1"], held["fc2"])
    fc1_pieces, fc2_pieces = split_cols(fc1_sum, shards), split_cols(fc2_sum, shards)
    order.mark(fc1_pieces, fc2_pieces)
    order.step(held["small"])
    cond_chain.tick()
    skip_grad = jnp.einsum(
        "tk,nt->kn", cat_low, order(grad_one), preferred_element_type=jnp.float32
    )
    held["skip"] = ScatterRing(images, [(rounded(skip_grad),)], [straight])
    order.step(held["skip"])
    order.step(held["qkv"])
    cond_chain.tick()
    grad_held, away_held, two_held = order(grad_one, cat_away, cat_two)
    cat_zero = jnp.einsum(
        "nt,kn->tk",
        part_at(grad_held, here * tokens_here, tokens_here, 1),
        skip_all,
        preferred_element_type=jnp.float32,
    )
    cat_parts = (cat_zero, away_held[:tokens_here], two_held, away_held[tokens_here:])
    d_skip_bias = sum(jnp.sum(wide(part), axis=0) for part in cat_parts)
    d_skip_gain = sum(
        jnp.sum(wide(part) * wide(pick(norm_rows, here ^ distance)), axis=0)
        for distance, part in enumerate(cat_parts)
    )
    cross_gains = lax.dynamic_update_index_in_dim(
        jnp.zeros((shards, 2 * own_cols), jnp.float32),
        jnp.concatenate([d_cross_gain, d_cross_bias]),
        here,
        0,
        allow_negative_indices=False,
    )
    gains = jnp.concatenate(
        [d_skip_gain, d_skip_bias, gain_terms.reshape(-1), cross_gains.reshape(-1)]
    )
    gain_chain = Chain(sum_of_all(gains))
    cond_chain.tick()
    order.step(held["skip"])
    order.step(held["small"])
    gain_chain.tick()
    cond_chain.tick()
    grad_text = wide(text_pair + order(text_far))[None]
    order.mark(grad_text)
    fc1_trade = trade_starts(order(fc1_pieces), here)
    fc2_trade = trade_starts(order(fc2_pieces), here)
    order.step(held["qkv"])
    cond_chain.tick()
    order.step(held["skip"])
    gain_chain.tick()
    cond_chain.tick()
    order.step(held["small"])
    gain_chain.tick()
    order.step(held["qkv"])
    cond_chain.tick()
    order.step(held["skip"])
    order.step(held["small"])
    fc2_back = place(order(*fc2_trade), here)
    fc1_back = join_cols(place(order(*fc1_trade), here))
    grad_fc2 = wide(fc2_back).reshape(-1, own_cols)
    grad_fc1 = jnp.dot(fc1_back, unit_map.T, preferred_element_type=jnp.float32)
    order.mark(grad_fc1, grad_fc2)
    cond_chain.tick()
    gain_chain.tick()
    qkv_sum = split_cols(rounded(held["qkv"].result(order.last)), 3)
    qkv_sum = jnp.stack(
        [select(qkv_sum[part], column_maps[part].T) for part in range(3)]
    )
    order.mark(qkv_sum)
    stay = pick(qkv_sum, qkv_home[0])
    middle = swap_core(pick(qkv_sum, qkv_home[1]))
    other = swap_chip(pick(qkv_sum, qkv_home[2]))
    cond_chain.tick()
    small_sum = held["small"].result(order.last)
    grad_attn_out, grad_cross_q, grad_cross_out = jnp.split(small_sum[: 3 * rows_here], 3)
    grad_crosskv = jnp.stack(jnp.split(small_sum[3 * rows_here :], 2), axis=1)
    order.mark(small_sum)
    gain_chain.tick()
    cond_chain.tick()

    here_wide = wide(joined_here)
    here_mid, here_inv = norm_stats(here_wide, 1)
    here_norm = (here_wide - here_mid) * here_inv
    cat_rows = cat_zero + wide(cat_got[:tokens_here]) + wide(order(cat_far))
    cat_scaled = cat_rows * skip_gain
    grad_joined = here_inv * (
        cat_scaled
        - jnp.mean(cat_scaled, axis=-1, keepdims=True)
        - here_norm * jnp.mean(cat_scaled * here_norm, axis=-1, keepdims=True)
    )
    grad_hidden = grad_joined[:, :D][None]
    grad_skip = grad_joined[:, D:][None]
    order.mark(grad_hidden)
    grad_w_skip = held["skip"].result(order.last)
    order.mark(grad_w_skip)
    gains = gain_chain.finish()
    cross_gains = gains[4 * D + 2 * HD :].reshape(shards, 2, own_cols)
    cross_gains = jnp.swapaxes(cross_gains, 0, 1).reshape(2, D)
    dmod_cols, cond_sum = cond_chain.finish()
    grad_mod = jnp.einsum(
        "nr,nc->rc",
        wide(cond_rows),
        dmod_cols,
        precision=lax.Precision.HIGHEST,
        preferred_element_type=jnp.float32,
    )
    cond_grad = reorder(cond_sum, [images.here ^ image for image in range(count)]).reshape(D)
    grad_condition = jax.vjp(jax.nn.silu, cond_vec)[1](cond_grad)[0][None]
    middle, other = order(middle, other)
    low_end = jnp.where(odd == 1, other, stay)
    high_end = jnp.where(odd == 1, stay, other)
    grad_w_qkv = wide(jnp.concatenate([low_end, middle, high_end], axis=-1))

    return (
        held["block_out"],
        grad_hidden,
        grad_skip,
        grad_text,
        grad_condition,
        gains[: 2 * D],
        gains[2 * D : 4 * D],
        grad_w_skip,
        grad_mod,
        gains[4 * D : 4 * D + HD],
        gains[4 * D + HD : 4 * D + 2 * HD],
        grad_w_qkv,
        grad_attn_out,
        cross_gains[0],
        cross_gains[1],
        grad_cross_q,
        grad_crosskv,
        grad_cross_out,
        grad_fc1,
        grad_fc2,
    )


def solution(mesh):
    in_specs = (
        P("img", "seq", None),
        P("img", "seq", None),
        P("img", None, None),
        P("img", None),
        P("img", "seq", None),
        P("img", "seq", None),
        P(),
        P(),
        P("img", "seq"),
        P("img", "seq"),
        P(),
        P(),
        P("img", "seq"),
        P("img", "seq"),
        P(),
        P(),
        P("img", "seq"),
        P("img", None, "seq"),
        P("img", "seq"),
        P("img", "seq"),
        P("img", "seq"),
    )
    out_specs = (
        P("img", "seq", None),
        P("img", "seq", None),
        P("img", "seq", None),
        P("img", None, None),
        P("img", None),
        P(),
        P(),
        P("img", "seq"),
        P("img", "seq"),
        P(),
        P(),
        P("img", "seq"),
        P("img", "seq"),
        P(),
        P(),
        P("img", "seq"),
        P("img", None, "seq"),
        P("img", "seq"),
        P("img", "seq"),
        P("img", "seq"),
    )
    return jax.shard_map(
        per_device, mesh=mesh, in_specs=in_specs, out_specs=out_specs, check_vma=False
    )
```
